256 devices in a mesh: dp: 8 (over x, core), tile: 32 (over z, y).
Axes of the slice: x: 4, y: 4, z: 8, core: 2. Of those that a mesh axis runs over, the one named last changes fastest.
Arguments:
- image_descriptors: bfloat16 [8, 1024, 256], P('dp', 'tile'), may hold values from -50 to 50
- image_distance_scores: bfloat16 [8, 1024, 64], P('dp', 'tile'), may hold values from -104 to 126
- entry_sender_location: int32 [8, 32, 32, 64], P('dp', 'tile'), may hold values from 0 to 2047, as said below
- entry_receiver_square: int32 [8, 32, 32, 64], P('dp', 'tile'), may hold values from 0 to 799
- entry_valid_tally: int32 [8, 32, 32], P('dp', 'tile'), may hold values from 1 to 64, as said below
- predicted_adjoint: bfloat16 [8, 64, 400, 256], P('dp', 'tile'), may hold values from -6 to 6
- initial_plane_filter: bfloat16 [2304, 256], replicated, may hold values from -0.125 to 0.125
- predictor_filter: bfloat16 [2304, 256], replicated, may hold values from -0.125 to 0.125
Outputs:
- predicted_scene: bfloat16 [8, 64, 400, 256], P('dp', 'tile')
- prenonlinear_derivative: bfloat16 [8, 64, 400, 256], P('dp', 'tile')
- predictor_filter_derivative: float32 [2304, 256], P('tile')
The draws below stay inside these ranges and needn't reach their ends.
Inputs may be any that keep to these rules, and one draw needn't show every extreme that they name: `entry_sender_location`: the entries of one source device's lists, over all strips and slots, are distinct; entry p stands for that device's local pixel p // 64 and depth bin p % 64. `entry_receiver_square`: cell row * 400 + column of the destination strip. The first entry_valid_tally slots of a list are live; in every frame some strip has 64 live slots from every source device.
All inputs are finite; a program needn't handle non-finite values.
Results may differ from the reference program's by a relative error of at most 0.0059.
Values may be sent and summed in bfloat16 or wider, within the bound.
No kernel may reach another device: no remote copies, remote signals or barrier semaphores. Data moves between devices by JAX's collectives and lax.ppermute only.
A program may use at most 64 MiB of HBM per device.

```python
import math
import jax
import jax.numpy as jnp
from jax import lax

EMBED_PLANES = 256
DB = 64
LATTICE_BREADTH = 400
COLS_DEV = 32
SNAPSHOT_SUM = 8
LATTICE_LENGTH = 64
COLS = 1024
CELLS_DEV = 800
CAP = 64
N_TILE = 32


def draw_image_descriptors(key, part):
    key = jax.random.fold_in(key, 5)
    key_values, key_chan, key_pixel = jax.random.split(key, 3)
    chan_scale = jnp.exp(jax.random.uniform(key_chan, (1, 1, EMBED_PLANES), jnp.float32, 0.0, math.log(10.0)))
    pixel_scale = jnp.exp(jax.random.uniform(key_pixel, (SNAPSHOT_SUM, COLS, 1), jnp.float32, 0.0, math.log(10.0)))
    raw_values = jnp.clip(jax.random.normal(key_values, (SNAPSHOT_SUM, COLS, EMBED_PLANES), jnp.float32), -5.0, 5.0)
    return (raw_values * chan_scale * pixel_scale / 10.0).astype(jnp.bfloat16)


def draw_image_distance_scores(key, part):
    key = jax.random.fold_in(key, 11)
    key_base = jax.random.fold_in(key, 0)
    raw_values = jnp.clip(2.5 * jax.random.normal(key_base, (SNAPSHOT_SUM, COLS, DB), jnp.float32), -8.0, 8.0)
    return raw_values.astype(jnp.bfloat16)


def draw_entry_sender_location(key, part):
    key = jax.random.fold_in(key, 17)
    frame_keys = jax.random.split(key, SNAPSHOT_SUM * N_TILE)
    perms = jax.vmap(lambda one_key: jax.random.permutation(one_key, COLS_DEV * DB))(frame_keys)
    return perms.reshape(SNAPSHOT_SUM, N_TILE, N_TILE, CAP).astype(jnp.int32)


def draw_entry_valid_tally(key, part):
    key = jax.random.fold_in(key, 23)
    key_centre, key_counts = jax.random.split(key)
    centre = jax.random.randint(key_centre, (SNAPSHOT_SUM, 1, 1), N_TILE // 4, 3 * N_TILE // 4)
    dest_tile = jnp.arange(N_TILE, dtype=jnp.int32)[None, None, :]
    distance = jnp.abs(dest_tile - centre)
    drawn_counts = jax.random.randint(key_counts, (SNAPSHOT_SUM, N_TILE, N_TILE), CAP // 2, CAP + 1)
    counts = jnp.maximum(1, drawn_counts * 8 // (8 + distance))
    counts = jnp.where(distance == 0, CAP, counts)
    return counts.astype(jnp.int32)


def place_ends(drawn, key, least, largest):
    shape = drawn.shape
    index_at = [jax.random.randint(jax.random.fold_in(key, axis), (), 0, shape[axis]) for axis in range(len(shape))]
    drawn = drawn.at[tuple(index_at)].set(least)
    longest = shape.index(max(shape))
    index_at[longest] = (index_at[longest] + 1) % shape[longest]
    return drawn.at[tuple(index_at)].set(largest)


def levels(rng, dims, shards, low, high):
    gain, own = 1.0, jax.random.fold_in(rng, 6)
    for position, parts in shards:
        steps = jnp.exp(jax.random.uniform(jax.random.fold_in(own, position), (parts,), jnp.float32, low / len(shards), high / len(shards)))
        gain = gain * jnp.repeat(steps, dims[position] // parts).reshape([-1 if axis == position else 1 for axis in range(len(dims))])
    return gain


def bell_draw(rng, extent, width, limit, cuts=(), kind=jnp.bfloat16):
    array = width * jax.random.normal(rng, extent, jnp.float32)
    if cuts:
        array = array * levels(rng, extent, cuts, -0.22, 0.18)
    return jnp.clip(array, -limit, limit).astype(kind)


def setup_inputs(seed: int = 0) -> dict:
    key_list = jax.random.split(jax.random.key(seed), 9)
    image_descriptors = draw_image_descriptors(jax.random.fold_in(key_list[8], 71), 0)
    image_distance_scores = draw_image_distance_scores(jax.random.fold_in(key_list[8], 71), 0)
    entry_sender_location = draw_entry_sender_location(jax.random.fold_in(key_list[8], 71), 0)
    entry_receiver_square = place_ends(jax.random.randint(key_list[3], (SNAPSHOT_SUM, N_TILE, N_TILE, CAP), 0, CELLS_DEV), jax.random.fold_in(key_list[3], 1), 0, CELLS_DEV - 1).astype(jnp.int32)
    entry_valid_tally = draw_entry_valid_tally(jax.random.fold_in(key_list[8], 71), 0)
    predicted_adjoint = bell_draw(key_list[5], (SNAPSHOT_SUM, LATTICE_LENGTH, LATTICE_BREADTH, EMBED_PLANES), 1.0, 6.0, ((0, 8), (1, 32)))
    initial_plane_filter = bell_draw(key_list[6], (9 * EMBED_PLANES, EMBED_PLANES), (9 * EMBED_PLANES) ** -0.5, 0.125)
    predictor_filter = bell_draw(key_list[7], (9 * EMBED_PLANES, EMBED_PLANES), (9 * EMBED_PLANES) ** -0.5, 0.125)
    return {"image_descriptors": image_descriptors, "image_distance_scores": image_distance_scores, "entry_sender_location": entry_sender_location, "entry_receiver_square": entry_receiver_square, "entry_valid_tally": entry_valid_tally, "predicted_adjoint": predicted_adjoint, "initial_plane_filter": initial_plane_filter, "predictor_filter": predictor_filter}


def tap_window(padded, tap_index, horizontal_tally, vertical_tally, flipped):
    shift_y = tap_index // 3 - 1
    shift_x = tap_index % 3 - 1
    if flipped:
        shift_y = -shift_y
        shift_x = -shift_x
    return padded[:, 1 + shift_y:1 + shift_y + horizontal_tally, 1 + shift_x:1 + shift_x + vertical_tally, :]

def stencil_offsets(padded, weight, horizontal_tally, vertical_tally, flipped):
    plane_tally = weight.shape[1]
    result = None
    for tap_index in range(9):
        window = tap_window(padded, tap_index, horizontal_tally, vertical_tally, flipped).astype(jnp.float32)
        block_weight = weight[tap_index * plane_tally:(tap_index + 1) * plane_tally].astype(jnp.float32)
        if flipped:
            term = jnp.einsum('fyxo,io->fyxi', window, block_weight)
        else:
            term = jnp.einsum('fyxi,io->fyxo', window, block_weight)
        result = term if result is None else result + term
    return result

def broadened_lattice(field):
    return jnp.pad(field, ((0, 0), (1, 1), (1, 1), (0, 0)))

def reference(image_descriptors, image_distance_scores, entry_sender_location, entry_receiver_square, entry_valid_tally, predicted_adjoint, initial_plane_filter, predictor_filter):
    depth_prob = jax.nn.softmax(image_distance_scores.astype(jnp.float32), axis=-1)
    flat_prob = depth_prob.reshape(SNAPSHOT_SUM, COLS * DB)
    source_base = (jnp.arange(N_TILE, dtype=jnp.int32) * (COLS_DEV * DB))[:, None, None]
    tile_base = (jnp.arange(N_TILE, dtype=jnp.int32) * CELLS_DEV)[None, :, None]
    slot_index = jnp.arange(CAP, dtype=jnp.int32)[None, None, :]

    def splat_frame(frame_inputs):
        features, probs_row, points, cell_ids, counts = frame_inputs
        global_point = (points + source_base).reshape(-1).astype(jnp.int32)
        live_mask = (slot_index < counts[:, :, None]).reshape(-1)
        chosen = jnp.where(live_mask, probs_row[global_point], jnp.zeros((), probs_row.dtype))
        lifted = (features[global_point // DB].astype(jnp.float32) * chosen[:, None]).astype(jnp.bfloat16)
        targets = (cell_ids + tile_base).reshape(-1).astype(jnp.int32)
        return jax.ops.segment_sum(lifted.astype(jnp.float32), targets, num_segments=LATTICE_LENGTH * LATTICE_BREADTH)
    splat_sum = lax.map(splat_frame, (image_descriptors, flat_prob, entry_sender_location, entry_receiver_square, entry_valid_tally))
    norm_factor = lax.rsqrt(lax.optimization_barrier(jnp.mean(splat_sum * splat_sum, axis=-1, keepdims=True)) + 1e-05)
    aerial_scene = (splat_sum * norm_factor).astype(jnp.bfloat16).reshape(SNAPSHOT_SUM, LATTICE_LENGTH, LATTICE_BREADTH, EMBED_PLANES)
    pre_first = stencil_offsets(broadened_lattice(aerial_scene), initial_plane_filter, LATTICE_LENGTH, LATTICE_BREADTH, False)
    hidden = jax.nn.silu(pre_first).astype(jnp.bfloat16)
    broadened_latent = broadened_lattice(hidden)
    predicted_scene = (aerial_scene.astype(jnp.float32) + stencil_offsets(broadened_latent, predictor_filter, LATTICE_LENGTH, LATTICE_BREADTH, False)).astype(jnp.bfloat16)
    yielded_derivative = stencil_offsets(broadened_lattice(predicted_adjoint), predictor_filter, LATTICE_LENGTH, LATTICE_BREADTH, True)
    sigma = jax.nn.sigmoid(pre_first)
    prenonlinear_derivative = (yielded_derivative * sigma * (1.0 + pre_first * (1.0 - sigma))).astype(jnp.bfloat16)
    derivative_alone = predicted_adjoint.astype(jnp.float32)
    derivative_pieces = []
    for tap_index in range(9):
        window = tap_window(broadened_latent, tap_index, LATTICE_LENGTH, LATTICE_BREADTH, False).astype(jnp.float32)
        derivative_pieces.append(jnp.einsum('fyxi,fyxo->io', window, derivative_alone))
    predictor_filter_derivative = jnp.concatenate(derivative_pieces, axis=0) / math.sqrt(SNAPSHOT_SUM * LATTICE_LENGTH * LATTICE_BREADTH)
    return (predicted_scene, prenonlinear_derivative, predictor_filter_derivative)
```

```python
import math

import jax
import jax.numpy as jnp
from jax import lax
from jax.sharding import PartitionSpec as P

epsilon = 1e-05


def with_halo(cells, sides, width):
    for axis, dim in sides:
        count = lax.axis_size(axis)
        ends = count - 1
        head = lax.slice_in_dim(cells, 0, width, axis=dim)
        tail = lax.slice_in_dim(cells, cells.shape[dim] - width, cells.shape[dim], axis=dim)
        cells = jnp.concatenate(
            [
                lax.ppermute(tail, axis, [(i, (i + 1) % count) for i in range(ends)]),
                cells,
                lax.ppermute(head, axis, [((i + 1) % count, i) for i in range(ends)]),
            ],
            axis=dim,
        )
    return cells


def silu_slope(pre_act):
    sigma = jax.nn.sigmoid(pre_act)
    return sigma * (1.0 + pre_act * (1.0 - sigma))


def tap_window(padded, tap_index, horizontal_tally, vertical_tally, flipped):
    shift_y = tap_index // 3 - 1
    shift_x = tap_index % 3 - 1
    if flipped:
        shift_y = -shift_y
        shift_x = -shift_x
    return padded[
        :,
        1 + shift_y : 1 + shift_y + horizontal_tally,
        1 + shift_x : 1 + shift_x + vertical_tally,
        :,
    ]


def stencil_offsets(padded, weight, horizontal_tally, vertical_tally, flipped):
    plane_tally = weight.shape[1]
    result = None
    for tap_index in range(9):
        window = tap_window(padded, tap_index, horizontal_tally, vertical_tally, flipped)
        block_weight = weight[tap_index * plane_tally : (tap_index + 1) * plane_tally]
        if flipped:
            term = jnp.einsum(
                "fyxo,io->fyxi", window, block_weight, preferred_element_type=jnp.float32
            )
        else:
            term = jnp.einsum(
                "fyxi,io->fyxo", window, block_weight, preferred_element_type=jnp.float32
            )
        result = term if result is None else result + term
    return result


def broadened_verticals(field):
    return jnp.pad(field, ((0, 0), (0, 0), (1, 1), (0, 0)))


def lift_values(features, flat_prob, point_index, live_mask, depth_bins):
    frame_rows = lax.broadcasted_iota(jnp.int32, point_index.shape, 0)
    chosen = flat_prob[frame_rows, point_index]
    weight_row = jnp.where(live_mask, chosen, 0.0)
    rows_taken = features[frame_rows, point_index // depth_bins]
    return (rows_taken.astype(jnp.float32) * weight_row[:, :, None]).astype(jnp.bfloat16)


def splat_frames(values, cell_ids, cell_total):
    snapshot_ordinal, slot_total, plane_tally = values.shape
    block_size = math.gcd(slot_total, 512)
    blocks = slot_total // block_size

    def add_block(block_index, summed):
        part_values = lax.dynamic_slice_in_dim(values, block_index * block_size, block_size, 1)
        part_cells = lax.dynamic_slice_in_dim(cell_ids, block_index * block_size, block_size, 1)
        onehot = (
            lax.broadcasted_iota(jnp.int32, (snapshot_ordinal, cell_total, block_size), 1)
            == part_cells[:, None, :]
        ).astype(jnp.bfloat16)
        return summed + jnp.einsum(
            "fcs,fsk->fck", onehot, part_values, preferred_element_type=jnp.float32
        )

    start_sum = jnp.zeros((snapshot_ordinal, cell_total, plane_tally), jnp.float32)
    return lax.fori_loop(0, blocks, add_block, start_sum)


def reduced_gradient(local_grad, share_rows, tile_count):
    half = local_grad.shape[1] // 2
    dp_count = lax.axis_size("dp")
    odd_core = lax.axis_index("dp") % 2 == 1
    left, right = local_grad[:, :half], local_grad[:, half:]
    kept = jnp.where(odd_core, right, left)
    given = jnp.where(odd_core, left, right).astype(jnp.bfloat16)
    taken = lax.ppermute(given, "dp", [(i, i ^ 1) for i in range(dp_count)])
    pair_sum = (kept + taken.astype(jnp.float32)).astype(jnp.bfloat16)
    shares = lax.all_to_all(
        pair_sum.reshape(tile_count, share_rows, half), "tile", 0, 0, tiled=True
    )
    own_share = jnp.sum(shares.astype(jnp.float32), axis=0)
    copies = jnp.broadcast_to(own_share[None], (dp_count, share_rows, half))
    dp_shares = lax.all_to_all(copies, "dp", 0, 0, tiled=True)
    whole = jnp.sum(dp_shares.reshape(dp_count // 2, 2, share_rows, half), axis=0)
    return jnp.concatenate([whole[0], whole[1]], axis=1)


def on_device(
    image_descriptors,
    image_distance_scores,
    entry_sender_location,
    entry_receiver_square,
    entry_valid_tally,
    predicted_adjoint,
    initial_plane_filter,
    predictor_filter,
):
    snapshot_ordinal, horizontal_tally, vertical_tally, plane_tally = predicted_adjoint.shape
    depth_bins = image_distance_scores.shape[2]
    cell_total = horizontal_tally * vertical_tally
    tile_count = lax.axis_size("tile")
    depth_prob = jax.nn.softmax(image_distance_scores.astype(jnp.float32), axis=-1)
    flat_prob = depth_prob.reshape(snapshot_ordinal, -1)
    own_lists = entry_sender_location[:, 0]
    points = own_lists.reshape(snapshot_ordinal, -1)
    live_mask = (
        lax.broadcasted_iota(jnp.int32, own_lists.shape, 2) < entry_valid_tally[:, 0][:, :, None]
    ).reshape(snapshot_ordinal, -1)
    lifted = lift_values(image_descriptors, flat_prob, points, live_mask, depth_bins)
    lifted = lifted.reshape(own_lists.shape + (plane_tally,))
    arrived, arrived_cells = (
        lax.all_to_all(lifted, "tile", split_axis=1, concat_axis=1, tiled=True),
        lax.all_to_all(
            entry_receiver_square[:, 0], "tile", split_axis=1, concat_axis=1, tiled=True
        ),
    )
    values = arrived.reshape(snapshot_ordinal, -1, plane_tally)
    cell_ids = arrived_cells.reshape(snapshot_ordinal, -1)
    splat_sum = splat_frames(values, cell_ids, cell_total)
    norm_factor = lax.rsqrt(jnp.mean(splat_sum * splat_sum, axis=-1, keepdims=True) + epsilon)
    aerial_scene = (
        (splat_sum * norm_factor)
        .astype(jnp.bfloat16)
        .reshape(snapshot_ordinal, horizontal_tally, vertical_tally, plane_tally)
    )
    bev_wide = broadened_verticals(with_halo(aerial_scene, (("tile", 1),), 1))
    pre_first = stencil_offsets(
        bev_wide, initial_plane_filter, horizontal_tally, vertical_tally, False
    )
    hidden = jax.nn.silu(pre_first).astype(jnp.bfloat16)
    broadened_latent = broadened_verticals(with_halo(hidden, (("tile", 1),), 1))
    predicted_scene = (
        aerial_scene.astype(jnp.float32)
        + stencil_offsets(
            broadened_latent, predictor_filter, horizontal_tally, vertical_tally, False
        )
    ).astype(jnp.bfloat16)
    broadened_derivative = broadened_verticals(with_halo(predicted_adjoint, (("tile", 1),), 1))
    yielded_derivative = stencil_offsets(
        broadened_derivative, predictor_filter, horizontal_tally, vertical_tally, True
    )
    prenonlinear_derivative = (yielded_derivative * silu_slope(pre_first)).astype(jnp.bfloat16)
    patches = jnp.concatenate(
        [
            tap_window(broadened_latent, tap_index, horizontal_tally, vertical_tally, False)
            for tap_index in range(9)
        ],
        axis=-1,
    )
    patches = patches.reshape(-1, 9 * plane_tally)
    linear_derivative = predicted_adjoint.reshape(-1, plane_tally)
    share_rows = 9 * plane_tally // tile_count
    local_grad = lax.dot_general(
        patches, linear_derivative, (((0,), (0,)), ((), ())), preferred_element_type=jnp.float32
    )
    local_portion = reduced_gradient(local_grad, share_rows, tile_count)
    square_tally = (
        snapshot_ordinal * lax.axis_size("dp") * horizontal_tally * tile_count * vertical_tally
    )
    predictor_filter_derivative = local_portion / math.sqrt(square_tally)
    return (predicted_scene, prenonlinear_derivative, predictor_filter_derivative)


def solution(mesh):
    placed = (
        P("dp", "tile", None),
        P("dp", "tile", None),
        P("dp", "tile", None, None),
        P("dp", "tile", None, None),
        P("dp", "tile", None),
        P("dp", "tile", None, None),
        P(),
        P(),
    )
    return jax.shard_map(
        on_device,
        mesh=mesh,
        in_specs=placed,
        out_specs=(P("dp", "tile", None, None), P("dp", "tile", None, None), P("tile", None)),
        check_vma=False,
    )
```

```python
import functools
import math

import jax
import jax.numpy as jnp
from jax import lax
from jax.experimental import pallas as pl
from jax.experimental.pallas import tpu as pltpu
from jax.sharding import PartitionSpec as P

epsilon = 1e-05

F32 = jnp.float32
BF16 = jnp.bfloat16
LANES = 128
META_ROWS = 8
FINE = 16
VMEM_LIMIT = 48 * 1024 * 1024


def params():
    return pltpu.CompilerParams(vmem_limit_bytes=VMEM_LIMIT)


def vmem():
    return pl.BlockSpec(memory_space=pltpu.VMEM)


def turned(values, shift):
    return pltpu.roll(values, shift % values.shape[0], 0)


def pack_kernel(features, scores, points, cells, counts, message, meta):
    pixels, bins = scores.shape
    strips, slots = points.shape
    logits = scores[...].astype(F32)
    grown = jnp.exp(logits - jnp.max(logits, axis=1, keepdims=True))
    prob = grown / jnp.sum(grown, axis=1, keepdims=True)
    blank = jnp.zeros((pixels, LANES - bins), F32)
    prob = jnp.concatenate([prob, blank], axis=1)
    unused = jnp.zeros((strips, LANES - slots), jnp.int32)
    point = jnp.concatenate([points[...], unused], axis=1)
    cell = jnp.concatenate([cells[...], unused], axis=1)
    bin_index = point % bins
    pixel = point // bins
    weight = jnp.zeros((strips, LANES), F32)
    for p in range(pixels):
        row = jnp.broadcast_to(prob[p : p + 1], (strips, LANES))
        weight = jnp.where(pixel == p, jnp.take_along_axis(row, bin_index, axis=1), weight)
    across = lax.broadcasted_iota(jnp.int32, (strips, strips), 1)
    down = lax.broadcasted_iota(jnp.int32, (strips, strips), 0)
    tally = jnp.sum(
        jnp.where(across == down, counts[...].astype(F32), 0.0), axis=1, keepdims=True
    )
    lane = lax.broadcasted_iota(jnp.int32, (strips, LANES), 1)
    weight = jnp.where(lane.astype(F32) < tally, weight, 0.0)
    coarse = weight.astype(BF16).astype(F32)
    fields = (coarse, weight - coarse, pixel.astype(F32), (cell // FINE).astype(F32), (cell % FINE).astype(F32))
    meta[...] = jnp.zeros_like(meta)
    strip = lax.broadcasted_iota(jnp.int32, (strips, LANES), 0)
    for r, field in enumerate(fields):
        before = jnp.where(strip == 0, 0.0, turned(field, 1))
        after = jnp.where(strip == strips - 1, 0.0, turned(field, -1))
        here = pltpu.roll(field, slots, 1)
        meta[:, r, :LANES] = jnp.where(lane < slots, before, here)
        meta[:, r, LANES:] = jnp.where(lane < slots, after, 0.0)

    @pl.loop(0, strips)
    def _(t):
        message[t, :pixels] = features[...]
        message[t, pixels:] = meta[t].astype(BF16)


def splat_kernel(arrived, bev, meta, lifted, onehot):
    sources, rows, planes = arrived.shape
    pixels = rows - META_ROWS
    slots = LANES // 2
    wide = bev.shape[1]
    breadth = onehot.shape[0]
    lane = lax.broadcasted_iota(jnp.int32, (META_ROWS, LANES), 1)
    for j in range(sources // 2):
        first = arrived[2 * j, pixels:].astype(F32)
        second = arrived[2 * j + 1, pixels:].astype(F32)
        at = slice(j * LANES, (j + 1) * LANES)
        low = lane < slots
        a0, a1 = first[:, :LANES], first[:, LANES:]
        b0, b1 = second[:, :LANES], second[:, LANES:]
        meta[0, :, at] = jnp.where(low, a0, pltpu.roll(b0, slots, 1))
        meta[1, :, at] = jnp.where(low, pltpu.roll(a0, slots, 1), b0)
        meta[2, :, at] = jnp.where(low, a1, pltpu.roll(b1, slots, 1))
    batch = 4
    span = batch * slots
    depth = batch * pixels
    home = (lax.broadcasted_iota(jnp.int32, (1, span), 1) // slots * pixels).astype(F32)
    order = lax.broadcasted_iota(jnp.int32, (depth, span), 0).astype(F32)
    for g in range(sources // batch):
        block = jnp.concatenate([arrived[batch * g + i, :pixels] for i in range(batch)], axis=0)
        turned_block = block.astype(F32).T.astype(BF16)
        twice = jnp.concatenate([turned_block, turned_block], axis=1)
        at = slice(g * span, (g + 1) * span)
        for s in range(3):
            match = order == meta[s, 2:3, at] + home
            coarse = jnp.where(match, meta[s, 0:1, at], 0.0).astype(BF16)
            rest = jnp.where(match, meta[s, 1:2, at], 0.0).astype(BF16)
            lifted[s, :, at] = jnp.dot(
                twice, jnp.concatenate([coarse, rest], axis=0), preferred_element_type=F32
            ).astype(BF16)
    total = sources * slots
    fine = lax.broadcasted_iota(jnp.int32, (FINE, total), 0).astype(F32)
    blocks = breadth // FINE

    @pl.loop(0, 6)
    def _(k):
        s = k // 2
        begin = (k % 2 * blocks).astype(F32)
        comb = jnp.where(fine == meta[s, 4:5, :], 1.0, 0.0).astype(BF16)
        coarse = meta[s, 3:4, :]
        for b in range(blocks):
            chosen = jnp.where(coarse == begin + b, 1.0, 0.0).astype(BF16)
            onehot[b * FINE : (b + 1) * FINE, :] = comb * chosen
        summed = lax.dot_general(
            onehot[...], lifted[s], (((1,), (1,)), ((), ())), preferred_element_type=F32
        )
        factor = lax.rsqrt(jnp.mean(summed * summed, axis=1, keepdims=True) + epsilon)
        bev[k, :breadth] = (summed * factor).astype(BF16)
        bev[k, breadth:] = jnp.zeros((wide - breadth, planes), BF16)


def wide_weight(weight, planes):
    return jnp.concatenate(
        [
            jnp.concatenate(
                [weight[(a * 3 + b) * planes : (a * 3 + b + 1) * planes] for b in range(3)], axis=1
            )
            for a in range(3)
        ],
        axis=0,
    )


def conv_row(field, k, weight):
    planes = field.shape[2]
    stacked = jnp.concatenate([field[k - 1], field[k], field[k + 1]], axis=1)
    product = jnp.dot(stacked, weight, preferred_element_type=F32)
    return (
        product[:, planes : 2 * planes]
        + turned(product[:, :planes], 1)
        + turned(product[:, 2 * planes :], -1)
    )


def inside(shape, breadth):
    return lax.broadcasted_iota(jnp.int32, shape, 0) < breadth


def adjoint_kernel(breadth, own, above, below, weight, shifted, back):
    wide, planes = back.shape[1:]
    filler = jnp.zeros((wide - breadth, planes), F32)
    for k in range(4):
        row = (above[...], own[0], own[1], below[...])[k]
        row = jnp.concatenate([row.astype(F32), filler], axis=0)
        for b in range(3):
            shifted[b, k] = turned(row, b - 1).astype(BF16)
    flipped = jnp.concatenate(
        [weight[tap * planes : (tap + 1) * planes] for tap in range(9)], axis=1
    )
    for y in range(2):
        stacked = jnp.concatenate(
            [shifted[b, y + 2 - a] for a in range(3) for b in range(3)], axis=1
        )
        back[y] = lax.dot_general(
            stacked, flipped, (((1,), (1,)), ((), ())), preferred_element_type=F32
        )


def hidden_kernel(breadth, bev, weight, shifted, pre, hidden, kept, given):
    wide, planes = bev.shape[1:]
    grid = wide_weight(weight, planes)
    for y in range(2):
        value = conv_row(bev, y + 2, grid)
        pre[y] = value
        active = value * jax.nn.sigmoid(value)
        hidden[y] = jnp.where(inside(value.shape, breadth), active, 0.0).astype(BF16)
    turned_hidden = hidden[...].reshape(2 * wide, planes).astype(F32).T.astype(BF16)
    odd = lax.axis_index("dp") % 2 == 1
    half = planes // 2
    for a in range(3):
        for b in range(3):
            cotangent = shifted[b, 2 - a : 4 - a].reshape(2 * wide, planes)
            term = jnp.dot(turned_hidden, cotangent, preferred_element_type=F32)
            left, right = term[:, :half], term[:, half:]
            at = slice((a * 3 + b) * planes, (a * 3 + b + 1) * planes)
            kept[at] = jnp.where(odd, right, left)
            given[at] = jnp.where(odd, left, right).astype(BF16)


def outputs_kernel(breadth, bev, pre, hidden, back, first, second, scene, derivative, latent):
    wide, planes = bev.shape[1:]
    strip = lax.axis_index("tile")
    last = lax.axis_size("tile") - 1
    grid = wide_weight(first, planes)
    mask = inside((wide, planes), breadth)
    for k, edge in ((0, 0), (3, last)):
        value = conv_row(bev, k + 1, grid)
        active = value * jax.nn.sigmoid(value)
        keep = jnp.logical_and(mask, strip != edge)
        latent[k] = jnp.where(keep, active, 0.0).astype(BF16)
    latent[1] = hidden[0]
    latent[2] = hidden[1]
    grid = wide_weight(second, planes)
    for y in range(2):
        value = conv_row(latent, y + 1, grid)
        scene[y] = (bev[y + 2, :breadth].astype(F32) + value[:breadth]).astype(BF16)
        value = pre[y, :breadth]
        sigma = jax.nn.sigmoid(value)
        slope = sigma * (1.0 + value * (1.0 - sigma))
        derivative[y] = (back[y, :breadth] * slope).astype(BF16)


def reduced_gradient(kept, given, tile_count):
    dp_count = lax.axis_size("dp")
    rows, half = kept.shape
    share_rows = rows // tile_count
    taken = lax.ppermute(given, "dp", [(i, i ^ 1) for i in range(dp_count)])
    pair_sum = (kept + taken.astype(F32)).astype(BF16)
    shares = lax.all_to_all(
        pair_sum.reshape(tile_count, share_rows, half), "tile", 0, 0, tiled=True
    )
    own_share = jnp.sum(shares.astype(F32), axis=0)
    copies = jnp.broadcast_to(own_share[None], (dp_count, share_rows, half))
    dp_shares = lax.all_to_all(copies, "dp", 0, 0, tiled=True)
    whole = jnp.sum(dp_shares.reshape(dp_count // 2, 2, share_rows, half), axis=0)
    return jnp.concatenate([whole[0], whole[1]], axis=1)


def on_device(
    image_descriptors,
    image_distance_scores,
    entry_sender_location,
    entry_receiver_square,
    entry_valid_tally,
    predicted_adjoint,
    initial_plane_filter,
    predictor_filter,
):
    _, height, breadth, planes = predicted_adjoint.shape
    pixels = image_descriptors.shape[1]
    strips, slots = entry_sender_location.shape[2:]
    wide = breadth // 16 * 16 + 16
    taps = predictor_filter.shape[0]
    half = planes // 2
    struct = jax.ShapeDtypeStruct

    message = pl.pallas_call(
        pack_kernel,
        out_shape=struct((strips, pixels + META_ROWS, planes), BF16),
        in_specs=[vmem()] * 5,
        out_specs=vmem(),
        scratch_shapes=[pltpu.VMEM((strips, META_ROWS, planes), F32)],
        compiler_params=params(),
        name="pack",
    )(
        image_descriptors[0],
        image_distance_scores[0],
        entry_sender_location[0, 0],
        entry_receiver_square[0, 0],
        entry_valid_tally[0],
    )
    arrived = lax.all_to_all(message, "tile", 0, 0, tiled=True)

    own = predicted_adjoint[0]
    ends = strips - 1
    above = lax.ppermute(own[height - 1], "tile", [(i, i + 1) for i in range(ends)])
    below = lax.ppermute(own[0], "tile", [(i + 1, i) for i in range(ends)])
    shifted, back = pl.pallas_call(
        functools.partial(adjoint_kernel, breadth),
        out_shape=(struct((3, 4, wide, planes), BF16), struct((2, wide, planes), F32)),
        in_specs=[vmem()] * 4,
        out_specs=(vmem(), vmem()),
        compiler_params=params(),
        cost_estimate=pl.CostEstimate(flops=2 * 2 * wide * taps * planes, bytes_accessed=10**7, transcendentals=0),
        name="adjoint",
    )(own, above, below, predictor_filter)

    bev = pl.pallas_call(
        splat_kernel,
        out_shape=struct((6, wide, planes), BF16),
        in_specs=[vmem()],
        out_specs=vmem(),
        scratch_shapes=[
            pltpu.VMEM((3, META_ROWS, strips * slots), F32),
            pltpu.VMEM((3, planes, strips * slots), BF16),
            pltpu.VMEM((breadth, strips * slots), BF16),
        ],
        compiler_params=params(),
        name="splat",
    )(arrived)
    pre, hidden, kept, given = pl.pallas_call(
        functools.partial(hidden_kernel, breadth),
        out_shape=(
            struct((2, wide, planes), F32),
            struct((2, wide, planes), BF16),
            struct((taps, half), F32),
            struct((taps, half), BF16),
        ),
        in_specs=[vmem()] * 3,
        out_specs=(vmem(),) * 4,
        compiler_params=params(),
        name="hidden",
    )(bev, initial_plane_filter, shifted)
    scene, derivative = pl.pallas_call(
        functools.partial(outputs_kernel, breadth),
        out_shape=(struct((2, breadth, planes), BF16),) * 2,
        in_specs=[vmem()] * 6,
        out_specs=(vmem(),) * 2,
        scratch_shapes=[pltpu.VMEM((4, wide, planes), BF16)],
        compiler_params=params(),
        cost_estimate=pl.CostEstimate(flops=4 * 2 * wide * taps * planes, bytes_accessed=10**7, transcendentals=10**6),
        name="outputs",
    )(bev, pre, hidden, back, initial_plane_filter, predictor_filter)
    gradient = reduced_gradient(kept, given, strips)
    square_tally = lax.axis_size("dp") * height * strips * breadth
    return scene[None], derivative[None], gradient / math.sqrt(square_tally)


def solution(mesh):
    placed = (
        P("dp", "tile", None),
        P("dp", "tile", None),
        P("dp", "tile", None, None),
        P("dp", "tile", None, None),
        P("dp", "tile", None),
        P("dp", "tile", None, None),
        P(),
        P(),
    )
    return jax.shard_map(
        on_device,
        mesh=mesh,
        in_specs=placed,
        out_specs=(P("dp", "tile", None, None), P("dp", "tile", None, None), P("tile", None)),
        check_vma=False,
    )
```

```python
import functools
import math

import jax
import jax.numpy as jnp
from jax import lax
from jax.experimental import pallas as pl
from jax.experimental.pallas import tpu as pltpu
from jax.sharding import PartitionSpec as P

epsilon = 1e-05

F32 = jnp.float32
BF16 = jnp.bfloat16
LANES = 128
CODE = 128
FINE = 16


def params(mebibytes):
    return pltpu.CompilerParams(vmem_limit_bytes=mebibytes * 1024 * 1024)


def vmem():
    return pl.BlockSpec(memory_space=pltpu.VMEM)


def turned(values, shift):
    return pltpu.roll(values, shift % values.shape[0], 0)


def pack_kernel(features, scores, points, cells, counts, packed, score_buf, point_buf, cell_buf, count_buf, sems):
    copies = [
        pltpu.make_async_copy(source, target, sems.at[i])
        for i, (source, target) in enumerate(
            (
                (points, point_buf),
                (scores, score_buf),
                (cells, cell_buf),
                (counts, count_buf),
                (features, packed.at[: features.shape[0]]),
            )
        )
    ]
    for copy in copies:
        copy.start()
    for copy in copies:
        copy.wait()
    pixels, bins = scores.shape
    strips, slots = points.shape
    logits = score_buf[...].astype(F32)
    grown = jnp.exp(logits - jnp.max(logits, axis=1, keepdims=True))
    prob = grown / jnp.sum(grown, axis=1, keepdims=True)
    blank = jnp.zeros((pixels, LANES - bins), F32)
    prob = jnp.concatenate([prob, blank], axis=1)
    unused = jnp.zeros((strips, LANES - slots), jnp.int32)
    point = jnp.concatenate([point_buf[...], unused], axis=1)
    cell = jnp.concatenate([cell_buf[...], unused], axis=1)
    bin_index = point % bins
    pixel = point // bins
    weight = jnp.zeros((strips, LANES), F32)
    for p in range(pixels):
        row = jnp.broadcast_to(prob[p : p + 1], (strips, LANES))
        weight = jnp.where(pixel == p, jnp.take_along_axis(row, bin_index, axis=1), weight)
    across = lax.broadcasted_iota(jnp.int32, (strips, strips), 1)
    down = lax.broadcasted_iota(jnp.int32, (strips, strips), 0)
    tally = jnp.sum(
        jnp.where(across == down, count_buf[...].astype(F32), 0.0), axis=1, keepdims=True
    )
    lane = lax.broadcasted_iota(jnp.int32, (strips, LANES), 1)
    low = lane < slots
    weight = jnp.where(lane.astype(F32) < tally, weight, 0.0)
    coarse = weight.astype(BF16).astype(F32)
    upper = (pixel * 8 + cell // CODE).astype(F32)
    under = (cell % CODE).astype(F32)
    weights = jnp.where(low, coarse, pltpu.roll(weight - coarse, slots, 1))
    codes = jnp.where(low, upper, pltpu.roll(under, slots, 1))
    packed[pixels:] = jnp.concatenate([weights, codes], axis=1).astype(BF16)


def line_kernel(*refs):
    sources, messages, lists = refs[:2], refs[2:6], refs[6]
    strips = lax.axis_size("tile")
    plane = lax.axis_index("tile") // 4
    pixels, planes = sources[0].shape[0] - strips, sources[0].shape[1]
    for i in range(2):
        lists[i] = sources[i][pixels:].astype(F32)
    lane = lax.broadcasted_iota(jnp.int32, (1, planes), 1)
    for k in range(4):
        rows = []
        for i in range(2):
            messages[k][i * pixels : (i + 1) * pixels] = sources[i][:pixels]
            for j in range(8):
                wanted = 4 * (plane ^ k) + (j - 1)
                there = jnp.logical_and(wanted >= 0, wanted < strips)
                row = lists[i, pl.ds(jnp.clip(wanted, 0, strips - 1), 1), :]
                rows.append(jnp.where(jnp.logical_or(there, lane >= planes // 2), row, 0.0))
        messages[k][2 * pixels :] = jnp.concatenate(rows, axis=0).astype(BF16)


def strip_kernel(*refs):
    sources, messages, lists = refs[:4], refs[4:8], refs[8]
    pixels, planes = messages[0].shape[0] // 9, messages[0].shape[1]
    own = lax.axis_index("tile") % 4
    for i in range(4):
        lists[i] = sources[i][2 * pixels :].astype(F32)
    for k in range(4):
        rows = []
        for i in range(8):
            begin = i % 2 * pixels
            messages[k][i * pixels : (i + 1) * pixels] = sources[i // 2][begin : begin + pixels]
            for j in range(3):
                rows.append(lists[i // 2, pl.ds(i % 2 * 8 + (own ^ k) + j, 1), :])
        rows.append(jnp.zeros((8, planes), F32))
        messages[k][8 * pixels :] = jnp.concatenate(rows, axis=0).astype(BF16)


def lift(messages, meta, lifted):
    pixels = messages[0].shape[0] // 9
    slots = LANES // 2
    batch = 4
    span = batch * slots
    depth = batch * pixels
    low = lax.broadcasted_iota(jnp.int32, (1, LANES), 1) < slots
    home = (lax.broadcasted_iota(jnp.int32, (1, span), 1) // slots * pixels).astype(F32)
    order = lax.broadcasted_iota(jnp.int32, (depth, span), 0).astype(F32)
    for m, message in enumerate(messages):
        lists = message[8 * pixels :].astype(F32)
        halves = []
        for h in range(2):
            straight = lists[:, h * LANES : (h + 1) * LANES]
            halves.append((straight, pltpu.roll(straight, slots, 1)))
        for g in range(2):
            block = message[g * depth : (g + 1) * depth]
            turned_block = block.astype(F32).T.astype(BF16)
            twice = jnp.concatenate([turned_block, turned_block], axis=1)
            at = slice((2 * m + g) * span, (2 * m + g + 1) * span)
            for s in range(3):
                fields = []
                for straight, rolled in halves:
                    first, second = [], []
                    for p in range(2):
                        r0 = 3 * (batch * g + 2 * p) + s
                        r1 = r0 + 3
                        first.append(jnp.where(low, straight[r0 : r0 + 1], rolled[r1 : r1 + 1]))
                        second.append(jnp.where(low, rolled[r0 : r0 + 1], straight[r1 : r1 + 1]))
                    fields.append(jnp.concatenate(first, axis=1))
                    fields.append(jnp.concatenate(second, axis=1))
                coarse, rest, upper, under = fields
                pixel = jnp.floor(upper * 0.125)
                sixteenths = jnp.floor(under * (1.0 / FINE))
                meta[s, 0:1, at] = (upper - 8.0 * pixel) * (CODE // FINE) + sixteenths
                meta[s, 1:2, at] = under - FINE * sixteenths
                match = order == pixel + home
                coarse = jnp.where(match, coarse, 0.0).astype(BF16)
                rest = jnp.where(match, rest, 0.0).astype(BF16)
                lifted[s, :, at] = jnp.dot(
                    twice, jnp.concatenate([coarse, rest], axis=0), preferred_element_type=F32
                ).astype(BF16)


def splat_row(s, r, meta, lifted, onehot):
    breadth, total = onehot.shape
    blocks = breadth // FINE
    fine = lax.broadcasted_iota(jnp.int32, (FINE, total), 0).astype(F32)
    comb = jnp.where(fine == meta[s, 1:2, :], 1.0, 0.0).astype(BF16)
    coarse = meta[s, 0:1, :]
    begin = r * blocks
    for b in range(blocks):
        chosen = jnp.where(coarse == (begin + b).astype(F32), 1.0, 0.0).astype(BF16)
        onehot[b * FINE : (b + 1) * FINE, :] = comb * chosen
    return lax.dot_general(
        onehot[...], lifted[s], (((1,), (1,)), ((), ())), preferred_element_type=F32
    )


def normalized(summed, bev, k):
    breadth, planes = summed.shape
    wide = bev.shape[1]
    factor = lax.rsqrt(jnp.mean(summed * summed, axis=1, keepdims=True) + epsilon)
    bev[k, :breadth] = (summed * factor).astype(BF16)
    bev[k, breadth:] = jnp.zeros((wide - breadth, planes), BF16)


def plane_kernel(message, partial, meta, lifted, onehot):
    lift([message], meta, lifted)

    @pl.loop(0, 6)
    def _(k):
        partial[k] = splat_row(k // 2, k % 2, meta, lifted, onehot)


def splat_kernel(one, two, three, partial, bev, meta, lifted, onehot):
    lift([one, two, three], meta, lifted)

    @pl.loop(0, 6)
    def _(k):
        normalized(partial[k] + splat_row(k // 2, k % 2, meta, lifted, onehot), bev, k)


def wide_weight(weight, planes):
    return jnp.concatenate(
        [
            jnp.concatenate(
                [weight[(a * 3 + b) * planes : (a * 3 + b + 1) * planes] for b in range(3)], axis=1
            )
            for a in range(3)
        ],
        axis=0,
    )


def conv_row(field, k, weight):
    planes = field.shape[2]
    stacked = jnp.concatenate([field[k - 1], field[k], field[k + 1]], axis=1)
    product = jnp.dot(stacked, weight, preferred_element_type=F32)
    return (
        product[:, planes : 2 * planes]
        + turned(product[:, :planes], 1)
        + turned(product[:, 2 * planes :], -1)
    )


def inside(shape, breadth):
    return lax.broadcasted_iota(jnp.int32, shape, 0) < breadth


def moved_kernel(breadth, own, shifted):
    wide = shifted.shape[1]
    planes = own.shape[2]
    filler = jnp.zeros((wide - breadth, planes), F32)
    for y in range(2):
        row = jnp.concatenate([own[y].astype(F32), filler], axis=0)
        for b in range(3):
            shifted[y, :, b * planes : (b + 1) * planes] = turned(row, b - 1).astype(BF16)


def hidden_kernel(breadth, bev, weight, shifted, pre, hidden, kept, given):
    wide, planes = bev.shape[1:]
    strip = lax.axis_index("tile")
    last = lax.axis_size("tile") - 1
    odd = lax.axis_index("dp") % 2 == 1
    half = planes // 2
    grid = wide_weight(weight, planes)
    mask = inside((wide, planes), breadth)
    columns = []
    for k in range(4):
        value = conv_row(bev, k + 1, grid)
        if k in (1, 2):
            pre[k - 1] = value
        keep = mask
        if k == 0:
            keep = jnp.logical_and(mask, strip != 0)
        if k == 3:
            keep = jnp.logical_and(mask, strip != last)
        active = jnp.where(keep, value * jax.nn.sigmoid(value), 0.0)
        hidden[k] = active.astype(BF16)
        columns.append(active.T.astype(BF16))
    for a in range(3):
        terms = jnp.dot(columns[a], shifted[0], preferred_element_type=F32)
        terms = terms + jnp.dot(columns[a + 1], shifted[1], preferred_element_type=F32)
        for b in range(3):
            left = terms[:, b * planes : b * planes + half]
            right = terms[:, b * planes + half : (b + 1) * planes]
            at = slice((a * 3 + b) * planes, (a * 3 + b + 1) * planes)
            kept[at] = jnp.where(odd, right, left)
            given[at] = jnp.where(odd, left, right).astype(BF16)


def scene_kernel(breadth, bev, hidden, weight, scene):
    grid = wide_weight(weight, bev.shape[2])
    for y in range(2):
        value = conv_row(hidden, y + 1, grid)
        scene[y] = (bev[y + 2, :breadth].astype(F32) + value[:breadth]).astype(BF16)


def derivative_kernel(breadth, own, first, second, weight, pre, derivative, field):
    wide, planes = pre.shape[1:]
    strip = lax.axis_index("tile")
    odd = strip % 2 == 1
    blank = jnp.zeros((wide - breadth, planes), BF16)
    zero = jnp.zeros((breadth, planes), BF16)
    above = jnp.where(odd, first[...], jnp.where(strip == 0, zero, second[...]))
    below = jnp.where(
        odd, jnp.where(strip == lax.axis_size("tile") - 1, zero, second[...]), first[...]
    )
    for k, row in enumerate((above, own[0], own[1], below)):
        field[k, :breadth] = row
        field[k, breadth:] = blank
    flipped = jnp.concatenate(
        [
            jnp.concatenate(
                [weight[(a * 3 + b) * planes : (a * 3 + b + 1) * planes] for a in (2, 1, 0)], axis=1
            )
            for b in (2, 1, 0)
        ],
        axis=0,
    )
    for y in range(2):
        stacked = jnp.concatenate([field[y], field[y + 1], field[y + 2]], axis=1)
        product = lax.dot_general(
            stacked, flipped, (((1,), (1,)), ((), ())), preferred_element_type=F32
        )
        back = (
            product[:, planes : 2 * planes]
            + turned(product[:, :planes], 1)
            + turned(product[:, 2 * planes :], -1)
        )
        value = pre[y, :breadth]
        sigma = jax.nn.sigmoid(value)
        slope = sigma * (1.0 + value * (1.0 - sigma))
        derivative[y] = (back[:breadth] * slope).astype(BF16)


def parts_kernel(kept, taken, *parts):
    own = lax.axis_index("tile") % 4
    for p in range(kept.shape[0] // 4):
        for k in range(4):
            t = 4 * p + (own ^ k)
            parts[k][p] = (kept[t] + taken[t].astype(F32)).astype(parts[k].dtype)


def planes_kernel(first, one, two, three, *parts):
    plane = lax.axis_index("tile") // 4
    for k in range(4):
        for i, p in enumerate((plane ^ k, 7 - (plane ^ k))):
            total = first[p] + one[p].astype(F32) + two[p].astype(F32) + three[p].astype(F32)
            parts[k][i] = total.astype(parts[k].dtype)


def swap(values, axis, partner):
    return lax.ppermute(values, axis, [(i, partner(i)) for i in range(lax.axis_size(axis))])


def line_swap(k):
    return lambda i: i ^ k


def mirror(i):
    return 28 - i // 4 * 4 + i % 4


def added(first, *others):
    for other in others:
        first = first + other.astype(F32)
    return first


def on_device(
    image_descriptors,
    image_distance_scores,
    entry_sender_location,
    entry_receiver_square,
    entry_valid_tally,
    predicted_adjoint,
    initial_plane_filter,
    predictor_filter,
):
    _, height, breadth, planes = predicted_adjoint.shape
    pixels = image_descriptors.shape[1]
    strips, slots = entry_sender_location.shape[2:]
    wide = breadth // 16 * 16 + 16
    taps = predictor_filter.shape[0]
    half = planes // 2
    struct = jax.ShapeDtypeStruct

    places = pixels + strips
    packed = pl.pallas_call(
        pack_kernel,
        out_shape=struct((places, planes), BF16),
        in_specs=[pl.BlockSpec(memory_space=pl.ANY)] * 5,
        out_specs=vmem(),
        scratch_shapes=[
            pltpu.VMEM((pixels, image_distance_scores.shape[2]), BF16),
            pltpu.VMEM((strips, slots), jnp.int32),
            pltpu.VMEM((strips, slots), jnp.int32),
            pltpu.VMEM((1, strips), jnp.int32),
            pltpu.SemaphoreType.DMA((5,)),
        ],
        compiler_params=params(60),
        name="pack",
    )(
        image_descriptors[0],
        image_distance_scores[0],
        entry_sender_location[0, 0],
        entry_receiver_square[0, 0],
        entry_valid_tally[0],
    )
    line = pl.pallas_call(
        line_kernel,
        out_shape=(struct((2 * pixels + 16, planes), BF16),) * 4,
        in_specs=[vmem()] * 2,
        out_specs=(vmem(),) * 4,
        scratch_shapes=[pltpu.VMEM((2, strips, planes), F32)],
        compiler_params=params(4),
        name="line",
    )(packed, swap(packed, "tile", mirror))
    line = [line[0]] + [swap(line[k], "tile", line_swap(4 * k)) for k in (1, 2, 3)]
    messages = pl.pallas_call(
        strip_kernel,
        out_shape=(struct((9 * pixels, planes), BF16),) * 4,
        in_specs=[vmem()] * 4,
        out_specs=(vmem(),) * 4,
        scratch_shapes=[pltpu.VMEM((4, 16, planes), F32)],
        compiler_params=params(4),
        name="strip",
    )(*line)
    arrived = [swap(messages[k], "tile", line_swap(k)) for k in (1, 2, 3)]

    own = predicted_adjoint[0]
    shifted = pl.pallas_call(
        functools.partial(moved_kernel, breadth),
        out_shape=struct((2, wide, 3 * planes), BF16),
        in_specs=[vmem()],
        out_specs=vmem(),
        compiler_params=params(8),
        cost_estimate=pl.CostEstimate(flops=10**6, bytes_accessed=10**6, transcendentals=0),
        name="moved",
    )(own)

    def splat_scratch(count):
        total = count * 8 * slots
        return [
            pltpu.VMEM((3, 8, total), F32),
            pltpu.VMEM((3, planes, total), BF16),
            pltpu.VMEM((breadth, total), BF16),
        ]

    partial = pl.pallas_call(
        plane_kernel,
        out_shape=struct((6, breadth, planes), F32),
        in_specs=[vmem()],
        out_specs=vmem(),
        scratch_shapes=splat_scratch(1),
        compiler_params=params(16),
        cost_estimate=pl.CostEstimate(flops=2 * 6 * breadth * 8 * slots * planes, bytes_accessed=10**6, transcendentals=0),
        name="plane",
    )(messages[0])
    bev = pl.pallas_call(
        splat_kernel,
        out_shape=struct((6, wide, planes), BF16),
        in_specs=[vmem()] * 4,
        out_specs=vmem(),
        scratch_shapes=splat_scratch(3),
        compiler_params=params(20),
        name="splat",
    )(*arrived, partial)
    pre, hidden, kept, given = pl.pallas_call(
        functools.partial(hidden_kernel, breadth),
        out_shape=(
            struct((2, wide, planes), F32),
            struct((4, wide, planes), BF16),
            struct((taps, half), F32),
            struct((taps, half), BF16),
        ),
        in_specs=[vmem()] * 3,
        out_specs=(vmem(),) * 4,
        compiler_params=params(20),
        name="hidden",
    )(bev, initial_plane_filter, shifted)

    share = taps // strips
    taken = swap(given, "dp", line_swap(1))
    parts = pl.pallas_call(
        parts_kernel,
        out_shape=tuple(struct((strips // 4, share, half), F32 if k == 0 else BF16) for k in range(4)),
        in_specs=[vmem()] * 2,
        out_specs=(vmem(),) * 4,
        compiler_params=params(8),
        name="parts",
    )(kept.reshape(strips, share, half), taken.reshape(strips, share, half))
    fetched = [swap(parts[k], "tile", line_swap(k)) for k in (1, 2, 3)]
    scene = pl.pallas_call(
        functools.partial(scene_kernel, breadth),
        out_shape=struct((2, breadth, planes), BF16),
        in_specs=[vmem()] * 3,
        out_specs=vmem(),
        compiler_params=params(16),
        cost_estimate=pl.CostEstimate(flops=2 * 2 * wide * taps * planes, bytes_accessed=10**6, transcendentals=0),
        name="scene",
    )(bev, hidden, predictor_filter)
    fetched, scene = lax.optimization_barrier((fetched, scene))
    pairs = pl.pallas_call(
        planes_kernel,
        out_shape=tuple(struct((2, share, half), F32 if k == 0 else BF16) for k in range(4)),
        in_specs=[vmem()] * 4,
        out_specs=(vmem(),) * 4,
        compiler_params=params(8),
        name="planes",
    )(parts[0], *fetched)
    fetched = [swap(pairs[k], "tile", line_swap(4 * k)) for k in (1, 2, 3)]
    pair = added(pairs[0], *fetched)
    ours = pair[0]
    theirs = pair[1].astype(BF16)
    strip = lax.axis_index("tile")
    near = jnp.where(strip % 2 == 1, own[0], own[height - 1])
    far = jnp.where(strip % 2 == 1, own[height - 1], own[0])
    theirs, near, far = lax.optimization_barrier((theirs, near, far))
    ours = added(ours, swap(theirs, "tile", mirror))
    first = swap(near, "tile", line_swap(1))
    second = swap(far, "tile", lambda i: (i - 1 + 2 * (i % 2)) % strips)
    fetched = [swap(ours, "dp", line_swap(2 * k)) for k in (1, 2, 3)]
    derivative = pl.pallas_call(
        functools.partial(derivative_kernel, breadth),
        out_shape=struct((2, breadth, planes), BF16),
        in_specs=[vmem()] * 5,
        out_specs=vmem(),
        scratch_shapes=[pltpu.VMEM((4, wide, planes), BF16)],
        compiler_params=params(16),
        cost_estimate=pl.CostEstimate(flops=2 * 2 * wide * taps * planes, bytes_accessed=10**6, transcendentals=10**6),
        name="derivative",
    )(own, first, second, predictor_filter, pre)
    fetched, derivative = lax.optimization_barrier((fetched, derivative))
    ours = added(ours, *fetched)
    other = swap(ours, "dp", line_swap(1))
    odd = lax.axis_index("dp") % 2 == 1
    gradient = jnp.concatenate([jnp.where(odd, other, ours), jnp.where(odd, ours, other)], axis=1)
    square_tally = lax.axis_size("dp") * height * strips * breadth
    return scene[None], derivative[None], gradient / math.sqrt(square_tally)


def solution(mesh):
    placed = (
        P("dp", "tile", None),
        P("dp", "tile", None),
        P("dp", "tile", None, None),
        P("dp", "tile", None, None),
        P("dp", "tile", None),
        P("dp", "tile", None, None),
        P(),
        P(),
    )
    return jax.shard_map(
        on_device,
        mesh=mesh,
        in_specs=placed,
        out_specs=(P("dp", "tile", None, None), P("dp", "tile", None, None), P("tile", None)),
        check_vma=False,
    )
```

```python
import functools
import math

import jax
import jax.numpy as jnp
from jax import lax
from jax.experimental import pallas as pl
from jax.experimental.pallas import tpu as pltpu
from jax.sharding import PartitionSpec as P

epsilon = 1e-05

F32 = jnp.float32
BF16 = jnp.bfloat16
LANES = 128
CODE = 128
FINE = 16


def params(mebibytes):
    return pltpu.CompilerParams(vmem_limit_bytes=mebibytes * 1024 * 1024)


def vmem():
    return pl.BlockSpec(memory_space=pltpu.VMEM)


def far_held(values):
    return pltpu.with_memory_space_constraint(values, pltpu.HBM)


def turned(values, shift):
    return pltpu.roll(values, shift % values.shape[0], 0)


def pack_kernel(features, scores, points, cells, counts, packed, score_buf, point_buf, cell_buf, count_buf, sems):
    copies = [
        pltpu.make_async_copy(source, target, sems.at[i])
        for i, (source, target) in enumerate(
            (
                (points, point_buf),
                (scores, score_buf),
                (cells, cell_buf),
                (counts, count_buf),
                (features, packed.at[: features.shape[0]]),
            )
        )
    ]
    for copy in copies:
        copy.start()
    for copy in copies:
        copy.wait()
    pixels, bins = scores.shape
    strips, slots = points.shape
    logits = score_buf[...].astype(F32)
    grown = jnp.exp(logits - jnp.max(logits, axis=1, keepdims=True))
    prob = grown / jnp.sum(grown, axis=1, keepdims=True)
    blank = jnp.zeros((pixels, LANES - bins), F32)
    prob = jnp.concatenate([prob, blank], axis=1)
    unused = jnp.zeros((strips, LANES - slots), jnp.int32)
    point = jnp.concatenate([point_buf[...], unused], axis=1)
    cell = jnp.concatenate([cell_buf[...], unused], axis=1)
    bin_index = point % bins
    pixel = point // bins
    weight = jnp.zeros((strips, LANES), F32)
    for p in range(pixels):
        row = jnp.broadcast_to(prob[p : p + 1], (strips, LANES))
        weight = jnp.where(pixel == p, jnp.take_along_axis(row, bin_index, axis=1), weight)
    across = lax.broadcasted_iota(jnp.int32, (strips, strips), 1)
    down = lax.broadcasted_iota(jnp.int32, (strips, strips), 0)
    tally = jnp.sum(
        jnp.where(across == down, count_buf[...].astype(F32), 0.0), axis=1, keepdims=True
    )
    lane = lax.broadcasted_iota(jnp.int32, (strips, LANES), 1)
    low = lane < slots
    weight = jnp.where(lane.astype(F32) < tally, weight, 0.0)
    coarse = weight.astype(BF16).astype(F32)
    upper = (pixel * 8 + cell // CODE).astype(F32)
    under = (cell % CODE).astype(F32)
    weights = jnp.where(low, coarse, pltpu.roll(weight - coarse, slots, 1))
    codes = jnp.where(low, upper, pltpu.roll(under, slots, 1))
    packed[pixels:] = jnp.concatenate([weights, codes], axis=1).astype(BF16)


def line_kernel(*refs):
    sources, messages, lists = refs[:2], refs[2:6], refs[6]
    strips = lax.axis_size("tile")
    plane = lax.axis_index("tile") // 4
    pixels, planes = sources[0].shape[0] - strips, sources[0].shape[1]
    for i in range(2):
        lists[i] = sources[i][pixels:].astype(F32)
    lane = lax.broadcasted_iota(jnp.int32, (1, planes), 1)
    for k in range(4):
        rows = []
        for i in range(2):
            messages[k][i * pixels : (i + 1) * pixels] = sources[i][:pixels]
            for j in range(8):
                wanted = 4 * (plane ^ k) + (j - 1)
                there = jnp.logical_and(wanted >= 0, wanted < strips)
                row = lists[i, pl.ds(jnp.clip(wanted, 0, strips - 1), 1), :]
                rows.append(jnp.where(jnp.logical_or(there, lane >= planes // 2), row, 0.0))
        messages[k][2 * pixels :] = jnp.concatenate(rows, axis=0).astype(BF16)


def strip_kernel(*refs):
    sources, messages, lists = refs[:4], refs[4:8], refs[8]
    pixels, planes = messages[0].shape[0] // 9, messages[0].shape[1]
    own = lax.axis_index("tile") % 4
    for i in range(4):
        lists[i] = sources[i][2 * pixels :].astype(F32)
    for k in range(4):
        rows = []
        for i in range(8):
            begin = i % 2 * pixels
            messages[k][i * pixels : (i + 1) * pixels] = sources[i // 2][begin : begin + pixels]
            for j in range(3):
                rows.append(lists[i // 2, pl.ds(i % 2 * 8 + (own ^ k) + j, 1), :])
        rows.append(jnp.zeros((8, planes), F32))
        messages[k][8 * pixels :] = jnp.concatenate(rows, axis=0).astype(BF16)


def lift(messages, meta, lifted):
    pixels = messages[0].shape[0] // 9
    slots = LANES // 2
    batch = 4
    span = batch * slots
    depth = batch * pixels
    low = lax.broadcasted_iota(jnp.int32, (1, LANES), 1) < slots
    home = (lax.broadcasted_iota(jnp.int32, (1, span), 1) // slots * pixels).astype(F32)
    order = lax.broadcasted_iota(jnp.int32, (depth, span), 0).astype(F32)
    for m, message in enumerate(messages):
        lists = message[8 * pixels :].astype(F32)
        halves = []
        for h in range(2):
            straight = lists[:, h * LANES : (h + 1) * LANES]
            halves.append((straight, pltpu.roll(straight, slots, 1)))
        for g in range(2):
            block = message[g * depth : (g + 1) * depth]
            turned_block = block.astype(F32).T.astype(BF16)
            twice = jnp.concatenate([turned_block, turned_block], axis=1)
            at = slice((2 * m + g) * span, (2 * m + g + 1) * span)
            for s in range(3):
                fields = []
                for straight, rolled in halves:
                    first, second = [], []
                    for p in range(2):
                        r0 = 3 * (batch * g + 2 * p) + s
                        r1 = r0 + 3
                        first.append(jnp.where(low, straight[r0 : r0 + 1], rolled[r1 : r1 + 1]))
                        second.append(jnp.where(low, rolled[r0 : r0 + 1], straight[r1 : r1 + 1]))
                    fields.append(jnp.concatenate(first, axis=1))
                    fields.append(jnp.concatenate(second, axis=1))
                coarse, rest, upper, under = fields
                pixel = jnp.floor(upper * 0.125)
                sixteenths = jnp.floor(under * (1.0 / FINE))
                meta[s, 0:1, at] = (upper - 8.0 * pixel) * (CODE // FINE) + sixteenths
                meta[s, 1:2, at] = under - FINE * sixteenths
                match = order == pixel + home
                coarse = jnp.where(match, coarse, 0.0).astype(BF16)
                rest = jnp.where(match, rest, 0.0).astype(BF16)
                lifted[s, :, at] = jnp.dot(
                    twice, jnp.concatenate([coarse, rest], axis=0), preferred_element_type=F32
                ).astype(BF16)


def splat_row(k, meta, lifted, onehot):
    s, r = k // 2, k % 2
    breadth, total = onehot.shape[1:]
    blocks = breadth // FINE
    fine = lax.broadcasted_iota(jnp.int32, (FINE, total), 0).astype(F32)
    comb = jnp.where(fine == meta[s, 1:2, :], 1.0, 0.0).astype(BF16)
    coarse = meta[s, 0:1, :]
    for b in range(blocks):
        chosen = jnp.where(coarse == float(r * blocks + b), 1.0, 0.0).astype(BF16)
        onehot[k % 2, b * FINE : (b + 1) * FINE, :] = comb * chosen
    return lax.dot_general(
        onehot[k % 2], lifted[s], (((1,), (1,)), ((), ())), preferred_element_type=F32
    )


def normalized(summed, bev, k):
    breadth, planes = summed.shape
    wide = bev.shape[1]
    factor = lax.rsqrt(jnp.mean(summed * summed, axis=1, keepdims=True) + epsilon)
    bev[k, :breadth] = (summed * factor).astype(BF16)
    bev[k, breadth:] = jnp.zeros((wide - breadth, planes), BF16)


def plane_kernel(message, sums, meta, lifted, onehot):
    lift([message], meta, lifted)
    for k in range(6):
        sums[k] = splat_row(k, meta, lifted, onehot)


def more_kernel(message, before, sums, meta, lifted, onehot):
    lift([message], meta, lifted)
    for k in range(6):
        sums[k] = before[k] + splat_row(k, meta, lifted, onehot)


def splat_kernel(two, three, before, bev, meta, lifted, onehot):
    lift([two, three], meta, lifted)
    for k in range(6):
        normalized(before[k] + splat_row(k, meta, lifted, onehot), bev, k)


def wide_weight(weight, planes):
    return jnp.concatenate(
        [
            jnp.concatenate(
                [weight[(a * 3 + b) * planes : (a * 3 + b + 1) * planes] for b in range(3)], axis=1
            )
            for a in range(3)
        ],
        axis=0,
    )


def conv_row(field, k, weight):
    planes = field.shape[2]
    stacked = jnp.concatenate([field[k - 1], field[k], field[k + 1]], axis=1)
    product = jnp.dot(stacked, weight, preferred_element_type=F32)
    return (
        product[:, planes : 2 * planes]
        + turned(product[:, :planes], 1)
        + turned(product[:, 2 * planes :], -1)
    )


def inside(shape, breadth):
    return lax.broadcasted_iota(jnp.int32, shape, 0) < breadth


def moved_kernel(breadth, own, shifted, near, far):
    odd = lax.axis_index("tile") % 2 == 1
    near[...] = jnp.where(odd, own[0], own[1])
    far[...] = jnp.where(odd, own[1], own[0])
    wide = shifted.shape[1]
    planes = own.shape[2]
    filler = jnp.zeros((wide - breadth, planes), F32)
    for y in range(2):
        row = jnp.concatenate([own[y].astype(F32), filler], axis=0)
        for b in range(3):
            shifted[y, :, b * planes : (b + 1) * planes] = turned(row, b - 1).astype(BF16)


def hidden_kernel(breadth, bev, weight, shifted, pre, hidden, kept, given):
    wide, planes = bev.shape[1:]
    strip = lax.axis_index("tile")
    last = lax.axis_size("tile") - 1
    odd = lax.axis_index("dp") % 2 == 1
    half = planes // 2
    grid = wide_weight(weight, planes)
    mask = inside((wide, planes), breadth)
    columns = []
    for k in range(4):
        value = conv_row(bev, k + 1, grid)
        if k in (1, 2):
            pre[k - 1] = value
        keep = mask
        if k == 0:
            keep = jnp.logical_and(mask, strip != 0)
        if k == 3:
            keep = jnp.logical_and(mask, strip != last)
        active = jnp.where(keep, value * jax.nn.sigmoid(value), 0.0)
        hidden[k] = active.astype(BF16)
        columns.append(active.T.astype(BF16))
    for a in range(3):
        terms = jnp.dot(columns[a], shifted[0], preferred_element_type=F32)
        terms = terms + jnp.dot(columns[a + 1], shifted[1], preferred_element_type=F32)
        for b in range(3):
            left = terms[:, b * planes : b * planes + half]
            right = terms[:, b * planes + half : (b + 1) * planes]
            at = slice((a * 3 + b) * planes, (a * 3 + b + 1) * planes)
            kept[at] = jnp.where(odd, right, left)
            given[at] = jnp.where(odd, left, right).astype(BF16)


def scene_kernel(breadth, bev, hidden, weight, scene):
    grid = wide_weight(weight, bev.shape[2])
    for y in range(2):
        value = conv_row(hidden, y + 1, grid)
        scene[y] = (bev[y + 2, :breadth].astype(F32) + value[:breadth]).astype(BF16)


def derivative_kernel(breadth, own, first, second, weight, pre, derivative, field):
    wide, planes = pre.shape[1:]
    strip = lax.axis_index("tile")
    odd = strip % 2 == 1
    blank = jnp.zeros((wide - breadth, planes), BF16)
    zero = jnp.zeros((breadth, planes), BF16)
    above = jnp.where(odd, first[...], jnp.where(strip == 0, zero, second[...]))
    below = jnp.where(
        odd, jnp.where(strip == lax.axis_size("tile") - 1, zero, second[...]), first[...]
    )
    for k, row in enumerate((above, own[0], own[1], below)):
        field[k, :breadth] = row
        field[k, breadth:] = blank
    flipped = jnp.concatenate(
        [
            jnp.concatenate(
                [weight[(a * 3 + b) * planes : (a * 3 + b + 1) * planes] for a in (2, 1, 0)], axis=1
            )
            for b in (2, 1, 0)
        ],
        axis=0,
    )
    for y in range(2):
        stacked = jnp.concatenate([field[y], field[y + 1], field[y + 2]], axis=1)
        product = lax.dot_general(
            stacked, flipped, (((1,), (1,)), ((), ())), preferred_element_type=F32
        )
        back = (
            product[:, planes : 2 * planes]
            + turned(product[:, :planes], 1)
            + turned(product[:, 2 * planes :], -1)
        )
        value = pre[y, :breadth]
        sigma = jax.nn.sigmoid(value)
        slope = sigma * (1.0 + value * (1.0 - sigma))
        derivative[y] = (back[:breadth] * slope).astype(BF16)


def parts_kernel(kept, taken, *parts):
    own = lax.axis_index("tile") % 4
    for p in range(kept.shape[0] // 4):
        for k in range(4):
            t = 4 * p + (own ^ k)
            parts[k][p] = (kept[t] + taken[t].astype(F32)).astype(parts[k].dtype)


def planes_kernel(first, one, two, three, *parts):
    plane = lax.axis_index("tile") // 4
    for k in range(4):
        for i, p in enumerate((plane ^ k, 7 - (plane ^ k))):
            total = first[p] + one[p].astype(F32) + two[p].astype(F32) + three[p].astype(F32)
            parts[k][i] = total.astype(parts[k].dtype)


def gradient_kernel(scale, ours, other, gradient):
    odd = lax.axis_index("dp") % 2 == 1
    half = ours.shape[1]
    mine, theirs = ours[...] * scale, other[...] * scale
    gradient[:, :half] = jnp.where(odd, theirs, mine)
    gradient[:, half:] = jnp.where(odd, mine, theirs)


def swap(values, axis, partner):
    return lax.ppermute(values, axis, [(i, partner(i)) for i in range(lax.axis_size(axis))])


def line_swap(k):
    return lambda i: i ^ k


def mirror(i):
    return 28 - i // 4 * 4 + i % 4


def added(first, *others):
    for other in others:
        first = first + other.astype(F32)
    return first


def on_device(
    image_descriptors,
    image_distance_scores,
    entry_sender_location,
    entry_receiver_square,
    entry_valid_tally,
    predicted_adjoint,
    initial_plane_filter,
    predictor_filter,
):
    _, height, breadth, planes = predicted_adjoint.shape
    pixels = image_descriptors.shape[1]
    strips, slots = entry_sender_location.shape[2:]
    wide = breadth // 16 * 16 + 16
    taps = predictor_filter.shape[0]
    half = planes // 2
    struct = jax.ShapeDtypeStruct
    held = pltpu.VMEM

    places = pixels + strips
    packed = pl.pallas_call(
        pack_kernel,
        out_shape=held((places, planes), BF16),
        in_specs=[pl.BlockSpec(memory_space=pl.ANY)] * 5,
        out_specs=vmem(),
        scratch_shapes=[
            pltpu.VMEM((pixels, image_distance_scores.shape[2]), BF16),
            pltpu.VMEM((strips, slots), jnp.int32),
            pltpu.VMEM((strips, slots), jnp.int32),
            pltpu.VMEM((1, strips), jnp.int32),
            pltpu.SemaphoreType.DMA((5,)),
        ],
        compiler_params=params(8),
        name="pack",
    )(
        far_held(image_descriptors[0]),
        far_held(image_distance_scores[0]),
        far_held(entry_sender_location[0, 0]),
        far_held(entry_receiver_square[0, 0]),
        far_held(entry_valid_tally[0]),
    )
    line = pl.pallas_call(
        line_kernel,
        out_shape=(held((2 * pixels + 16, planes), BF16),) * 4,
        in_specs=[vmem()] * 2,
        out_specs=(vmem(),) * 4,
        scratch_shapes=[pltpu.VMEM((2, strips, planes), F32)],
        compiler_params=params(4),
        name="line",
    )(packed, swap(packed, "tile", mirror))
    line = [line[0]] + [swap(line[k], "tile", line_swap(4 * k)) for k in (1, 2, 3)]
    own = predicted_adjoint[0]
    shifted, near, far = pl.pallas_call(
        functools.partial(moved_kernel, breadth),
        out_shape=(held((2, wide, 3 * planes), BF16),) + (held((breadth, planes), BF16),) * 2,
        in_specs=[vmem()],
        out_specs=(vmem(),) * 3,
        compiler_params=params(4),
        cost_estimate=pl.CostEstimate(flops=10**6, bytes_accessed=10**6, transcendentals=0),
        name="moved",
    )(own)
    line, shifted = lax.optimization_barrier((line, shifted))
    messages = pl.pallas_call(
        strip_kernel,
        out_shape=(held((9 * pixels, planes), BF16),) * 4,
        in_specs=[vmem()] * 4,
        out_specs=(vmem(),) * 4,
        scratch_shapes=[pltpu.VMEM((4, 16, planes), F32)],
        compiler_params=params(4),
        name="strip",
    )(*line)
    arrived = [swap(messages[k], "tile", line_swap(k)) for k in (1, 2, 3)]

    def splat_scratch(count):
        total = count * 8 * slots
        return [
            pltpu.VMEM((3, 8, total), F32),
            pltpu.VMEM((3, planes, total), BF16),
            pltpu.VMEM((2, breadth, total), BF16),
        ]

    sums = pl.pallas_call(
        plane_kernel,
        out_shape=held((6, breadth, planes), F32),
        in_specs=[vmem()],
        out_specs=vmem(),
        scratch_shapes=splat_scratch(1),
        compiler_params=params(8),
        cost_estimate=pl.CostEstimate(flops=2 * 6 * breadth * 8 * slots * planes, bytes_accessed=10**6, transcendentals=0),
        name="plane",
    )(messages[0])
    sums = pl.pallas_call(
        more_kernel,
        out_shape=held((6, breadth, planes), F32),
        in_specs=[vmem()] * 2,
        out_specs=vmem(),
        scratch_shapes=splat_scratch(1),
        compiler_params=params(8),
        cost_estimate=pl.CostEstimate(flops=2 * 6 * breadth * 8 * slots * planes, bytes_accessed=10**6, transcendentals=0),
        name="more",
    )(arrived[0], sums)
    bev = pl.pallas_call(
        splat_kernel,
        out_shape=held((6, wide, planes), BF16),
        in_specs=[vmem()] * 3,
        out_specs=vmem(),
        scratch_shapes=splat_scratch(2),
        compiler_params=params(12),
        name="splat",
    )(arrived[1], arrived[2], sums)
    pre, hidden, kept, given = pl.pallas_call(
        functools.partial(hidden_kernel, breadth),
        out_shape=(
            held((2, wide, planes), F32),
            held((4, wide, planes), BF16),
            held((taps, half), F32),
            held((taps, half), BF16),
        ),
        in_specs=[vmem()] * 3,
        out_specs=(vmem(),) * 4,
        compiler_params=params(10),
        name="hidden",
    )(bev, initial_plane_filter, shifted)

    share = taps // strips
    taken = swap(given, "dp", line_swap(1))
    parts = pl.pallas_call(
        parts_kernel,
        out_shape=tuple(held((strips // 4, share, half), F32 if k == 0 else BF16) for k in range(4)),
        in_specs=[vmem()] * 2,
        out_specs=(vmem(),) * 4,
        compiler_params=params(2),
        name="parts",
    )(kept.reshape(strips, share, half), taken.reshape(strips, share, half))
    fetched = [swap(parts[k], "tile", line_swap(k)) for k in (1, 2, 3)]
    scene = pl.pallas_call(
        functools.partial(scene_kernel, breadth),
        out_shape=struct((2, breadth, planes), BF16),
        in_specs=[vmem()] * 3,
        out_specs=vmem(),
        compiler_params=params(8),
        cost_estimate=pl.CostEstimate(flops=2 * 2 * wide * taps * planes, bytes_accessed=10**6, transcendentals=0),
        name="scene",
    )(bev, hidden, predictor_filter)
    fetched, scene = lax.optimization_barrier((fetched, scene))
    pairs = pl.pallas_call(
        planes_kernel,
        out_shape=tuple(held((2, share, half), F32 if k == 0 else BF16) for k in range(4)),
        in_specs=[vmem()] * 4,
        out_specs=(vmem(),) * 4,
        compiler_params=params(2),
        name="planes",
    )(parts[0], *fetched)
    fetched = [swap(pairs[k], "tile", line_swap(4 * k)) for k in (1, 2, 3)]
    pair = added(pairs[0], *fetched)
    ours = pair[0]
    theirs = pair[1].astype(BF16)
    theirs, near, far = lax.optimization_barrier((theirs, near, far))
    ours = added(ours, swap(theirs, "tile", mirror))
    first = swap(near, "tile", line_swap(1))
    second = swap(far, "tile", lambda i: (i - 1 + 2 * (i % 2)) % strips)
    fetched = [swap(ours, "dp", line_swap(2 * k)) for k in (1, 2, 3)]
    derivative = pl.pallas_call(
        functools.partial(derivative_kernel, breadth),
        out_shape=struct((2, breadth, planes), BF16),
        in_specs=[vmem()] * 5,
        out_specs=vmem(),
        scratch_shapes=[pltpu.VMEM((4, wide, planes), BF16)],
        compiler_params=params(8),
        cost_estimate=pl.CostEstimate(flops=2 * 2 * wide * taps * planes, bytes_accessed=10**6, transcendentals=10**6),
        name="derivative",
    )(own, first, second, predictor_filter, pre)
    fetched, derivative = lax.optimization_barrier((fetched, derivative))
    ours = added(ours, *fetched)
    other = swap(ours, "dp", line_swap(1))
    square_tally = lax.axis_size("dp") * height * strips * breadth
    gradient = pl.pallas_call(
        functools.partial(gradient_kernel, 1.0 / math.sqrt(square_tally)),
        out_shape=struct((share, planes), F32),
        in_specs=[vmem()] * 2,
        out_specs=vmem(),
        compiler_params=params(2),
        name="gradient",
    )(ours, other)
    return scene[None], derivative[None], gradient


def solution(mesh):
    placed = (
        P("dp", "tile", None),
        P("dp", "tile", None),
        P("dp", "tile", None, None),
        P("dp", "tile", None, None),
        P("dp", "tile", None),
        P("dp", "tile", None, None),
        P(),
        P(),
    )
    return jax.shard_map(
        on_device,
        mesh=mesh,
        in_specs=placed,
        out_specs=(P("dp", "tile", None, None), P("dp", "tile", None, None), P("tile", None)),
        check_vma=False,
    )
```

```python
import functools
import math

import jax
import jax.numpy as jnp
from jax import lax
from jax.experimental import pallas as pl
from jax.experimental.pallas import tpu as pltpu
from jax.sharding import PartitionSpec as P

epsilon = 1e-05

F32 = jnp.float32
BF16 = jnp.bfloat16
LANES = 128
CODE = 128
FINE = 16


def params(mebibytes):
    return pltpu.CompilerParams(vmem_limit_bytes=mebibytes * 1024 * 1024)


def vmem():
    return pl.BlockSpec(memory_space=pltpu.VMEM)


def far_held(values):
    return pltpu.with_memory_space_constraint(values, pltpu.HBM)


def turned(values, shift):
    return pltpu.roll(values, shift % values.shape[0], 0)


def pack_kernel(features, scores, points, cells, counts, packed, score_buf, point_buf, cell_buf, count_buf, sems):
    copies = [
        pltpu.make_async_copy(source, target, sems.at[i])
        for i, (source, target) in enumerate(
            (
                (points, point_buf),
                (scores, score_buf),
                (cells, cell_buf),
                (counts, count_buf),
                (features, packed.at[: features.shape[0]]),
            )
        )
    ]
    for copy in copies:
        copy.start()
    for copy in copies:
        copy.wait()
    pixels, bins = scores.shape
    strips, slots = points.shape
    logits = score_buf[...].astype(F32)
    grown = jnp.exp(logits - jnp.max(logits, axis=1, keepdims=True))
    prob = grown / jnp.sum(grown, axis=1, keepdims=True)
    blank = jnp.zeros((pixels, LANES - bins), F32)
    prob = jnp.concatenate([prob, blank], axis=1)
    unused = jnp.zeros((strips, LANES - slots), jnp.int32)
    point = jnp.concatenate([point_buf[...], unused], axis=1)
    cell = jnp.concatenate([cell_buf[...], unused], axis=1)
    bin_index = point % bins
    pixel = point // bins
    weight = jnp.zeros((strips, LANES), F32)
    for p in range(pixels):
        row = jnp.broadcast_to(prob[p : p + 1], (strips, LANES))
        weight = jnp.where(pixel == p, jnp.take_along_axis(row, bin_index, axis=1), weight)
    across = lax.broadcasted_iota(jnp.int32, (strips, strips), 1)
    down = lax.broadcasted_iota(jnp.int32, (strips, strips), 0)
    tally = jnp.sum(
        jnp.where(across == down, count_buf[...].astype(F32), 0.0), axis=1, keepdims=True
    )
    lane = lax.broadcasted_iota(jnp.int32, (strips, LANES), 1)
    low = lane < slots
    weight = jnp.where(lane.astype(F32) < tally, weight, 0.0)
    coarse = weight.astype(BF16).astype(F32)
    upper = (pixel * 8 + cell // CODE).astype(F32)
    under = (cell % CODE).astype(F32)
    weights = jnp.where(low, coarse, pltpu.roll(weight - coarse, slots, 1))
    codes = jnp.where(low, upper, pltpu.roll(under, slots, 1))
    packed[pixels:] = jnp.concatenate([weights, codes], axis=1).astype(BF16)


def line_kernel(*refs):
    sources, messages, lists = refs[:2], refs[2:6], refs[6]
    strips = lax.axis_size("tile")
    plane = lax.axis_index("tile") // 4
    pixels, planes = sources[0].shape[0] - strips, sources[0].shape[1]
    for i in range(2):
        lists[i] = sources[i][pixels:].astype(F32)
    lane = lax.broadcasted_iota(jnp.int32, (1, planes), 1)
    for k in range(4):
        rows = []
        for i in range(2):
            messages[k][i * pixels : (i + 1) * pixels] = sources[i][:pixels]
            for j in range(8):
                wanted = 4 * (plane ^ k) + (j - 1)
                there = jnp.logical_and(wanted >= 0, wanted < strips)
                row = lists[i, pl.ds(jnp.clip(wanted, 0, strips - 1), 1), :]
                rows.append(jnp.where(jnp.logical_or(there, lane >= planes // 2), row, 0.0))
        messages[k][2 * pixels :] = jnp.concatenate(rows, axis=0).astype(BF16)


def strip_kernel(*refs):
    sources, messages, lists = refs[:4], refs[4:8], refs[8]
    pixels, planes = messages[0].shape[0] // 9, messages[0].shape[1]
    own = lax.axis_index("tile") % 4
    for i in range(4):
        lists[i] = sources[i][2 * pixels :].astype(F32)
    for k in range(4):
        rows = []
        for i in range(8):
            begin = i % 2 * pixels
            messages[k][i * pixels : (i + 1) * pixels] = sources[i // 2][begin : begin + pixels]
            for j in range(3):
                rows.append(lists[i // 2, pl.ds(i % 2 * 8 + (own ^ k) + j, 1), :])
        rows.append(jnp.zeros((8, planes), F32))
        messages[k][8 * pixels :] = jnp.concatenate(rows, axis=0).astype(BF16)


def lift(messages, meta, lifted):
    pixels = messages[0].shape[0] // 9
    slots = LANES // 2
    batch = 4
    span = batch * slots
    depth = batch * pixels
    low = lax.broadcasted_iota(jnp.int32, (1, LANES), 1) < slots
    home = (lax.broadcasted_iota(jnp.int32, (1, span), 1) // slots * pixels).astype(F32)
    order = lax.broadcasted_iota(jnp.int32, (depth, span), 0).astype(F32)
    for m, message in enumerate(messages):
        lists = message[8 * pixels :].astype(F32)
        halves = []
        for h in range(2):
            straight = lists[:, h * LANES : (h + 1) * LANES]
            halves.append((straight, pltpu.roll(straight, slots, 1)))
        for g in range(2):
            block = message[g * depth : (g + 1) * depth]
            turned_block = block.astype(F32).T.astype(BF16)
            twice = jnp.concatenate([turned_block, turned_block], axis=1)
            at = slice((2 * m + g) * span, (2 * m + g + 1) * span)
            for s in range(3):
                fields = []
                for straight, rolled in halves:
                    first, second = [], []
                    for p in range(2):
                        r0 = 3 * (batch * g + 2 * p) + s
                        r1 = r0 + 3
                        first.append(jnp.where(low, straight[r0 : r0 + 1], rolled[r1 : r1 + 1]))
                        second.append(jnp.where(low, rolled[r0 : r0 + 1], straight[r1 : r1 + 1]))
                    fields.append(jnp.concatenate(first, axis=1))
                    fields.append(jnp.concatenate(second, axis=1))
                coarse, rest, upper, under = fields
                pixel = jnp.floor(upper * 0.125)
                sixteenths = jnp.floor(under * (1.0 / FINE))
                meta[s, 0:1, at] = (upper - 8.0 * pixel) * (CODE // FINE) + sixteenths
                meta[s, 1:2, at] = under - FINE * sixteenths
                match = order == pixel + home
                coarse = jnp.where(match, coarse, 0.0).astype(BF16)
                rest = jnp.where(match, rest, 0.0).astype(BF16)
                lifted[s, :, at] = jnp.dot(
                    twice, jnp.concatenate([coarse, rest], axis=0), preferred_element_type=F32
                ).astype(BF16)


def splat_row(k, meta, lifted, onehot):
    s, r = k // 2, k % 2
    breadth, total = onehot.shape[1:]
    blocks = breadth // FINE
    fine = lax.broadcasted_iota(jnp.int32, (FINE, total), 0).astype(F32)
    comb = jnp.where(fine == meta[s, 1:2, :], 1.0, 0.0).astype(BF16)
    coarse = meta[s, 0:1, :]
    for b in range(blocks):
        chosen = jnp.where(coarse == float(r * blocks + b), 1.0, 0.0).astype(BF16)
        onehot[k % 2, b * FINE : (b + 1) * FINE, :] = comb * chosen
    return lax.dot_general(
        onehot[k % 2], lifted[s], (((1,), (1,)), ((), ())), preferred_element_type=F32
    )


def normalized(summed, bev, k):
    breadth, planes = summed.shape
    wide = bev.shape[1]
    factor = lax.rsqrt(jnp.mean(summed * summed, axis=1, keepdims=True) + epsilon)
    bev[k, :breadth] = (summed * factor).astype(BF16)
    bev[k, breadth:] = jnp.zeros((wide - breadth, planes), BF16)


def plane_kernel(message, sums, meta, lifted, onehot):
    lift([message], meta, lifted)
    for k in range(6):
        sums[k] = splat_row(k, meta, lifted, onehot)


def more_kernel(message, before, sums, meta, lifted, onehot):
    lift([message], meta, lifted)
    for k in range(6):
        sums[k] = before[k] + splat_row(k, meta, lifted, onehot)


def splat_kernel(message, before, bev, meta, lifted, onehot):
    lift([message], meta, lifted)
    for k in range(6):
        normalized(before[k] + splat_row(k, meta, lifted, onehot), bev, k)


def wide_weight(weight, planes):
    return jnp.concatenate(
        [
            jnp.concatenate(
                [weight[(a * 3 + b) * planes : (a * 3 + b + 1) * planes] for b in range(3)], axis=1
            )
            for a in range(3)
        ],
        axis=0,
    )


def conv_row(field, k, weight):
    planes = field.shape[2]
    stacked = jnp.concatenate([field[k - 1], field[k], field[k + 1]], axis=1)
    product = jnp.dot(stacked, weight, preferred_element_type=F32)
    return (
        product[:, planes : 2 * planes]
        + turned(product[:, :planes], 1)
        + turned(product[:, 2 * planes :], -1)
    )


def inside(shape, breadth):
    return lax.broadcasted_iota(jnp.int32, shape, 0) < breadth


def moved_kernel(breadth, own, kept, given, near, far):
    odd = lax.axis_index("tile") % 2 == 1
    near[...] = jnp.where(odd, own[0], own[1])
    far[...] = jnp.where(odd, own[1], own[0])
    right_core = lax.axis_index("dp") % 2 == 1
    wide = kept.shape[1]
    planes = own.shape[2]
    half = planes // 2
    filler = jnp.zeros((wide - breadth, planes), F32)
    for y in range(2):
        row = jnp.concatenate([own[y].astype(F32), filler], axis=0)
        for b in range(3):
            value = turned(row, b - 1).astype(BF16)
            left, right = value[:, :half], value[:, half:]
            at = slice(b * half, (b + 1) * half)
            kept[y, :, at] = jnp.where(right_core, right, left)
            given[y, :, at] = jnp.where(right_core, left, right)


def gradient_terms(columns, cotangent, terms):
    half = terms.shape[1]
    planes = columns.shape[1]
    for a in range(3):
        term = jnp.dot(columns[a], cotangent[0], preferred_element_type=F32)
        term = term + jnp.dot(columns[a + 1], cotangent[1], preferred_element_type=F32)
        for b in range(3):
            at = slice((a * 3 + b) * planes, (a * 3 + b + 1) * planes)
            terms[at] = term[:, b * half : (b + 1) * half].astype(terms.dtype)


def hidden_kernel(breadth, bev, weight, cotangent, pre, hidden, columns, given):
    wide, planes = bev.shape[1:]
    strip = lax.axis_index("tile")
    last = lax.axis_size("tile") - 1
    grid = wide_weight(weight, planes)
    mask = inside((wide, planes), breadth)
    for k in range(4):
        value = conv_row(bev, k + 1, grid)
        if k in (1, 2):
            pre[k - 1] = value
        keep = mask
        if k == 0:
            keep = jnp.logical_and(mask, strip != 0)
        if k == 3:
            keep = jnp.logical_and(mask, strip != last)
        active = jnp.where(keep, value * jax.nn.sigmoid(value), 0.0)
        hidden[k] = active.astype(BF16)
        columns[k] = active.T.astype(BF16)
    gradient_terms(columns, cotangent, given)


def scene_kernel(breadth, bev, hidden, weight, scene):
    grid = wide_weight(weight, bev.shape[2])
    for y in range(2):
        value = conv_row(hidden, y + 1, grid)
        scene[y] = (bev[y + 2, :breadth].astype(F32) + value[:breadth]).astype(BF16)


def derivative_kernel(breadth, own, first, second, weight, pre, derivative, field):
    wide, planes = pre.shape[1:]
    strip = lax.axis_index("tile")
    odd = strip % 2 == 1
    blank = jnp.zeros((wide - breadth, planes), BF16)
    zero = jnp.zeros((breadth, planes), BF16)
    above = jnp.where(odd, first[...], jnp.where(strip == 0, zero, second[...]))
    below = jnp.where(
        odd, jnp.where(strip == lax.axis_size("tile") - 1, zero, second[...]), first[...]
    )
    for k, row in enumerate((above, own[0], own[1], below)):
        field[k, :breadth] = row
        field[k, breadth:] = blank
    flipped = jnp.concatenate(
        [
            jnp.concatenate(
                [weight[(a * 3 + b) * planes : (a * 3 + b + 1) * planes] for a in (2, 1, 0)], axis=1
            )
            for b in (2, 1, 0)
        ],
        axis=0,
    )
    for y in range(2):
        stacked = jnp.concatenate([field[y], field[y + 1], field[y + 2]], axis=1)
        product = lax.dot_general(
            stacked, flipped, (((1,), (1,)), ((), ())), preferred_element_type=F32
        )
        back = (
            product[:, planes : 2 * planes]
            + turned(product[:, :planes], 1)
            + turned(product[:, 2 * planes :], -1)
        )
        value = pre[y, :breadth]
        sigma = jax.nn.sigmoid(value)
        slope = sigma * (1.0 + value * (1.0 - sigma))
        derivative[y] = (back[:breadth] * slope).astype(BF16)


def parts_kernel(kept, taken, *parts):
    own = lax.axis_index("tile") % 4
    for p in range(kept.shape[0] // 4):
        for k in range(4):
            t = 4 * p + (own ^ k)
            parts[k][p] = (kept[t] + taken[t].astype(F32)).astype(parts[k].dtype)


def planes_kernel(first, one, two, three, *parts):
    plane = lax.axis_index("tile") // 4
    for k in range(4):
        for i, p in enumerate((plane ^ k, 7 - (plane ^ k))):
            total = first[p] + one[p].astype(F32) + two[p].astype(F32) + three[p].astype(F32)
            parts[k][i] = total.astype(parts[k].dtype)


def gradient_kernel(scale, ours, other, gradient):
    odd = lax.axis_index("dp") % 2 == 1
    half = ours.shape[1]
    mine, theirs = ours[...] * scale, other[...] * scale
    gradient[:, :half] = jnp.where(odd, theirs, mine)
    gradient[:, half:] = jnp.where(odd, mine, theirs)


def swap(values, axis, partner):
    return lax.ppermute(values, axis, [(i, partner(i)) for i in range(lax.axis_size(axis))])


def line_swap(k):
    return lambda i: i ^ k


def mirror(i):
    return 28 - i // 4 * 4 + i % 4


def added(first, *others):
    for other in others:
        first = first + other.astype(F32)
    return first


def on_device(
    image_descriptors,
    image_distance_scores,
    entry_sender_location,
    entry_receiver_square,
    entry_valid_tally,
    predicted_adjoint,
    initial_plane_filter,
    predictor_filter,
):
    _, height, breadth, planes = predicted_adjoint.shape
    pixels = image_descriptors.shape[1]
    strips, slots = entry_sender_location.shape[2:]
    wide = breadth // 16 * 16 + 16
    taps = predictor_filter.shape[0]
    half = planes // 2
    struct = jax.ShapeDtypeStruct
    held = pltpu.VMEM

    places = pixels + strips
    packed = pl.pallas_call(
        pack_kernel,
        out_shape=held((places, planes), BF16),
        in_specs=[pl.BlockSpec(memory_space=pl.ANY)] * 5,
        out_specs=vmem(),
        scratch_shapes=[
            pltpu.VMEM((pixels, image_distance_scores.shape[2]), BF16),
            pltpu.VMEM((strips, slots), jnp.int32),
            pltpu.VMEM((strips, slots), jnp.int32),
            pltpu.VMEM((1, strips), jnp.int32),
            pltpu.SemaphoreType.DMA((5,)),
        ],
        compiler_params=params(8),
        name="pack",
    )(
        far_held(image_descriptors[0]),
        far_held(image_distance_scores[0]),
        far_held(entry_sender_location[0, 0]),
        far_held(entry_receiver_square[0, 0]),
        far_held(entry_valid_tally[0]),
    )
    line = pl.pallas_call(
        line_kernel,
        out_shape=(held((2 * pixels + 16, planes), BF16),) * 4,
        in_specs=[vmem()] * 2,
        out_specs=(vmem(),) * 4,
        scratch_shapes=[pltpu.VMEM((2, strips, planes), F32)],
        compiler_params=params(4),
        name="line",
    )(packed, swap(packed, "tile", mirror))
    line = [line[0]] + [swap(line[k], "tile", line_swap(4 * k)) for k in (1, 2, 3)]
    own = predicted_adjoint[0]
    keep, give, near, far = pl.pallas_call(
        functools.partial(moved_kernel, breadth),
        out_shape=(held((2, wide, 3 * half), BF16),) * 2 + (held((breadth, planes), BF16),) * 2,
        in_specs=[vmem()],
        out_specs=(vmem(),) * 4,
        compiler_params=params(4),
        cost_estimate=pl.CostEstimate(flops=10**6, bytes_accessed=10**6, transcendentals=0),
        name="moved",
    )(own)
    line, keep, give = lax.optimization_barrier((line, keep, give))
    messages = pl.pallas_call(
        strip_kernel,
        out_shape=(held((9 * pixels, planes), BF16),) * 4,
        in_specs=[vmem()] * 4,
        out_specs=(vmem(),) * 4,
        scratch_shapes=[pltpu.VMEM((4, 16, planes), F32)],
        compiler_params=params(4),
        name="strip",
    )(*line)
    arrived = [swap(messages[k], "tile", line_swap(k)) for k in (1, 2, 3)]

    def splat_scratch(count):
        total = count * 8 * slots
        return [
            pltpu.VMEM((3, 8, total), F32),
            pltpu.VMEM((3, planes, total), BF16),
            pltpu.VMEM((2, breadth, total), BF16),
        ]

    sums = pl.pallas_call(
        plane_kernel,
        out_shape=held((6, breadth, planes), F32),
        in_specs=[vmem()],
        out_specs=vmem(),
        scratch_shapes=splat_scratch(1),
        compiler_params=params(8),
        cost_estimate=pl.CostEstimate(flops=2 * 6 * breadth * 8 * slots * planes, bytes_accessed=10**6, transcendentals=0),
        name="plane",
    )(messages[0])
    sums = pl.pallas_call(
        more_kernel,
        out_shape=held((6, breadth, planes), F32),
        in_specs=[vmem()] * 2,
        out_specs=vmem(),
        scratch_shapes=splat_scratch(1),
        compiler_params=params(8),
        cost_estimate=pl.CostEstimate(flops=2 * 6 * breadth * 8 * slots * planes, bytes_accessed=10**6, transcendentals=0),
        name="more",
    )(arrived[0], sums)
    sums = pl.pallas_call(
        more_kernel,
        out_shape=held((6, breadth, planes), F32),
        in_specs=[vmem()] * 2,
        out_specs=vmem(),
        scratch_shapes=splat_scratch(1),
        compiler_params=params(8),
        cost_estimate=pl.CostEstimate(flops=2 * 6 * breadth * 8 * slots * planes, bytes_accessed=10**6, transcendentals=0),
        name="again",
    )(arrived[1], sums)
    bev = pl.pallas_call(
        splat_kernel,
        out_shape=held((6, wide, planes), BF16),
        in_specs=[vmem()] * 2,
        out_specs=vmem(),
        scratch_shapes=splat_scratch(1),
        compiler_params=params(8),
        name="splat",
    )(arrived[2], sums)
    pre, hidden, columns, given = pl.pallas_call(
        functools.partial(hidden_kernel, breadth),
        out_shape=(
            held((2, wide, planes), F32),
            held((4, wide, planes), BF16),
            held((4, planes, wide), BF16),
            held((taps, half), BF16),
        ),
        in_specs=[vmem()] * 3,
        out_specs=(vmem(),) * 4,
        compiler_params=params(10),
        name="hidden",
    )(bev, initial_plane_filter, give)
    taken = swap(given, "dp", line_swap(1))
    kept = pl.pallas_call(
        gradient_terms,
        out_shape=held((taps, half), F32),
        in_specs=[vmem()] * 2,
        out_specs=vmem(),
        compiler_params=params(8),
        cost_estimate=pl.CostEstimate(flops=4 * wide * taps * half, bytes_accessed=10**6, transcendentals=0),
        name="kept",
    )(columns, keep)
    kept, taken = lax.optimization_barrier((kept, taken))

    share = taps // strips
    parts = pl.pallas_call(
        parts_kernel,
        out_shape=tuple(held((strips // 4, share, half), F32 if k == 0 else BF16) for k in range(4)),
        in_specs=[vmem()] * 2,
        out_specs=(vmem(),) * 4,
        compiler_params=params(2),
        name="parts",
    )(kept.reshape(strips, share, half), taken.reshape(strips, share, half))
    fetched = [swap(parts[k], "tile", line_swap(k)) for k in (1, 2, 3)]
    scene = pl.pallas_call(
        functools.partial(scene_kernel, breadth),
        out_shape=struct((2, breadth, planes), BF16),
        in_specs=[vmem()] * 3,
        out_specs=vmem(),
        compiler_params=params(8),
        cost_estimate=pl.CostEstimate(flops=2 * 2 * wide * taps * planes, bytes_accessed=10**6, transcendentals=0),
        name="scene",
    )(bev, hidden, predictor_filter)
    fetched, scene = lax.optimization_barrier((fetched, scene))
    pairs = pl.pallas_call(
        planes_kernel,
        out_shape=tuple(held((2, share, half), F32 if k == 0 else BF16) for k in range(4)),
        in_specs=[vmem()] * 4,
        out_specs=(vmem(),) * 4,
        compiler_params=params(2),
        name="planes",
    )(parts[0], *fetched)
    fetched = [swap(pairs[k], "tile", line_swap(4 * k)) for k in (1, 2, 3)]
    pair = added(pairs[0], *fetched)
    ours = pair[0]
    theirs, near, far = lax.optimization_barrier((pair[1].astype(BF16), near, far))
    first = swap(near, "tile", line_swap(1))
    second = swap(far, "tile", lambda i: (i - 1 + 2 * (i % 2)) % strips)
    ours = added(ours, swap(theirs, "tile", mirror))
    fetched = [swap(ours.astype(BF16), "dp", line_swap(2 * k)) for k in (1, 2, 3)]
    fetched, first, second = lax.optimization_barrier((fetched, first, second))
    derivative = pl.pallas_call(
        functools.partial(derivative_kernel, breadth),
        out_shape=struct((2, breadth, planes), BF16),
        in_specs=[vmem()] * 5,
        out_specs=vmem(),
        scratch_shapes=[pltpu.VMEM((4, wide, planes), BF16)],
        compiler_params=params(8),
        cost_estimate=pl.CostEstimate(flops=2 * 2 * wide * taps * planes, bytes_accessed=10**6, transcendentals=10**6),
        name="derivative",
    )(own, first, second, predictor_filter, pre)
    ours = added(ours, *fetched)
    other, derivative = lax.optimization_barrier((swap(ours, "dp", line_swap(1)), derivative))
    square_tally = lax.axis_size("dp") * height * strips * breadth
    gradient = pl.pallas_call(
        functools.partial(gradient_kernel, 1.0 / math.sqrt(square_tally)),
        out_shape=struct((share, planes), F32),
        in_specs=[vmem()] * 2,
        out_specs=vmem(),
        compiler_params=params(2),
        name="gradient",
    )(ours, other)
    return scene[None], derivative[None], gradient


def solution(mesh):
    placed = (
        P("dp", "tile", None),
        P("dp", "tile", None),
        P("dp", "tile", None, None),
        P("dp", "tile", None, None),
        P("dp", "tile", None),
        P("dp", "tile", None, None),
        P(),
        P(),
    )
    return jax.shard_map(
        on_device,
        mesh=mesh,
        in_specs=placed,
        out_specs=(P("dp", "tile", None, None), P("dp", "tile", None, None), P("tile", None)),
        check_vma=False,
    )
```

```python
import functools
import math

import jax
import jax.numpy as jnp
from jax import lax
from jax.experimental import pallas as pl
from jax.experimental.pallas import tpu as pltpu
from jax.sharding import PartitionSpec as P

epsilon = 1e-05

F32 = jnp.float32
BF16 = jnp.bfloat16
LANES = 128
CODE = 128
FINE = 16


def params(mebibytes):
    return pltpu.CompilerParams(vmem_limit_bytes=mebibytes * 1024 * 1024)


def vmem():
    return pl.BlockSpec(memory_space=pltpu.VMEM)


def far_held(values):
    return pltpu.with_memory_space_constraint(values, pltpu.HBM)


def turned(values, shift):
    return pltpu.roll(values, shift % values.shape[0], 0)


def pack_kernel(features, scores, points, cells, counts, packed, score_buf, point_buf, cell_buf, count_buf, sems):
    copies = [
        pltpu.make_async_copy(source, target, sems.at[i])
        for i, (source, target) in enumerate(
            (
                (points, point_buf),
                (scores, score_buf),
                (cells, cell_buf),
                (counts, count_buf),
                (features, packed.at[: features.shape[0]]),
            )
        )
    ]
    for copy in copies:
        copy.start()
    for copy in copies:
        copy.wait()
    pixels, bins = scores.shape
    strips, slots = points.shape
    logits = score_buf[...].astype(F32)
    grown = jnp.exp(logits - jnp.max(logits, axis=1, keepdims=True))
    prob = grown / jnp.sum(grown, axis=1, keepdims=True)
    blank = jnp.zeros((pixels, LANES - bins), F32)
    prob = jnp.concatenate([prob, blank], axis=1)
    unused = jnp.zeros((strips, LANES - slots), jnp.int32)
    point = jnp.concatenate([point_buf[...], unused], axis=1)
    cell = jnp.concatenate([cell_buf[...], unused], axis=1)
    bin_index = point % bins
    pixel = point // bins
    weight = jnp.zeros((strips, LANES), F32)
    for p in range(pixels):
        row = jnp.broadcast_to(prob[p : p + 1], (strips, LANES))
        weight = jnp.where(pixel == p, jnp.take_along_axis(row, bin_index, axis=1), weight)
    across = lax.broadcasted_iota(jnp.int32, (strips, strips), 1)
    down = lax.broadcasted_iota(jnp.int32, (strips, strips), 0)
    tally = jnp.sum(
        jnp.where(across == down, count_buf[...].astype(F32), 0.0), axis=1, keepdims=True
    )
    lane = lax.broadcasted_iota(jnp.int32, (strips, LANES), 1)
    low = lane < slots
    weight = jnp.where(lane.astype(F32) < tally, weight, 0.0)
    coarse = weight.astype(BF16).astype(F32)
    upper = (pixel * 8 + cell // CODE).astype(F32)
    under = (cell % CODE).astype(F32)
    weights = jnp.where(low, coarse, pltpu.roll(weight - coarse, slots, 1))
    codes = jnp.where(low, upper, pltpu.roll(under, slots, 1))
    packed[pixels:] = jnp.concatenate([weights, codes], axis=1).astype(BF16)


def line_kernel(*refs):
    sources, messages, lists = refs[:2], refs[2:6], refs[6]
    strips = lax.axis_size("tile")
    plane = lax.axis_index("tile") // 4
    pixels, planes = sources[0].shape[0] - strips, sources[0].shape[1]
    for i in range(2):
        lists[i] = sources[i][pixels:].astype(F32)
    lane = lax.broadcasted_iota(jnp.int32, (1, planes), 1)
    for k in range(4):
        rows = []
        for i in range(2):
            messages[k][i * pixels : (i + 1) * pixels] = sources[i][:pixels]
            for j in range(8):
                wanted = 4 * (plane ^ k) + (j - 1)
                there = jnp.logical_and(wanted >= 0, wanted < strips)
                row = lists[i, pl.ds(jnp.clip(wanted, 0, strips - 1), 1), :]
                rows.append(jnp.where(jnp.logical_or(there, lane >= planes // 2), row, 0.0))
        messages[k][2 * pixels :] = jnp.concatenate(rows, axis=0).astype(BF16)


def strip_kernel(*refs):
    sources, messages, lists = refs[:4], refs[4:8], refs[8]
    pixels, planes = messages[0].shape[0] // 9, messages[0].shape[1]
    own = lax.axis_index("tile") % 4
    for i in range(4):
        lists[i] = sources[i][2 * pixels :].astype(F32)
    for k in range(4):
        rows = []
        for i in range(8):
            begin = i % 2 * pixels
            messages[k][i * pixels : (i + 1) * pixels] = sources[i // 2][begin : begin + pixels]
            for j in range(3):
                rows.append(lists[i // 2, pl.ds(i % 2 * 8 + (own ^ k) + j, 1), :])
        rows.append(jnp.zeros((8, planes), F32))
        messages[k][8 * pixels :] = jnp.concatenate(rows, axis=0).astype(BF16)


def lift(messages, meta, lifted):
    pixels = messages[0].shape[0] // 9
    slots = LANES // 2
    batch = 4
    span = batch * slots
    depth = batch * pixels
    low = lax.broadcasted_iota(jnp.int32, (1, LANES), 1) < slots
    home = (lax.broadcasted_iota(jnp.int32, (1, span), 1) // slots * pixels).astype(F32)
    order = lax.broadcasted_iota(jnp.int32, (depth, span), 0).astype(F32)
    for m, message in enumerate(messages):
        lists = message[8 * pixels :].astype(F32)
        halves = []
        for h in range(2):
            straight = lists[:, h * LANES : (h + 1) * LANES]
            halves.append((straight, pltpu.roll(straight, slots, 1)))
        for g in range(2):
            block = message[g * depth : (g + 1) * depth]
            turned_block = block.astype(F32).T.astype(BF16)
            twice = jnp.concatenate([turned_block, turned_block], axis=1)
            at = slice((2 * m + g) * span, (2 * m + g + 1) * span)
            for s in range(3):
                fields = []
                for straight, rolled in halves:
                    first, second = [], []
                    for p in range(2):
                        r0 = 3 * (batch * g + 2 * p) + s
                        r1 = r0 + 3
                        first.append(jnp.where(low, straight[r0 : r0 + 1], rolled[r1 : r1 + 1]))
                        second.append(jnp.where(low, rolled[r0 : r0 + 1], straight[r1 : r1 + 1]))
                    fields.append(jnp.concatenate(first, axis=1))
                    fields.append(jnp.concatenate(second, axis=1))
                coarse, rest, upper, under = fields
                pixel = jnp.floor(upper * 0.125)
                sixteenths = jnp.floor(under * (1.0 / FINE))
                meta[s, 0:1, at] = (upper - 8.0 * pixel) * (CODE // FINE) + sixteenths
                meta[s, 1:2, at] = under - FINE * sixteenths
                match = order == pixel + home
                coarse = jnp.where(match, coarse, 0.0).astype(BF16)
                rest = jnp.where(match, rest, 0.0).astype(BF16)
                lifted[s, :, at] = jnp.dot(
                    twice, jnp.concatenate([coarse, rest], axis=0), preferred_element_type=F32
                ).astype(BF16)


def splat_row(k, meta, lifted, onehot):
    s, r = k // 2, k % 2
    breadth, total = onehot.shape[1:]
    blocks = breadth // FINE
    fine = lax.broadcasted_iota(jnp.int32, (FINE, total), 0).astype(F32)
    comb = jnp.where(fine == meta[s, 1:2, :], 1.0, 0.0).astype(BF16)
    coarse = meta[s, 0:1, :]
    for b in range(blocks):
        chosen = jnp.where(coarse == float(r * blocks + b), 1.0, 0.0).astype(BF16)
        onehot[k % 2, b * FINE : (b + 1) * FINE, :] = comb * chosen
    return lax.dot_general(
        onehot[k % 2], lifted[s], (((1,), (1,)), ((), ())), preferred_element_type=F32
    )


def normalized(summed, bev, k):
    breadth, planes = summed.shape
    wide = bev.shape[1]
    factor = lax.rsqrt(jnp.mean(summed * summed, axis=1, keepdims=True) + epsilon)
    bev[k, :breadth] = (summed * factor).astype(BF16)
    bev[k, breadth:] = jnp.zeros((wide - breadth, planes), BF16)


def plane_kernel(message, sums, meta, lifted, onehot):
    lift([message], meta, lifted)
    for k in range(6):
        sums[k] = splat_row(k, meta, lifted, onehot)


def more_kernel(message, before, sums, meta, lifted, onehot):
    lift([message], meta, lifted)
    for k in range(6):
        sums[k] = before[k] + splat_row(k, meta, lifted, onehot)


def splat_kernel(message, before, bev, meta, lifted, onehot):
    lift([message], meta, lifted)
    for k in range(6):
        normalized(before[k] + splat_row(k, meta, lifted, onehot), bev, k)


def wide_weight(weight, planes):
    return jnp.concatenate(
        [
            jnp.concatenate(
                [weight[(a * 3 + b) * planes : (a * 3 + b + 1) * planes] for b in range(3)], axis=1
            )
            for a in range(3)
        ],
        axis=0,
    )


def conv_row(field, k, weight):
    planes = field.shape[2]
    stacked = jnp.concatenate([field[k - 1], field[k], field[k + 1]], axis=1)
    product = jnp.dot(stacked, weight, preferred_element_type=F32)
    return (
        product[:, planes : 2 * planes]
        + turned(product[:, :planes], 1)
        + turned(product[:, 2 * planes :], -1)
    )


def inside(shape, breadth):
    return lax.broadcasted_iota(jnp.int32, shape, 0) < breadth


def moved_kernel(breadth, own, kept, given, near, far):
    odd = lax.axis_index("tile") % 2 == 1
    near[...] = jnp.where(odd, own[0], own[1])
    far[...] = jnp.where(odd, own[1], own[0])
    right_core = lax.axis_index("dp") % 2 == 1
    wide = kept.shape[1]
    planes = own.shape[2]
    half = planes // 2
    filler = jnp.zeros((wide - breadth, planes), F32)
    for y in range(2):
        row = jnp.concatenate([own[y].astype(F32), filler], axis=0)
        for b in range(3):
            value = turned(row, b - 1).astype(BF16)
            left, right = value[:, :half], value[:, half:]
            at = slice(b * half, (b + 1) * half)
            kept[y, :, at] = jnp.where(right_core, right, left)
            given[y, :, at] = jnp.where(right_core, left, right)


def gradient_terms(columns, cotangent, terms):
    half = terms.shape[1]
    planes = columns.shape[1]
    for a in range(3):
        term = jnp.dot(columns[a], cotangent[0], preferred_element_type=F32)
        term = term + jnp.dot(columns[a + 1], cotangent[1], preferred_element_type=F32)
        for b in range(3):
            at = slice((a * 3 + b) * planes, (a * 3 + b + 1) * planes)
            terms[at] = term[:, b * half : (b + 1) * half].astype(terms.dtype)


def hidden_kernel(breadth, bev, weight, cotangent, pre, hidden, columns, given):
    wide, planes = bev.shape[1:]
    strip = lax.axis_index("tile")
    last = lax.axis_size("tile") - 1
    grid = wide_weight(weight, planes)
    mask = inside((wide, planes), breadth)
    for k in range(4):
        value = conv_row(bev, k + 1, grid)
        if k in (1, 2):
            pre[k - 1] = value
        keep = mask
        if k == 0:
            keep = jnp.logical_and(mask, strip != 0)
        if k == 3:
            keep = jnp.logical_and(mask, strip != last)
        active = jnp.where(keep, value * jax.nn.sigmoid(value), 0.0)
        hidden[k] = active.astype(BF16)
        columns[k] = active.T.astype(BF16)
    gradient_terms(columns, cotangent, given)


def scene_kernel(breadth, bev, hidden, weight, scene):
    grid = wide_weight(weight, bev.shape[2])
    for y in range(2):
        value = conv_row(hidden, y + 1, grid)
        scene[y] = (bev[y + 2, :breadth].astype(F32) + value[:breadth]).astype(BF16)


def flipped_taps(weight, planes, rows):
    return jnp.concatenate(
        [
            jnp.concatenate(
                [weight[(a * 3 + b) * planes : (a * 3 + b + 1) * planes] for a in rows], axis=1
            )
            for b in (2, 1, 0)
        ],
        axis=0,
    )


def back_products(stacked, flipped):
    return lax.dot_general(
        stacked, flipped, (((1,), (1,)), ((), ())), preferred_element_type=F32
    )


def joined(product, planes):
    return (
        product[:, planes : 2 * planes]
        + turned(product[:, :planes], 1)
        + turned(product[:, 2 * planes :], -1)
    )


def inner_kernel(breadth, own, weight, back, field):
    wide, planes = back.shape[1:]
    for k in range(2):
        field[k, :breadth] = own[k]
        field[k, breadth:] = jnp.zeros((wide - breadth, planes), BF16)
    stacked = jnp.concatenate([field[0], field[1]], axis=1)
    back[0] = joined(back_products(stacked, flipped_taps(weight, planes, (1, 0))), planes)
    back[1] = joined(back_products(stacked, flipped_taps(weight, planes, (2, 1))), planes)


def derivative_kernel(breadth, first, second, back, weight, pre, derivative, field):
    wide, planes = pre.shape[1:]
    strip = lax.axis_index("tile")
    odd = strip % 2 == 1
    zero = jnp.zeros((breadth, planes), BF16)
    above = jnp.where(odd, first[...], jnp.where(strip == 0, zero, second[...]))
    below = jnp.where(
        odd, jnp.where(strip == lax.axis_size("tile") - 1, zero, second[...]), first[...]
    )
    for y, (row, a) in enumerate(((above, 2), (below, 0))):
        field[y, :breadth] = row
        field[y, breadth:] = jnp.zeros((wide - breadth, planes), BF16)
        rest = joined(back_products(field[y], flipped_taps(weight, planes, (a,))), planes)
        value = pre[y, :breadth]
        sigma = jax.nn.sigmoid(value)
        slope = sigma * (1.0 + value * (1.0 - sigma))
        derivative[y] = ((back[y, :breadth] + rest[:breadth]) * slope).astype(BF16)


def parts_kernel(kept, taken, *parts):
    own = lax.axis_index("tile") % 4
    for p in range(kept.shape[0] // 4):
        for k in range(4):
            t = 4 * p + (own ^ k)
            parts[k][p] = (kept[t] + taken[t].astype(F32)).astype(parts[k].dtype)


def planes_kernel(first, one, two, three, *parts):
    plane = lax.axis_index("tile") // 4
    for k in range(4):
        for i, p in enumerate((plane ^ k, 7 - (plane ^ k))):
            total = first[p] + one[p].astype(F32) + two[p].astype(F32) + three[p].astype(F32)
            parts[k][i] = total.astype(parts[k].dtype)


def gradient_kernel(scale, ours, other, gradient):
    odd = lax.axis_index("dp") % 2 == 1
    half = ours.shape[1]
    mine, theirs = ours[...] * scale, other[...] * scale
    gradient[:, :half] = jnp.where(odd, theirs, mine)
    gradient[:, half:] = jnp.where(odd, mine, theirs)


def swap(values, axis, partner):
    return lax.ppermute(values, axis, [(i, partner(i)) for i in range(lax.axis_size(axis))])


def line_swap(k):
    return lambda i: i ^ k


def mirror(i):
    return 28 - i // 4 * 4 + i % 4


def added(first, *others):
    for other in others:
        first = first + other.astype(F32)
    return first


def on_device(
    image_descriptors,
    image_distance_scores,
    entry_sender_location,
    entry_receiver_square,
    entry_valid_tally,
    predicted_adjoint,
    initial_plane_filter,
    predictor_filter,
):
    _, height, breadth, planes = predicted_adjoint.shape
    pixels = image_descriptors.shape[1]
    strips, slots = entry_sender_location.shape[2:]
    wide = breadth // 16 * 16 + 16
    taps = predictor_filter.shape[0]
    half = planes // 2
    struct = jax.ShapeDtypeStruct
    held = pltpu.VMEM

    places = pixels + strips
    packed = pl.pallas_call(
        pack_kernel,
        out_shape=held((places, planes), BF16),
        in_specs=[pl.BlockSpec(memory_space=pl.ANY)] * 5,
        out_specs=vmem(),
        scratch_shapes=[
            pltpu.VMEM((pixels, image_distance_scores.shape[2]), BF16),
            pltpu.VMEM((strips, slots), jnp.int32),
            pltpu.VMEM((strips, slots), jnp.int32),
            pltpu.VMEM((1, strips), jnp.int32),
            pltpu.SemaphoreType.DMA((5,)),
        ],
        compiler_params=params(8),
        name="pack",
    )(
        far_held(image_descriptors[0]),
        far_held(image_distance_scores[0]),
        far_held(entry_sender_location[0, 0]),
        far_held(entry_receiver_square[0, 0]),
        far_held(entry_valid_tally[0]),
    )
    line = pl.pallas_call(
        line_kernel,
        out_shape=(held((2 * pixels + 16, planes), BF16),) * 4,
        in_specs=[vmem()] * 2,
        out_specs=(vmem(),) * 4,
        scratch_shapes=[pltpu.VMEM((2, strips, planes), F32)],
        compiler_params=params(4),
        name="line",
    )(packed, swap(packed, "tile", mirror))
    line = [line[0]] + [swap(line[k], "tile", line_swap(4 * k)) for k in (3, 2, 1)]
    own = predicted_adjoint[0]
    keep, give, near, far = pl.pallas_call(
        functools.partial(moved_kernel, breadth),
        out_shape=(held((2, wide, 3 * half), BF16),) * 2 + (held((breadth, planes), BF16),) * 2,
        in_specs=[vmem()],
        out_specs=(vmem(),) * 4,
        compiler_params=params(4),
        cost_estimate=pl.CostEstimate(flops=10**6, bytes_accessed=10**6, transcendentals=0),
        name="moved",
    )(own)
    line, keep, give = lax.optimization_barrier((line, keep, give))
    messages = pl.pallas_call(
        strip_kernel,
        out_shape=(held((9 * pixels, planes), BF16),) * 4,
        in_specs=[vmem()] * 4,
        out_specs=(vmem(),) * 4,
        scratch_shapes=[pltpu.VMEM((4, 16, planes), F32)],
        compiler_params=params(4),
        name="strip",
    )(*line)
    arrived = [swap(messages[k], "tile", line_swap(k)) for k in (3, 2, 1)]

    def splat_scratch(count):
        total = count * 8 * slots
        return [
            pltpu.VMEM((3, 8, total), F32),
            pltpu.VMEM((3, planes, total), BF16),
            pltpu.VMEM((2, breadth, total), BF16),
        ]

    sums = pl.pallas_call(
        plane_kernel,
        out_shape=held((6, breadth, planes), F32),
        in_specs=[vmem()],
        out_specs=vmem(),
        scratch_shapes=splat_scratch(1),
        compiler_params=params(8),
        cost_estimate=pl.CostEstimate(flops=2 * 6 * breadth * 8 * slots * planes, bytes_accessed=10**6, transcendentals=0),
        name="plane",
    )(messages[0])
    sums = pl.pallas_call(
        more_kernel,
        out_shape=held((6, breadth, planes), F32),
        in_specs=[vmem()] * 2,
        out_specs=vmem(),
        scratch_shapes=splat_scratch(1),
        compiler_params=params(8),
        cost_estimate=pl.CostEstimate(flops=2 * 6 * breadth * 8 * slots * planes, bytes_accessed=10**6, transcendentals=0),
        name="more",
    )(arrived[0], sums)
    sums = pl.pallas_call(
        more_kernel,
        out_shape=held((6, breadth, planes), F32),
        in_specs=[vmem()] * 2,
        out_specs=vmem(),
        scratch_shapes=splat_scratch(1),
        compiler_params=params(8),
        cost_estimate=pl.CostEstimate(flops=2 * 6 * breadth * 8 * slots * planes, bytes_accessed=10**6, transcendentals=0),
        name="again",
    )(arrived[1], sums)
    bev = pl.pallas_call(
        splat_kernel,
        out_shape=held((6, wide, planes), BF16),
        in_specs=[vmem()] * 2,
        out_specs=vmem(),
        scratch_shapes=splat_scratch(1),
        compiler_params=params(8),
        name="splat",
    )(arrived[2], sums)
    pre, hidden, columns, given = pl.pallas_call(
        functools.partial(hidden_kernel, breadth),
        out_shape=(
            held((2, wide, planes), F32),
            held((4, wide, planes), BF16),
            held((4, planes, wide), BF16),
            held((taps, half), BF16),
        ),
        in_specs=[vmem()] * 3,
        out_specs=(vmem(),) * 4,
        compiler_params=params(10),
        name="hidden",
    )(bev, initial_plane_filter, give)
    taken = swap(given, "dp", line_swap(1))
    kept = pl.pallas_call(
        gradient_terms,
        out_shape=held((taps, half), F32),
        in_specs=[vmem()] * 2,
        out_specs=vmem(),
        compiler_params=params(8),
        cost_estimate=pl.CostEstimate(flops=4 * wide * taps * half, bytes_accessed=10**6, transcendentals=0),
        name="kept",
    )(columns, keep)
    kept, taken = lax.optimization_barrier((kept, taken))

    share = taps // strips
    parts = pl.pallas_call(
        parts_kernel,
        out_shape=tuple(held((strips // 4, share, half), F32 if k == 0 else BF16) for k in range(4)),
        in_specs=[vmem()] * 2,
        out_specs=(vmem(),) * 4,
        compiler_params=params(2),
        name="parts",
    )(kept.reshape(strips, share, half), taken.reshape(strips, share, half))
    fetched = [swap(parts[k], "tile", line_swap(k)) for k in (3, 2, 1)]
    scene = pl.pallas_call(
        functools.partial(scene_kernel, breadth),
        out_shape=struct((2, breadth, planes), BF16),
        in_specs=[vmem()] * 3,
        out_specs=vmem(),
        compiler_params=params(8),
        cost_estimate=pl.CostEstimate(flops=2 * 2 * wide * taps * planes, bytes_accessed=10**6, transcendentals=0),
        name="scene",
    )(bev, hidden, predictor_filter)
    back = pl.pallas_call(
        functools.partial(inner_kernel, breadth),
        out_shape=held((2, wide, planes), F32),
        in_specs=[vmem()] * 2,
        out_specs=vmem(),
        scratch_shapes=[pltpu.VMEM((2, wide, planes), BF16)],
        compiler_params=params(8),
        cost_estimate=pl.CostEstimate(flops=4 * wide * taps * planes // 3 * 2, bytes_accessed=10**6, transcendentals=0),
        name="inner",
    )(own, predictor_filter)
    fetched, scene, back = lax.optimization_barrier((fetched, scene, back))
    pairs = pl.pallas_call(
        planes_kernel,
        out_shape=tuple(held((2, share, half), F32 if k == 0 else BF16) for k in range(4)),
        in_specs=[vmem()] * 4,
        out_specs=(vmem(),) * 4,
        compiler_params=params(2),
        name="planes",
    )(parts[0], *fetched)
    fetched = [swap(pairs[k], "tile", line_swap(4 * k)) for k in (3, 2, 1)]
    pair = added(pairs[0], *fetched)
    ours = pair[0]
    theirs, near, far = lax.optimization_barrier((pair[1].astype(BF16), near, far))
    first = swap(near, "tile", line_swap(1))
    second = swap(far, "tile", lambda i: (i - 1 + 2 * (i % 2)) % strips)
    ours = added(ours, swap(theirs, "tile", mirror))
    fetched = [swap(ours.astype(BF16), "dp", line_swap(2 * k)) for k in (3, 2, 1)]
    fetched, first, second = lax.optimization_barrier((fetched, first, second))
    derivative = pl.pallas_call(
        functools.partial(derivative_kernel, breadth),
        out_shape=struct((2, breadth, planes), BF16),
        in_specs=[vmem()] * 5,
        out_specs=vmem(),
        scratch_shapes=[pltpu.VMEM((2, wide, planes), BF16)],
        compiler_params=params(8),
        cost_estimate=pl.CostEstimate(flops=4 * wide * taps * planes // 3, bytes_accessed=10**6, transcendentals=10**6),
        name="derivative",
    )(first, second, back, predictor_filter, pre)
    ours = added(ours, *fetched)
    other, derivative = lax.optimization_barrier((swap(ours, "dp", line_swap(1)), derivative))
    square_tally = lax.axis_size("dp") * height * strips * breadth
    gradient = pl.pallas_call(
        functools.partial(gradient_kernel, 1.0 / math.sqrt(square_tally)),
        out_shape=struct((share, planes), F32),
        in_specs=[vmem()] * 2,
        out_specs=vmem(),
        compiler_params=params(2),
        name="gradient",
    )(ours, other)
    return scene[None], derivative[None], gradient


def solution(mesh):
    placed = (
        P("dp", "tile", None),
        P("dp", "tile", None),
        P("dp", "tile", None, None),
        P("dp", "tile", None, None),
        P("dp", "tile", None),
        P("dp", "tile", None, None),
        P(),
        P(),
    )
    return jax.shard_map(
        on_device,
        mesh=mesh,
        in_specs=placed,
        out_specs=(P("dp", "tile", None, None), P("dp", "tile", None, None), P("tile", None)),
        check_vma=False,
    )
```

```python
import functools
import math

import jax
import jax.numpy as jnp
from jax import lax
from jax.experimental import pallas as pl
from jax.experimental.pallas import tpu as pltpu
from jax.sharding import PartitionSpec as P

epsilon = 1e-05

F32 = jnp.float32
BF16 = jnp.bfloat16
LANES = 128
CODE = 128
FINE = 16


def params(mebibytes):
    return pltpu.CompilerParams(vmem_limit_bytes=mebibytes * 1024 * 1024)


def vmem():
    return pl.BlockSpec(memory_space=pltpu.VMEM)


def far_held(values):
    return pltpu.with_memory_space_constraint(values, pltpu.HBM)


def turned(values, shift):
    return pltpu.roll(values, shift % values.shape[0], 0)


def pack_kernel(features, scores, points, cells, counts, packed, score_buf, point_buf, cell_buf, count_buf, sems):
    copies = [
        pltpu.make_async_copy(source, target, sems.at[i])
        for i, (source, target) in enumerate(
            (
                (points, point_buf),
                (scores, score_buf),
                (cells, cell_buf),
                (counts, count_buf),
                (features, packed.at[: features.shape[0]]),
            )
        )
    ]
    for copy in copies:
        copy.start()
    for copy in copies:
        copy.wait()
    pixels, bins = scores.shape
    strips, slots = points.shape
    logits = score_buf[...].astype(F32)
    grown = jnp.exp(logits - jnp.max(logits, axis=1, keepdims=True))
    prob = grown / jnp.sum(grown, axis=1, keepdims=True)
    blank = jnp.zeros((pixels, LANES - bins), F32)
    prob = jnp.concatenate([prob, blank], axis=1)
    unused = jnp.zeros((strips, LANES - slots), jnp.int32)
    point = jnp.concatenate([point_buf[...], unused], axis=1)
    cell = jnp.concatenate([cell_buf[...], unused], axis=1)
    bin_index = point % bins
    pixel = point // bins
    weight = jnp.zeros((strips, LANES), F32)
    for p in range(pixels):
        row = jnp.broadcast_to(prob[p : p + 1], (strips, LANES))
        weight = jnp.where(pixel == p, jnp.take_along_axis(row, bin_index, axis=1), weight)
    across = lax.broadcasted_iota(jnp.int32, (strips, strips), 1)
    down = lax.broadcasted_iota(jnp.int32, (strips, strips), 0)
    tally = jnp.sum(
        jnp.where(across == down, count_buf[...].astype(F32), 0.0), axis=1, keepdims=True
    )
    lane = lax.broadcasted_iota(jnp.int32, (strips, LANES), 1)
    low = lane < slots
    weight = jnp.where(lane.astype(F32) < tally, weight, 0.0)
    coarse = weight.astype(BF16).astype(F32)
    upper = (pixel * 8 + cell // CODE).astype(F32)
    under = (cell % CODE).astype(F32)
    weights = jnp.where(low, coarse, pltpu.roll(weight - coarse, slots, 1))
    codes = jnp.where(low, upper, pltpu.roll(under, slots, 1))
    packed[pixels:] = jnp.concatenate([weights, codes], axis=1).astype(BF16)


def line_kernel(*refs):
    sources, messages, lists = refs[:2], refs[2:6], refs[6]
    strips = lax.axis_size("tile")
    plane = lax.axis_index("tile") // 4
    pixels, planes = sources[0].shape[0] - strips, sources[0].shape[1]
    for i in range(2):
        lists[i] = sources[i][pixels:].astype(F32)
    lane = lax.broadcasted_iota(jnp.int32, (1, planes), 1)
    for k in range(4):
        rows = []
        for i in range(2):
            messages[k][i * pixels : (i + 1) * pixels] = sources[i][:pixels]
            for j in range(8):
                wanted = 4 * (plane ^ k) + (j - 1)
                there = jnp.logical_and(wanted >= 0, wanted < strips)
                row = lists[i, pl.ds(jnp.clip(wanted, 0, strips - 1), 1), :]
                rows.append(jnp.where(jnp.logical_or(there, lane >= planes // 2), row, 0.0))
        messages[k][2 * pixels :] = jnp.concatenate(rows, axis=0).astype(BF16)


def strip_kernel(*refs):
    sources, messages, lists = refs[:4], refs[4:8], refs[8]
    pixels, planes = messages[0].shape[0] // 9, messages[0].shape[1]
    own = lax.axis_index("tile") % 4
    for i in range(4):
        lists[i] = sources[i][2 * pixels :].astype(F32)
    for k in range(4):
        rows = []
        for i in range(8):
            begin = i % 2 * pixels
            messages[k][i * pixels : (i + 1) * pixels] = sources[i // 2][begin : begin + pixels]
            for j in range(3):
                rows.append(lists[i // 2, pl.ds(i % 2 * 8 + (own ^ k) + j, 1), :])
        rows.append(jnp.zeros((8, planes), F32))
        messages[k][8 * pixels :] = jnp.concatenate(rows, axis=0).astype(BF16)


def lift(messages, meta, lifted):
    pixels = messages[0].shape[0] // 9
    slots = LANES // 2
    batch = 4
    span = batch * slots
    depth = batch * pixels
    low = lax.broadcasted_iota(jnp.int32, (1, LANES), 1) < slots
    home = (lax.broadcasted_iota(jnp.int32, (1, span), 1) // slots * pixels).astype(F32)
    order = lax.broadcasted_iota(jnp.int32, (depth, span), 0).astype(F32)
    for m, message in enumerate(messages):
        lists = message[8 * pixels :].astype(F32)
        halves = []
        for h in range(2):
            straight = lists[:, h * LANES : (h + 1) * LANES]
            halves.append((straight, pltpu.roll(straight, slots, 1)))
        for g in range(2):
            block = message[g * depth : (g + 1) * depth]
            turned_block = block.astype(F32).T.astype(BF16)
            twice = jnp.concatenate([turned_block, turned_block], axis=1)
            at = slice((2 * m + g) * span, (2 * m + g + 1) * span)
            for s in range(3):
                fields = []
                for straight, rolled in halves:
                    first, second = [], []
                    for p in range(2):
                        r0 = 3 * (batch * g + 2 * p) + s
                        r1 = r0 + 3
                        first.append(jnp.where(low, straight[r0 : r0 + 1], rolled[r1 : r1 + 1]))
                        second.append(jnp.where(low, rolled[r0 : r0 + 1], straight[r1 : r1 + 1]))
                    fields.append(jnp.concatenate(first, axis=1))
                    fields.append(jnp.concatenate(second, axis=1))
                coarse, rest, upper, under = fields
                pixel = jnp.floor(upper * 0.125)
                sixteenths = jnp.floor(under * (1.0 / FINE))
                meta[s, 0:1, at] = (upper - 8.0 * pixel) * (CODE // FINE) + sixteenths
                meta[s, 1:2, at] = under - FINE * sixteenths
                match = order == pixel + home
                coarse = jnp.where(match, coarse, 0.0).astype(BF16)
                rest = jnp.where(match, rest, 0.0).astype(BF16)
                lifted[s, :, at] = jnp.dot(
                    twice, jnp.concatenate([coarse, rest], axis=0), preferred_element_type=F32
                ).astype(BF16)


def splat_row(k, meta, lifted, onehot):
    s, r = k // 2, k % 2
    breadth, total = onehot.shape[1:]
    blocks = breadth // FINE
    fine = lax.broadcasted_iota(jnp.int32, (FINE, total), 0).astype(F32)
    comb = jnp.where(fine == meta[s, 1:2, :], 1.0, 0.0).astype(BF16)
    coarse = meta[s, 0:1, :]
    for b in range(blocks):
        chosen = jnp.where(coarse == float(r * blocks + b), 1.0, 0.0).astype(BF16)
        onehot[k % 2, b * FINE : (b + 1) * FINE, :] = comb * chosen
    return lax.dot_general(
        onehot[k % 2], lifted[s], (((1,), (1,)), ((), ())), preferred_element_type=F32
    )


def normalized(summed, bev, k):
    breadth, planes = summed.shape
    wide = bev.shape[1]
    factor = lax.rsqrt(jnp.mean(summed * summed, axis=1, keepdims=True) + epsilon)
    bev[k, :breadth] = (summed * factor).astype(BF16)
    bev[k, breadth:] = jnp.zeros((wide - breadth, planes), BF16)


def plane_kernel(message, sums, meta, lifted, onehot):
    lift([message], meta, lifted)
    for k in range(6):
        sums[k] = splat_row(k, meta, lifted, onehot)


def more_kernel(message, before, sums, meta, lifted, onehot):
    lift([message], meta, lifted)
    for k in range(6):
        sums[k] = before[k] + splat_row(k, meta, lifted, onehot)


def splat_kernel(message, before, bev, meta, lifted, onehot):
    lift([message], meta, lifted)
    for k in range(6):
        normalized(before[k] + splat_row(k, meta, lifted, onehot), bev, k)


def wide_weight(weight, planes):
    return jnp.concatenate(
        [
            jnp.concatenate(
                [weight[(a * 3 + b) * planes : (a * 3 + b + 1) * planes] for b in range(3)], axis=1
            )
            for a in range(3)
        ],
        axis=0,
    )


def conv_row(field, k, weight):
    planes = field.shape[2]
    stacked = jnp.concatenate([field[k - 1], field[k], field[k + 1]], axis=1)
    product = jnp.dot(stacked, weight, preferred_element_type=F32)
    return (
        product[:, planes : 2 * planes]
        + turned(product[:, :planes], 1)
        + turned(product[:, 2 * planes :], -1)
    )


def inside(shape, breadth):
    return lax.broadcasted_iota(jnp.int32, shape, 0) < breadth


def moved_kernel(breadth, own, kept, given, near, far):
    odd = lax.axis_index("tile") % 2 == 1
    near[...] = jnp.where(odd, own[0], own[1])
    far[...] = jnp.where(odd, own[1], own[0])
    right_core = lax.axis_index("dp") % 2 == 1
    wide = kept.shape[1]
    planes = own.shape[2]
    half = planes // 2
    filler = jnp.zeros((wide - breadth, planes), F32)
    for y in range(2):
        row = jnp.concatenate([own[y].astype(F32), filler], axis=0)
        for b in range(3):
            value = turned(row, b - 1).astype(BF16)
            left, right = value[:, :half], value[:, half:]
            at = slice(b * half, (b + 1) * half)
            kept[y, :, at] = jnp.where(right_core, right, left)
            given[y, :, at] = jnp.where(right_core, left, right)


def gradient_terms(columns, cotangent, terms):
    half = terms.shape[1]
    planes = columns.shape[1]
    for a in range(3):
        term = jnp.dot(columns[a], cotangent[0], preferred_element_type=F32)
        term = term + jnp.dot(columns[a + 1], cotangent[1], preferred_element_type=F32)
        for b in range(3):
            at = slice((a * 3 + b) * planes, (a * 3 + b + 1) * planes)
            terms[at] = term[:, b * half : (b + 1) * half].astype(terms.dtype)


def hidden_kernel(breadth, bev, weight, cotangent, pre, hidden, columns, given):
    wide, planes = bev.shape[1:]
    strip = lax.axis_index("tile")
    last = lax.axis_size("tile") - 1
    grid = wide_weight(weight, planes)
    mask = inside((wide, planes), breadth)
    for k in range(4):
        value = conv_row(bev, k + 1, grid)
        if k in (1, 2):
            pre[k - 1] = value
        keep = mask
        if k == 0:
            keep = jnp.logical_and(mask, strip != 0)
        if k == 3:
            keep = jnp.logical_and(mask, strip != last)
        active = jnp.where(keep, value * jax.nn.sigmoid(value), 0.0)
        hidden[k] = active.astype(BF16)
        columns[k] = active.T.astype(BF16)
    gradient_terms(columns, cotangent, given)


def scene_kernel(breadth, bev, hidden, weight, scene):
    grid = wide_weight(weight, bev.shape[2])
    for y in range(2):
        value = conv_row(hidden, y + 1, grid)
        scene[y] = (bev[y + 2, :breadth].astype(F32) + value[:breadth]).astype(BF16)


def flipped_taps(weight, planes, rows):
    return jnp.concatenate(
        [
            jnp.concatenate(
                [weight[(a * 3 + b) * planes : (a * 3 + b + 1) * planes] for a in rows], axis=1
            )
            for b in (2, 1, 0)
        ],
        axis=0,
    )


def back_products(stacked, flipped):
    return lax.dot_general(
        stacked, flipped, (((1,), (1,)), ((), ())), preferred_element_type=F32
    )


def joined(product, planes):
    return (
        product[:, planes : 2 * planes]
        + turned(product[:, :planes], 1)
        + turned(product[:, 2 * planes :], -1)
    )


def inner_kernel(breadth, own, weight, back, field):
    wide, planes = back.shape[1:]
    for k in range(2):
        field[k, :breadth] = own[k]
        field[k, breadth:] = jnp.zeros((wide - breadth, planes), BF16)
    stacked = jnp.concatenate([field[0], field[1]], axis=1)
    back[0] = joined(back_products(stacked, flipped_taps(weight, planes, (1, 0))), planes)
    back[1] = joined(back_products(stacked, flipped_taps(weight, planes, (2, 1))), planes)


def derivative_kernel(breadth, first, second, back, weight, pre, derivative, field):
    wide, planes = pre.shape[1:]
    strip = lax.axis_index("tile")
    odd = strip % 2 == 1
    zero = jnp.zeros((breadth, planes), BF16)
    above = jnp.where(odd, first[...], jnp.where(strip == 0, zero, second[...]))
    below = jnp.where(
        odd, jnp.where(strip == lax.axis_size("tile") - 1, zero, second[...]), first[...]
    )
    for y, (row, a) in enumerate(((above, 2), (below, 0))):
        field[y, :breadth] = row
        field[y, breadth:] = jnp.zeros((wide - breadth, planes), BF16)
        rest = joined(back_products(field[y], flipped_taps(weight, planes, (a,))), planes)
        value = pre[y, :breadth]
        sigma = jax.nn.sigmoid(value)
        slope = sigma * (1.0 + value * (1.0 - sigma))
        derivative[y] = ((back[y, :breadth] + rest[:breadth]) * slope).astype(BF16)


def parts_kernel(kept, taken, *parts):
    own = lax.axis_index("tile") % 4
    for p in range(kept.shape[0] // 4):
        for k in range(4):
            t = 4 * p + (own ^ k)
            parts[k][p] = (kept[t] + taken[t].astype(F32)).astype(parts[k].dtype)


def planes_kernel(first, one, two, three, *parts):
    plane = lax.axis_index("tile") // 4
    for k in range(4):
        for i, p in enumerate((plane ^ k, 7 - (plane ^ k))):
            total = first[p] + one[p].astype(F32) + two[p].astype(F32) + three[p].astype(F32)
            parts[k][i] = total.astype(parts[k].dtype)


def gradient_kernel(scale, ours, other, gradient):
    odd = lax.axis_index("dp") % 2 == 1
    half = ours.shape[1]
    mine, theirs = ours[...] * scale, other[...] * scale
    gradient[:, :half] = jnp.where(odd, theirs, mine)
    gradient[:, half:] = jnp.where(odd, mine, theirs)


def swap(values, axis, partner):
    return lax.ppermute(values, axis, [(i, partner(i)) for i in range(lax.axis_size(axis))])


def line_swap(k):
    return lambda i: i ^ k


def mirror(i):
    return 28 - i // 4 * 4 + i % 4


def added(first, *others):
    for other in others:
        first = first + other.astype(F32)
    return first


def on_device(
    image_descriptors,
    image_distance_scores,
    entry_sender_location,
    entry_receiver_square,
    entry_valid_tally,
    predicted_adjoint,
    initial_plane_filter,
    predictor_filter,
):
    _, height, breadth, planes = predicted_adjoint.shape
    pixels = image_descriptors.shape[1]
    strips, slots = entry_sender_location.shape[2:]
    wide = breadth // 16 * 16 + 16
    taps = predictor_filter.shape[0]
    half = planes // 2
    struct = jax.ShapeDtypeStruct
    held = pltpu.VMEM

    places = pixels + strips
    packed = pl.pallas_call(
        pack_kernel,
        out_shape=held((places, planes), BF16),
        in_specs=[pl.BlockSpec(memory_space=pl.ANY)] * 5,
        out_specs=vmem(),
        scratch_shapes=[
            pltpu.VMEM((pixels, image_distance_scores.shape[2]), BF16),
            pltpu.VMEM((strips, slots), jnp.int32),
            pltpu.VMEM((strips, slots), jnp.int32),
            pltpu.VMEM((1, strips), jnp.int32),
            pltpu.SemaphoreType.DMA((5,)),
        ],
        compiler_params=params(8),
        name="pack",
    )(
        far_held(image_descriptors[0]),
        far_held(image_distance_scores[0]),
        far_held(entry_sender_location[0, 0]),
        far_held(entry_receiver_square[0, 0]),
        far_held(entry_valid_tally[0]),
    )
    line = pl.pallas_call(
        line_kernel,
        out_shape=(held((2 * pixels + 16, planes), BF16),) * 4,
        in_specs=[vmem()] * 2,
        out_specs=(vmem(),) * 4,
        scratch_shapes=[pltpu.VMEM((2, strips, planes), F32)],
        compiler_params=params(4),
        name="line",
    )(packed, swap(packed, "tile", mirror))
    line = [line[0]] + [swap(line[k], "tile", line_swap(4 * k)) for k in (3, 2, 1)]
    own = predicted_adjoint[0]
    keep, give, near, far = pl.pallas_call(
        functools.partial(moved_kernel, breadth),
        out_shape=(held((2, wide, 3 * half), BF16),) * 2 + (held((breadth, planes), BF16),) * 2,
        in_specs=[vmem()],
        out_specs=(vmem(),) * 4,
        compiler_params=params(4),
        cost_estimate=pl.CostEstimate(flops=10**6, bytes_accessed=10**6, transcendentals=0),
        name="moved",
    )(own)
    line, keep, give = lax.optimization_barrier((line, keep, give))
    messages = pl.pallas_call(
        strip_kernel,
        out_shape=(held((9 * pixels, planes), BF16),) * 4,
        in_specs=[vmem()] * 4,
        out_specs=(vmem(),) * 4,
        scratch_shapes=[pltpu.VMEM((4, 16, planes), F32)],
        compiler_params=params(4),
        name="strip",
    )(*line)
    arrived = [swap(messages[k], "tile", line_swap(k)) for k in (2, 1, 3)]

    def splat_scratch(count):
        total = count * 8 * slots
        return [
            pltpu.VMEM((3, 8, total), F32),
            pltpu.VMEM((3, planes, total), BF16),
            pltpu.VMEM((2, breadth, total), BF16),
        ]

    sums = pl.pallas_call(
        plane_kernel,
        out_shape=held((6, breadth, planes), F32),
        in_specs=[vmem()],
        out_specs=vmem(),
        scratch_shapes=splat_scratch(1),
        compiler_params=params(8),
        cost_estimate=pl.CostEstimate(flops=2 * 6 * breadth * 8 * slots * planes, bytes_accessed=10**6, transcendentals=0),
        name="plane",
    )(messages[0])
    sums = pl.pallas_call(
        more_kernel,
        out_shape=held((6, breadth, planes), F32),
        in_specs=[vmem()] * 2,
        out_specs=vmem(),
        scratch_shapes=splat_scratch(1),
        compiler_params=params(8),
        cost_estimate=pl.CostEstimate(flops=2 * 6 * breadth * 8 * slots * planes, bytes_accessed=10**6, transcendentals=0),
        name="more",
    )(arrived[0], sums)
    sums = pl.pallas_call(
        more_kernel,
        out_shape=held((6, breadth, planes), F32),
        in_specs=[vmem()] * 2,
        out_specs=vmem(),
        scratch_shapes=splat_scratch(1),
        compiler_params=params(8),
        cost_estimate=pl.CostEstimate(flops=2 * 6 * breadth * 8 * slots * planes, bytes_accessed=10**6, transcendentals=0),
        name="again",
    )(arrived[1], sums)
    bev = pl.pallas_call(
        splat_kernel,
        out_shape=held((6, wide, planes), BF16),
        in_specs=[vmem()] * 2,
        out_specs=vmem(),
        scratch_shapes=splat_scratch(1),
        compiler_params=params(8),
        name="splat",
    )(arrived[2], sums)
    pre, hidden, columns, given = pl.pallas_call(
        functools.partial(hidden_kernel, breadth),
        out_shape=(
            held((2, wide, planes), F32),
            held((4, wide, planes), BF16),
            held((4, planes, wide), BF16),
            held((taps, half), BF16),
        ),
        in_specs=[vmem()] * 3,
        out_specs=(vmem(),) * 4,
        compiler_params=params(10),
        name="hidden",
    )(bev, initial_plane_filter, give)
    taken = swap(given, "dp", line_swap(1))
    kept = pl.pallas_call(
        gradient_terms,
        out_shape=held((taps, half), F32),
        in_specs=[vmem()] * 2,
        out_specs=vmem(),
        compiler_params=params(8),
        cost_estimate=pl.CostEstimate(flops=4 * wide * taps * half, bytes_accessed=10**6, transcendentals=0),
        name="kept",
    )(columns, keep)
    kept, taken = lax.optimization_barrier((kept, taken))

    share = taps // strips
    parts = pl.pallas_call(
        parts_kernel,
        out_shape=tuple(held((strips // 4, share, half), F32 if k == 0 else BF16) for k in range(4)),
        in_specs=[vmem()] * 2,
        out_specs=(vmem(),) * 4,
        compiler_params=params(2),
        name="parts",
    )(kept.reshape(strips, share, half), taken.reshape(strips, share, half))
    fetched = [swap(parts[k], "tile", line_swap(k)) for k in (2, 3, 1)]
    scene = pl.pallas_call(
        functools.partial(scene_kernel, breadth),
        out_shape=struct((2, breadth, planes), BF16),
        in_specs=[vmem()] * 3,
        out_specs=vmem(),
        compiler_params=params(8),
        cost_estimate=pl.CostEstimate(flops=2 * 2 * wide * taps * planes, bytes_accessed=10**6, transcendentals=0),
        name="scene",
    )(bev, hidden, predictor_filter)
    back = pl.pallas_call(
        functools.partial(inner_kernel, breadth),
        out_shape=held((2, wide, planes), F32),
        in_specs=[vmem()] * 2,
        out_specs=vmem(),
        scratch_shapes=[pltpu.VMEM((2, wide, planes), BF16)],
        compiler_params=params(8),
        cost_estimate=pl.CostEstimate(flops=4 * wide * taps * planes // 3 * 2, bytes_accessed=10**6, transcendentals=0),
        name="inner",
    )(own, predictor_filter)
    fetched, scene, back = lax.optimization_barrier((fetched, scene, back))
    pairs = pl.pallas_call(
        planes_kernel,
        out_shape=tuple(held((2, share, half), F32 if k == 0 else BF16) for k in range(4)),
        in_specs=[vmem()] * 4,
        out_specs=(vmem(),) * 4,
        compiler_params=params(2),
        name="planes",
    )(parts[0], *fetched)
    fetched = [swap(pairs[k], "tile", line_swap(4 * k)) for k in (1, 2, 3)]
    pair = added(pairs[0], *fetched)
    ours = pair[0]
    theirs, near, far = lax.optimization_barrier((pair[1].astype(BF16), near, far))
    first = swap(near, "tile", line_swap(1))
    second = swap(far, "tile", lambda i: (i - 1 + 2 * (i % 2)) % strips)
    ours = added(ours, swap(theirs, "tile", mirror))
    fetched = [swap(ours.astype(BF16), "dp", line_swap(2 * k)) for k in (3, 2, 1)]
    fetched, first, second = lax.optimization_barrier((fetched, first, second))
    derivative = pl.pallas_call(
        functools.partial(derivative_kernel, breadth),
        out_shape=struct((2, breadth, planes), BF16),
        in_specs=[vmem()] * 5,
        out_specs=vmem(),
        scratch_shapes=[pltpu.VMEM((2, wide, planes), BF16)],
        compiler_params=params(8),
        cost_estimate=pl.CostEstimate(flops=4 * wide * taps * planes // 3, bytes_accessed=10**6, transcendentals=10**6),
        name="derivative",
    )(first, second, back, predictor_filter, pre)
    ours = added(ours, *fetched)
    other, derivative = lax.optimization_barrier((swap(ours, "dp", line_swap(1)), derivative))
    square_tally = lax.axis_size("dp") * height * strips * breadth
    gradient = pl.pallas_call(
        functools.partial(gradient_kernel, 1.0 / math.sqrt(square_tally)),
        out_shape=struct((share, planes), F32),
        in_specs=[vmem()] * 2,
        out_specs=vmem(),
        compiler_params=params(2),
        name="gradient",
    )(ours, other)
    return scene[None], derivative[None], gradient


def solution(mesh):
    placed = (
        P("dp", "tile", None),
        P("dp", "tile", None),
        P("dp", "tile", None, None),
        P("dp", "tile", None, None),
        P("dp", "tile", None),
        P("dp", "tile", None, None),
        P(),
        P(),
    )
    return jax.shard_map(
        on_device,
        mesh=mesh,
        in_specs=placed,
        out_specs=(P("dp", "tile", None, None), P("dp", "tile", None, None), P("tile", None)),
        check_vma=False,
    )
```

```python
import functools
import math

import jax
import jax.numpy as jnp
from jax import lax
from jax.experimental import pallas as pl
from jax.experimental.pallas import tpu as pltpu
from jax.sharding import PartitionSpec as P

epsilon = 1e-05

F32 = jnp.float32
BF16 = jnp.bfloat16
LANES = 128
CODE = 128
FINE = 16


def params(mebibytes):
    return pltpu.CompilerParams(vmem_limit_bytes=mebibytes * 1024 * 1024)


def vmem():
    return pl.BlockSpec(memory_space=pltpu.VMEM)


def far_held(values):
    return pltpu.with_memory_space_constraint(values, pltpu.HBM)


def turned(values, shift):
    return pltpu.roll(values, shift % values.shape[0], 0)


def pack_kernel(features, scores, points, cells, counts, packed, score_buf, point_buf, cell_buf, count_buf, sems):
    copies = [
        pltpu.make_async_copy(source, target, sems.at[i])
        for i, (source, target) in enumerate(
            (
                (points, point_buf),
                (scores, score_buf),
                (cells, cell_buf),
                (counts, count_buf),
                (features, packed.at[: features.shape[0]]),
            )
        )
    ]
    for copy in copies:
        copy.start()
    for copy in copies[:-1]:
        copy.wait()
    pixels, bins = scores.shape
    strips, slots = points.shape
    logits = score_buf[...].astype(F32)
    grown = jnp.exp(logits - jnp.max(logits, axis=1, keepdims=True))
    prob = grown / jnp.sum(grown, axis=1, keepdims=True)
    blank = jnp.zeros((pixels, LANES - bins), F32)
    prob = jnp.concatenate([prob, blank], axis=1)
    unused = jnp.zeros((strips, LANES - slots), jnp.int32)
    point = jnp.concatenate([point_buf[...], unused], axis=1)
    cell = jnp.concatenate([cell_buf[...], unused], axis=1)
    bin_index = point % bins
    pixel = point // bins
    weight = jnp.zeros((strips, LANES), F32)
    for p in range(pixels):
        row = jnp.broadcast_to(prob[p : p + 1], (strips, LANES))
        weight = jnp.where(pixel == p, jnp.take_along_axis(row, bin_index, axis=1), weight)
    across = lax.broadcasted_iota(jnp.int32, (strips, strips), 1)
    down = lax.broadcasted_iota(jnp.int32, (strips, strips), 0)
    tally = jnp.sum(
        jnp.where(across == down, count_buf[...].astype(F32), 0.0), axis=1, keepdims=True
    )
    lane = lax.broadcasted_iota(jnp.int32, (strips, LANES), 1)
    low = lane < slots
    weight = jnp.where(lane.astype(F32) < tally, weight, 0.0)
    coarse = weight.astype(BF16).astype(F32)
    upper = (pixel * 8 + cell // CODE).astype(F32)
    under = (cell % CODE).astype(F32)
    weights = jnp.where(low, coarse, pltpu.roll(weight - coarse, slots, 1))
    codes = jnp.where(low, upper, pltpu.roll(under, slots, 1))
    packed[pixels:] = jnp.concatenate([weights, codes], axis=1).astype(BF16)
    copies[-1].wait()


def line_kernel(*refs):
    sources, messages, lists = refs[:2], refs[2:6], refs[6]
    strips = lax.axis_size("tile")
    plane = lax.axis_index("tile") // 4
    pixels, planes = sources[0].shape[0] - strips, sources[0].shape[1]
    for i in range(2):
        lists[i] = sources[i][pixels:].astype(F32)
    lane = lax.broadcasted_iota(jnp.int32, (1, planes), 1)
    for k in range(4):
        rows = []
        for i in range(2):
            messages[k][i * pixels : (i + 1) * pixels] = sources[i][:pixels]
            for j in range(8):
                wanted = 4 * (plane ^ k) + (j - 1)
                there = jnp.logical_and(wanted >= 0, wanted < strips)
                row = lists[i, pl.ds(jnp.clip(wanted, 0, strips - 1), 1), :]
                rows.append(jnp.where(jnp.logical_or(there, lane >= planes // 2), row, 0.0))
        messages[k][2 * pixels :] = jnp.concatenate(rows, axis=0).astype(BF16)


def strip_kernel(*refs):
    sources, messages, lists = refs[:4], refs[4:8], refs[8]
    pixels, planes = messages[0].shape[0] // 9, messages[0].shape[1]
    own = lax.axis_index("tile") % 4
    for i in range(4):
        lists[i] = sources[i][2 * pixels :].astype(F32)
    for k in range(4):
        rows = []
        for i in range(8):
            begin = i % 2 * pixels
            messages[k][i * pixels : (i + 1) * pixels] = sources[i // 2][begin : begin + pixels]
            for j in range(3):
                rows.append(lists[i // 2, pl.ds(i % 2 * 8 + (own ^ k) + j, 1), :])
        rows.append(jnp.zeros((8, planes), F32))
        messages[k][8 * pixels :] = jnp.concatenate(rows, axis=0).astype(BF16)


def lift(messages, meta, lifted):
    pixels = messages[0].shape[0] // 9
    slots = LANES // 2
    batch = 4
    span = batch * slots
    depth = batch * pixels
    low = lax.broadcasted_iota(jnp.int32, (1, LANES), 1) < slots
    home = (lax.broadcasted_iota(jnp.int32, (1, span), 1) // slots * pixels).astype(F32)
    order = lax.broadcasted_iota(jnp.int32, (depth, span), 0).astype(F32)
    for m, message in enumerate(messages):
        lists = message[8 * pixels :].astype(F32)
        halves = []
        for h in range(2):
            straight = lists[:, h * LANES : (h + 1) * LANES]
            halves.append((straight, pltpu.roll(straight, slots, 1)))
        for g in range(2):
            block = message[g * depth : (g + 1) * depth]
            turned_block = block.astype(F32).T.astype(BF16)
            twice = jnp.concatenate([turned_block, turned_block], axis=1)
            at = slice((2 * m + g) * span, (2 * m + g + 1) * span)
            for s in range(3):
                fields = []
                for straight, rolled in halves:
                    first, second = [], []
                    for p in range(2):
                        r0 = 3 * (batch * g + 2 * p) + s
                        r1 = r0 + 3
                        first.append(jnp.where(low, straight[r0 : r0 + 1], rolled[r1 : r1 + 1]))
                        second.append(jnp.where(low, rolled[r0 : r0 + 1], straight[r1 : r1 + 1]))
                    fields.append(jnp.concatenate(first, axis=1))
                    fields.append(jnp.concatenate(second, axis=1))
                coarse, rest, upper, under = fields
                pixel = jnp.floor(upper * 0.125)
                sixteenths = jnp.floor(under * (1.0 / FINE))
                meta[s, 0:1, at] = (upper - 8.0 * pixel) * (CODE // FINE) + sixteenths
                meta[s, 1:2, at] = under - FINE * sixteenths
                match = order == pixel + home
                coarse = jnp.where(match, coarse, 0.0).astype(BF16)
                rest = jnp.where(match, rest, 0.0).astype(BF16)
                lifted[s, :, at] = jnp.dot(
                    twice, jnp.concatenate([coarse, rest], axis=0), preferred_element_type=F32
                ).astype(BF16)


def splat_row(k, meta, lifted, onehot):
    s, r = k // 2, k % 2
    breadth, total = onehot.shape[1:]
    blocks = breadth // FINE
    fine = lax.broadcasted_iota(jnp.int32, (FINE, total), 0).astype(F32)
    comb = jnp.where(fine == meta[s, 1:2, :], 1.0, 0.0).astype(BF16)
    coarse = meta[s, 0:1, :]
    for b in range(blocks):
        chosen = jnp.where(coarse == float(r * blocks + b), 1.0, 0.0).astype(BF16)
        onehot[k % 2, b * FINE : (b + 1) * FINE, :] = comb * chosen
    return lax.dot_general(
        onehot[k % 2], lifted[s], (((1,), (1,)), ((), ())), preferred_element_type=F32
    )


def normalized(summed, bev, k):
    breadth, planes = summed.shape
    wide = bev.shape[1]
    factor = lax.rsqrt(jnp.mean(summed * summed, axis=1, keepdims=True) + epsilon)
    bev[k, :breadth] = (summed * factor).astype(BF16)
    bev[k, breadth:] = jnp.zeros((wide - breadth, planes), BF16)


def plane_kernel(message, sums, meta, lifted, onehot):
    lift([message], meta, lifted)
    for k in range(6):
        sums[k] = splat_row(k, meta, lifted, onehot)


def more_kernel(message, before, sums, meta, lifted, onehot):
    lift([message], meta, lifted)
    for k in range(6):
        sums[k] = before[k] + splat_row(k, meta, lifted, onehot)


def splat_kernel(message, before, bev, meta, lifted, onehot):
    lift([message], meta, lifted)
    for k in range(6):
        normalized(before[k] + splat_row(k, meta, lifted, onehot), bev, k)


def wide_weight(weight, planes):
    return jnp.concatenate(
        [
            jnp.concatenate(
                [weight[(a * 3 + b) * planes : (a * 3 + b + 1) * planes] for b in range(3)], axis=1
            )
            for a in range(3)
        ],
        axis=0,
    )


def conv_row(field, k, weight):
    planes = field.shape[2]
    stacked = jnp.concatenate([field[k - 1], field[k], field[k + 1]], axis=1)
    product = jnp.dot(stacked, weight, preferred_element_type=F32)
    return (
        product[:, planes : 2 * planes]
        + turned(product[:, :planes], 1)
        + turned(product[:, 2 * planes :], -1)
    )


def inside(shape, breadth):
    return lax.broadcasted_iota(jnp.int32, shape, 0) < breadth


def moved_kernel(breadth, own, kept, given, near, far):
    odd = lax.axis_index("tile") % 2 == 1
    near[...] = jnp.where(odd, own[0], own[1])
    far[...] = jnp.where(odd, own[1], own[0])
    right_core = lax.axis_index("dp") % 2 == 1
    wide = kept.shape[1]
    planes = own.shape[2]
    half = planes // 2
    filler = jnp.zeros((wide - breadth, planes), F32)
    for y in range(2):
        row = jnp.concatenate([own[y].astype(F32), filler], axis=0)
        for b in range(3):
            value = turned(row, b - 1).astype(BF16)
            left, right = value[:, :half], value[:, half:]
            at = slice(b * half, (b + 1) * half)
            kept[y, :, at] = jnp.where(right_core, right, left)
            given[y, :, at] = jnp.where(right_core, left, right)


def gradient_terms(columns, cotangent, terms):
    half = terms.shape[1]
    planes = columns.shape[1]
    for a in range(3):
        term = jnp.dot(columns[a], cotangent[0], preferred_element_type=F32)
        term = term + jnp.dot(columns[a + 1], cotangent[1], preferred_element_type=F32)
        for b in range(3):
            at = slice((a * 3 + b) * planes, (a * 3 + b + 1) * planes)
            terms[at] = term[:, b * half : (b + 1) * half].astype(terms.dtype)


def hidden_kernel(breadth, bev, weight, cotangent, pre, hidden, columns, given):
    wide, planes = bev.shape[1:]
    strip = lax.axis_index("tile")
    last = lax.axis_size("tile") - 1
    grid = wide_weight(weight, planes)
    mask = inside((wide, planes), breadth)
    for k in range(4):
        value = conv_row(bev, k + 1, grid)
        if k in (1, 2):
            pre[k - 1] = value
        keep = mask
        if k == 0:
            keep = jnp.logical_and(mask, strip != 0)
        if k == 3:
            keep = jnp.logical_and(mask, strip != last)
        active = jnp.where(keep, value * jax.nn.sigmoid(value), 0.0)
        hidden[k] = active.astype(BF16)
        columns[k] = active.T.astype(BF16)
    gradient_terms(columns, cotangent, given)


def scene_kernel(breadth, bev, hidden, weight, scene):
    grid = wide_weight(weight, bev.shape[2])
    for y in range(2):
        value = conv_row(hidden, y + 1, grid)
        scene[y] = (bev[y + 2, :breadth].astype(F32) + value[:breadth]).astype(BF16)


def flipped_taps(weight, planes, rows):
    return jnp.concatenate(
        [
            jnp.concatenate(
                [weight[(a * 3 + b) * planes : (a * 3 + b + 1) * planes] for a in rows], axis=1
            )
            for b in (2, 1, 0)
        ],
        axis=0,
    )


def back_products(stacked, flipped):
    return lax.dot_general(
        stacked, flipped, (((1,), (1,)), ((), ())), preferred_element_type=F32
    )


def joined(product, planes):
    return (
        product[:, planes : 2 * planes]
        + turned(product[:, :planes], 1)
        + turned(product[:, 2 * planes :], -1)
    )


def inner_kernel(breadth, own, weight, pre, back, slope, field):
    wide, planes = back.shape[1:]
    for k in range(2):
        field[k, :breadth] = own[k]
        field[k, breadth:] = jnp.zeros((wide - breadth, planes), BF16)
    stacked = jnp.concatenate([field[0], field[1]], axis=1)
    back[0] = joined(back_products(stacked, flipped_taps(weight, planes, (1, 0))), planes)
    back[1] = joined(back_products(stacked, flipped_taps(weight, planes, (2, 1))), planes)
    for y in range(2):
        value = pre[y]
        sigma = jax.nn.sigmoid(value)
        slope[y] = sigma * (1.0 + value * (1.0 - sigma))


def derivative_kernel(breadth, first, second, back, weight, slope, derivative, field):
    wide, planes = slope.shape[1:]
    strip = lax.axis_index("tile")
    odd = strip % 2 == 1
    zero = jnp.zeros((breadth, planes), BF16)
    above = jnp.where(odd, first[...], jnp.where(strip == 0, zero, second[...]))
    below = jnp.where(
        odd, jnp.where(strip == lax.axis_size("tile") - 1, zero, second[...]), first[...]
    )
    for y, (row, a) in enumerate(((above, 2), (below, 0))):
        field[y, :breadth] = row
        field[y, breadth:] = jnp.zeros((wide - breadth, planes), BF16)
        rest = joined(back_products(field[y], flipped_taps(weight, planes, (a,))), planes)
        derivative[y] = ((back[y, :breadth] + rest[:breadth]) * slope[y, :breadth]).astype(BF16)


def parts_kernel(kept, taken, *parts):
    own = lax.axis_index("tile") % 4
    for p in range(kept.shape[0] // 4):
        for k in range(4):
            t = 4 * p + (own ^ k)
            parts[k][p] = (kept[t] + taken[t].astype(F32)).astype(parts[k].dtype)


def planes_kernel(first, one, two, three, *parts):
    plane = lax.axis_index("tile") // 4
    for k in range(4):
        for i, p in enumerate((plane ^ k, 7 - (plane ^ k))):
            total = first[p] + one[p].astype(F32) + two[p].astype(F32) + three[p].astype(F32)
            parts[k][i] = total.astype(parts[k].dtype)


def gradient_kernel(scale, ours, other, gradient):
    odd = lax.axis_index("dp") % 2 == 1
    half = ours.shape[1]
    mine, theirs = ours[...] * scale, other[...] * scale
    gradient[:, :half] = jnp.where(odd, theirs, mine)
    gradient[:, half:] = jnp.where(odd, mine, theirs)


def swap(values, axis, partner):
    return lax.ppermute(values, axis, [(i, partner(i)) for i in range(lax.axis_size(axis))])


def line_swap(k):
    return lambda i: i ^ k


def mirror(i):
    return 28 - i // 4 * 4 + i % 4


def added(first, *others):
    for other in others:
        first = first + other.astype(F32)
    return first


def on_device(
    image_descriptors,
    image_distance_scores,
    entry_sender_location,
    entry_receiver_square,
    entry_valid_tally,
    predicted_adjoint,
    initial_plane_filter,
    predictor_filter,
):
    _, height, breadth, planes = predicted_adjoint.shape
    pixels = image_descriptors.shape[1]
    strips, slots = entry_sender_location.shape[2:]
    wide = breadth // 16 * 16 + 16
    taps = predictor_filter.shape[0]
    half = planes // 2
    struct = jax.ShapeDtypeStruct
    held = pltpu.VMEM

    places = pixels + strips
    packed = pl.pallas_call(
        pack_kernel,
        out_shape=held((places, planes), BF16),
        in_specs=[pl.BlockSpec(memory_space=pl.ANY)] * 5,
        out_specs=vmem(),
        scratch_shapes=[
            pltpu.VMEM((pixels, image_distance_scores.shape[2]), BF16),
            pltpu.VMEM((strips, slots), jnp.int32),
            pltpu.VMEM((strips, slots), jnp.int32),
            pltpu.VMEM((1, strips), jnp.int32),
            pltpu.SemaphoreType.DMA((5,)),
        ],
        compiler_params=params(8),
        name="pack",
    )(
        far_held(image_descriptors[0]),
        far_held(image_distance_scores[0]),
        far_held(entry_sender_location[0, 0]),
        far_held(entry_receiver_square[0, 0]),
        far_held(entry_valid_tally[0]),
    )
    line = pl.pallas_call(
        line_kernel,
        out_shape=(held((2 * pixels + 16, planes), BF16),) * 4,
        in_specs=[vmem()] * 2,
        out_specs=(vmem(),) * 4,
        scratch_shapes=[pltpu.VMEM((2, strips, planes), F32)],
        compiler_params=params(4),
        name="line",
    )(packed, swap(packed, "tile", mirror))
    line = [line[0]] + [swap(line[k], "tile", line_swap(4 * k)) for k in (3, 2, 1)]
    own = predicted_adjoint[0]
    keep, give, near, far = pl.pallas_call(
        functools.partial(moved_kernel, breadth),
        out_shape=(held((2, wide, 3 * half), BF16),) * 2 + (held((breadth, planes), BF16),) * 2,
        in_specs=[vmem()],
        out_specs=(vmem(),) * 4,
        compiler_params=params(4),
        cost_estimate=pl.CostEstimate(flops=10**6, bytes_accessed=10**6, transcendentals=0),
        name="moved",
    )(own)
    line, keep, give = lax.optimization_barrier((line, keep, give))
    messages = pl.pallas_call(
        strip_kernel,
        out_shape=(held((9 * pixels, planes), BF16),) * 4,
        in_specs=[vmem()] * 4,
        out_specs=(vmem(),) * 4,
        scratch_shapes=[pltpu.VMEM((4, 16, planes), F32)],
        compiler_params=params(4),
        name="strip",
    )(*line)
    arrived = [swap(messages[k], "tile", line_swap(k)) for k in (2, 1, 3)]

    def splat_scratch(count):
        total = count * 8 * slots
        return [
            pltpu.VMEM((3, 8, total), F32),
            pltpu.VMEM((3, planes, total), BF16),
            pltpu.VMEM((2, breadth, total), BF16),
        ]

    sums = pl.pallas_call(
        plane_kernel,
        out_shape=held((6, breadth, planes), F32),
        in_specs=[vmem()],
        out_specs=vmem(),
        scratch_shapes=splat_scratch(1),
        compiler_params=params(8),
        cost_estimate=pl.CostEstimate(flops=2 * 6 * breadth * 8 * slots * planes, bytes_accessed=10**6, transcendentals=0),
        name="plane",
    )(messages[0])
    sums = pl.pallas_call(
        more_kernel,
        out_shape=held((6, breadth, planes), F32),
        in_specs=[vmem()] * 2,
        out_specs=vmem(),
        scratch_shapes=splat_scratch(1),
        compiler_params=params(8),
        cost_estimate=pl.CostEstimate(flops=2 * 6 * breadth * 8 * slots * planes, bytes_accessed=10**6, transcendentals=0),
        name="more",
    )(arrived[0], sums)
    sums = pl.pallas_call(
        more_kernel,
        out_shape=held((6, breadth, planes), F32),
        in_specs=[vmem()] * 2,
        out_specs=vmem(),
        scratch_shapes=splat_scratch(1),
        compiler_params=params(8),
        cost_estimate=pl.CostEstimate(flops=2 * 6 * breadth * 8 * slots * planes, bytes_accessed=10**6, transcendentals=0),
        name="again",
    )(arrived[1], sums)
    bev = pl.pallas_call(
        splat_kernel,
        out_shape=held((6, wide, planes), BF16),
        in_specs=[vmem()] * 2,
        out_specs=vmem(),
        scratch_shapes=splat_scratch(1),
        compiler_params=params(8),
        name="splat",
    )(arrived[2], sums)
    pre, hidden, columns, given = pl.pallas_call(
        functools.partial(hidden_kernel, breadth),
        out_shape=(
            held((2, wide, planes), F32),
            held((4, wide, planes), BF16),
            held((4, planes, wide), BF16),
            held((taps, half), BF16),
        ),
        in_specs=[vmem()] * 3,
        out_specs=(vmem(),) * 4,
        compiler_params=params(10),
        name="hidden",
    )(bev, initial_plane_filter, give)
    taken = swap(given, "dp", line_swap(1))
    kept = pl.pallas_call(
        gradient_terms,
        out_shape=held((taps, half), F32),
        in_specs=[vmem()] * 2,
        out_specs=vmem(),
        compiler_params=params(8),
        cost_estimate=pl.CostEstimate(flops=4 * wide * taps * half, bytes_accessed=10**6, transcendentals=0),
        name="kept",
    )(columns, keep)
    kept, taken = lax.optimization_barrier((kept, taken))

    share = taps // strips
    parts = pl.pallas_call(
        parts_kernel,
        out_shape=tuple(held((strips // 4, share, half), F32 if k == 0 else BF16) for k in range(4)),
        in_specs=[vmem()] * 2,
        out_specs=(vmem(),) * 4,
        compiler_params=params(2),
        name="parts",
    )(kept.reshape(strips, share, half), taken.reshape(strips, share, half))
    fetched = [swap(parts[k], "tile", line_swap(k)) for k in (2, 3, 1)]
    scene = pl.pallas_call(
        functools.partial(scene_kernel, breadth),
        out_shape=struct((2, breadth, planes), BF16),
        in_specs=[vmem()] * 3,
        out_specs=vmem(),
        compiler_params=params(8),
        cost_estimate=pl.CostEstimate(flops=2 * 2 * wide * taps * planes, bytes_accessed=10**6, transcendentals=0),
        name="scene",
    )(bev, hidden, predictor_filter)
    back, slope = pl.pallas_call(
        functools.partial(inner_kernel, breadth),
        out_shape=(held((2, wide, planes), F32),) * 2,
        in_specs=[vmem()] * 3,
        out_specs=(vmem(),) * 2,
        scratch_shapes=[pltpu.VMEM((2, wide, planes), BF16)],
        compiler_params=params(8),
        cost_estimate=pl.CostEstimate(flops=4 * wide * taps * planes // 3 * 2, bytes_accessed=10**6, transcendentals=0),
        name="inner",
    )(own, predictor_filter, pre)
    fetched, scene, back, slope = lax.optimization_barrier((fetched, scene, back, slope))
    pairs = pl.pallas_call(
        planes_kernel,
        out_shape=tuple(held((2, share, half), F32 if k == 0 else BF16) for k in range(4)),
        in_specs=[vmem()] * 4,
        out_specs=(vmem(),) * 4,
        compiler_params=params(2),
        name="planes",
    )(parts[0], *fetched)
    fetched = [swap(pairs[k], "tile", line_swap(4 * k)) for k in (1, 2, 3)]
    pair = added(pairs[0], *fetched)
    ours = pair[0]
    theirs, near, far = lax.optimization_barrier((pair[1].astype(BF16), near, far))
    first = swap(near, "tile", line_swap(1))
    second = swap(far, "tile", lambda i: (i - 1 + 2 * (i % 2)) % strips)
    ours = added(ours, swap(theirs, "tile", mirror))
    fetched = [swap(ours.astype(BF16), "dp", line_swap(2 * k)) for k in (3, 2, 1)]
    fetched, first, second = lax.optimization_barrier((fetched, first, second))
    derivative = pl.pallas_call(
        functools.partial(derivative_kernel, breadth),
        out_shape=struct((2, breadth, planes), BF16),
        in_specs=[vmem()] * 5,
        out_specs=vmem(),
        scratch_shapes=[pltpu.VMEM((2, wide, planes), BF16)],
        compiler_params=params(8),
        cost_estimate=pl.CostEstimate(flops=4 * wide * taps * planes // 3, bytes_accessed=10**6, transcendentals=10**6),
        name="derivative",
    )(first, second, back, predictor_filter, slope)
    ours = added(ours, *fetched)
    other, derivative = lax.optimization_barrier((swap(ours, "dp", line_swap(1)), derivative))
    square_tally = lax.axis_size("dp") * height * strips * breadth
    gradient = pl.pallas_call(
        functools.partial(gradient_kernel, 1.0 / math.sqrt(square_tally)),
        out_shape=struct((share, planes), F32),
        in_specs=[vmem()] * 2,
        out_specs=vmem(),
        compiler_params=params(2),
        name="gradient",
    )(ours, other)
    return scene[None], derivative[None], gradient


def solution(mesh):
    placed = (
        P("dp", "tile", None),
        P("dp", "tile", None),
        P("dp", "tile", None, None),
        P("dp", "tile", None, None),
        P("dp", "tile", None),
        P("dp", "tile", None, None),
        P(),
        P(),
    )
    return jax.shard_map(
        on_device,
        mesh=mesh,
        in_specs=placed,
        out_specs=(P("dp", "tile", None, None), P("dp", "tile", None, None), P("tile", None)),
        check_vma=False,
    )
```

```python
import functools
import math

import jax
import jax.numpy as jnp
from jax import lax
from jax.experimental import pallas as pl
from jax.experimental.pallas import tpu as pltpu
from jax.sharding import PartitionSpec as P

epsilon = 1e-05

F32 = jnp.float32
BF16 = jnp.bfloat16
LANES = 128
CODE = 128
FINE = 16


def params(mebibytes):
    return pltpu.CompilerParams(vmem_limit_bytes=mebibytes * 1024 * 1024)


def vmem():
    return pl.BlockSpec(memory_space=pltpu.VMEM)


def far_held(values):
    return pltpu.with_memory_space_constraint(values, pltpu.HBM)


def turned(values, shift):
    return pltpu.roll(values, shift % values.shape[0], 0)


def pack_kernel(features, scores, points, cells, counts, packed, score_buf, point_buf, cell_buf, count_buf, sems):
    copies = [
        pltpu.make_async_copy(source, target, sems.at[i])
        for i, (source, target) in enumerate(
            (
                (points, point_buf),
                (scores, score_buf),
                (cells, cell_buf),
                (counts, count_buf),
                (features, packed.at[: features.shape[0]]),
            )
        )
    ]
    for copy in copies:
        copy.start()
    for copy in copies[:-1]:
        copy.wait()
    pixels, bins = scores.shape
    strips, slots = points.shape
    logits = score_buf[...].astype(F32)
    grown = jnp.exp(logits - jnp.max(logits, axis=1, keepdims=True))
    prob = grown / jnp.sum(grown, axis=1, keepdims=True)
    blank = jnp.zeros((pixels, LANES - bins), F32)
    prob = jnp.concatenate([prob, blank], axis=1)
    unused = jnp.zeros((strips, LANES - slots), jnp.int32)
    point = jnp.concatenate([point_buf[...], unused], axis=1)
    cell = jnp.concatenate([cell_buf[...], unused], axis=1)
    bin_index = point % bins
    pixel = point // bins
    weight = jnp.zeros((strips, LANES), F32)
    for p in range(pixels):
        row = jnp.broadcast_to(prob[p : p + 1], (strips, LANES))
        weight = jnp.where(pixel == p, jnp.take_along_axis(row, bin_index, axis=1), weight)
    across = lax.broadcasted_iota(jnp.int32, (strips, strips), 1)
    down = lax.broadcasted_iota(jnp.int32, (strips, strips), 0)
    tally = jnp.sum(
        jnp.where(across == down, count_buf[...].astype(F32), 0.0), axis=1, keepdims=True
    )
    lane = lax.broadcasted_iota(jnp.int32, (strips, LANES), 1)
    low = lane < slots
    weight = jnp.where(lane.astype(F32) < tally, weight, 0.0)
    coarse = weight.astype(BF16).astype(F32)
    upper = (pixel * 8 + cell // CODE).astype(F32)
    under = (cell % CODE).astype(F32)
    weights = jnp.where(low, coarse, pltpu.roll(weight - coarse, slots, 1))
    codes = jnp.where(low, upper, pltpu.roll(under, slots, 1))
    packed[pixels:] = jnp.concatenate([weights, codes], axis=1).astype(BF16)
    copies[-1].wait()


def line_kernel(*refs):
    sources, messages, lists = refs[:2], refs[2:6], refs[6]
    strips = lax.axis_size("tile")
    plane = lax.axis_index("tile") // 4
    pixels, planes = sources[0].shape[0] - strips, sources[0].shape[1]
    for i in range(2):
        lists[i] = sources[i][pixels:].astype(F32)
    lane = lax.broadcasted_iota(jnp.int32, (1, planes), 1)
    for k in range(4):
        rows = []
        for i in range(2):
            messages[k][i * pixels : (i + 1) * pixels] = sources[i][:pixels]
            for j in range(8):
                wanted = 4 * (plane ^ k) + (j - 1)
                there = jnp.logical_and(wanted >= 0, wanted < strips)
                row = lists[i, pl.ds(jnp.clip(wanted, 0, strips - 1), 1), :]
                rows.append(jnp.where(jnp.logical_or(there, lane >= planes // 2), row, 0.0))
        messages[k][2 * pixels :] = jnp.concatenate(rows, axis=0).astype(BF16)


def strip_kernel(*refs):
    sources, messages, lists = refs[:4], refs[4:8], refs[8]
    pixels, planes = messages[0].shape[0] // 9, messages[0].shape[1]
    own = lax.axis_index("tile") % 4
    for i in range(4):
        lists[i] = sources[i][2 * pixels :].astype(F32)
    for k in range(4):
        rows = []
        for i in range(8):
            begin = i % 2 * pixels
            messages[k][i * pixels : (i + 1) * pixels] = sources[i // 2][begin : begin + pixels]
            for j in range(3):
                rows.append(lists[i // 2, pl.ds(i % 2 * 8 + (own ^ k) + j, 1), :])
        rows.append(jnp.zeros((8, planes), F32))
        messages[k][8 * pixels :] = jnp.concatenate(rows, axis=0).astype(BF16)


def lift(messages, meta, lifted):
    pixels = messages[0].shape[0] // 9
    slots = LANES // 2
    batch = 4
    span = batch * slots
    depth = batch * pixels
    low = lax.broadcasted_iota(jnp.int32, (1, LANES), 1) < slots
    home = (lax.broadcasted_iota(jnp.int32, (1, span), 1) // slots * pixels).astype(F32)
    order = lax.broadcasted_iota(jnp.int32, (depth, span), 0).astype(F32)
    for m, message in enumerate(messages):
        lists = message[8 * pixels :].astype(F32)
        halves = []
        for h in range(2):
            straight = lists[:, h * LANES : (h + 1) * LANES]
            halves.append((straight, pltpu.roll(straight, slots, 1)))
        for g in range(2):
            block = message[g * depth : (g + 1) * depth]
            turned_block = block.astype(F32).T.astype(BF16)
            twice = jnp.concatenate([turned_block, turned_block], axis=1)
            at = slice((2 * m + g) * span, (2 * m + g + 1) * span)
            for s in range(3):
                fields = []
                for straight, rolled in halves:
                    first, second = [], []
                    for p in range(2):
                        r0 = 3 * (batch * g + 2 * p) + s
                        r1 = r0 + 3
                        first.append(jnp.where(low, straight[r0 : r0 + 1], rolled[r1 : r1 + 1]))
                        second.append(jnp.where(low, rolled[r0 : r0 + 1], straight[r1 : r1 + 1]))
                    fields.append(jnp.concatenate(first, axis=1))
                    fields.append(jnp.concatenate(second, axis=1))
                coarse, rest, upper, under = fields
                pixel = jnp.floor(upper * 0.125)
                sixteenths = jnp.floor(under * (1.0 / FINE))
                meta[s, 0:1, at] = (upper - 8.0 * pixel) * (CODE // FINE) + sixteenths
                meta[s, 1:2, at] = under - FINE * sixteenths
                match = order == pixel + home
                coarse = jnp.where(match, coarse, 0.0).astype(BF16)
                rest = jnp.where(match, rest, 0.0).astype(BF16)
                lifted[s, :, at] = jnp.dot(
                    twice, jnp.concatenate([coarse, rest], axis=0), preferred_element_type=F32
                ).astype(BF16)


def splat_row(k, meta, lifted, onehot):
    s, r = k // 2, k % 2
    breadth, total = onehot.shape[1:]
    blocks = breadth // FINE
    fine = lax.broadcasted_iota(jnp.int32, (FINE, total), 0).astype(F32)
    comb = jnp.where(fine == meta[s, 1:2, :], 1.0, 0.0).astype(BF16)
    coarse = meta[s, 0:1, :]
    for b in range(blocks):
        chosen = jnp.where(coarse == float(r * blocks + b), 1.0, 0.0).astype(BF16)
        onehot[k % 2, b * FINE : (b + 1) * FINE, :] = comb * chosen
    return lax.dot_general(
        onehot[k % 2], lifted[s], (((1,), (1,)), ((), ())), preferred_element_type=F32
    )


def normalized(summed, bev, k):
    breadth, planes = summed.shape
    wide = bev.shape[1]
    factor = lax.rsqrt(jnp.mean(summed * summed, axis=1, keepdims=True) + epsilon)
    bev[k, :breadth] = (summed * factor).astype(BF16)
    bev[k, breadth:] = jnp.zeros((wide - breadth, planes), BF16)


def plane_kernel(message, sums, meta, lifted, onehot):
    lift([message], meta, lifted)
    for k in range(6):
        sums[k] = splat_row(k, meta, lifted, onehot)


def more_kernel(message, before, sums, meta, lifted, onehot):
    lift([message], meta, lifted)
    for k in range(6):
        sums[k] = before[k] + splat_row(k, meta, lifted, onehot)


def splat_kernel(message, before, bev, meta, lifted, onehot):
    lift([message], meta, lifted)
    for k in range(6):
        normalized(before[k] + splat_row(k, meta, lifted, onehot), bev, k)


def wide_weight(weight, planes):
    return jnp.concatenate(
        [
            jnp.concatenate(
                [weight[(a * 3 + b) * planes : (a * 3 + b + 1) * planes] for b in range(3)], axis=1
            )
            for a in range(3)
        ],
        axis=0,
    )


def conv_row(field, k, weight):
    planes = field.shape[2]
    stacked = jnp.concatenate([field[k - 1], field[k], field[k + 1]], axis=1)
    product = jnp.dot(stacked, weight, preferred_element_type=F32)
    return (
        product[:, planes : 2 * planes]
        + turned(product[:, :planes], 1)
        + turned(product[:, 2 * planes :], -1)
    )


def inside(shape, breadth):
    return lax.broadcasted_iota(jnp.int32, shape, 0) < breadth


def moved_kernel(breadth, own, kept, given, near, far):
    odd = lax.axis_index("tile") % 2 == 1
    near[...] = jnp.where(odd, own[0], own[1])
    far[...] = jnp.where(odd, own[1], own[0])
    right_core = lax.axis_index("dp") % 2 == 1
    wide = kept.shape[1]
    planes = own.shape[2]
    half = planes // 2
    filler = jnp.zeros((wide - breadth, planes), F32)
    for y in range(2):
        row = jnp.concatenate([own[y].astype(F32), filler], axis=0)
        for b in range(3):
            value = turned(row, b - 1).astype(BF16)
            left, right = value[:, :half], value[:, half:]
            at = slice(b * half, (b + 1) * half)
            kept[y, :, at] = jnp.where(right_core, right, left)
            given[y, :, at] = jnp.where(right_core, left, right)


def gradient_terms(columns, cotangent, terms):
    half = terms.shape[1]
    planes = columns.shape[1]
    for a in range(3):
        term = jnp.dot(columns[a], cotangent[0], preferred_element_type=F32)
        term = term + jnp.dot(columns[a + 1], cotangent[1], preferred_element_type=F32)
        for b in range(3):
            at = slice((a * 3 + b) * planes, (a * 3 + b + 1) * planes)
            terms[at] = term[:, b * half : (b + 1) * half].astype(terms.dtype)


def hidden_kernel(breadth, bev, weight, cotangent, pre, hidden, columns, given):
    wide, planes = bev.shape[1:]
    strip = lax.axis_index("tile")
    last = lax.axis_size("tile") - 1
    grid = wide_weight(weight, planes)
    mask = inside((wide, planes), breadth)
    for k in range(4):
        value = conv_row(bev, k + 1, grid)
        if k in (1, 2):
            pre[k - 1] = value
        keep = mask
        if k == 0:
            keep = jnp.logical_and(mask, strip != 0)
        if k == 3:
            keep = jnp.logical_and(mask, strip != last)
        active = jnp.where(keep, value * jax.nn.sigmoid(value), 0.0)
        hidden[k] = active.astype(BF16)
        columns[k] = active.T.astype(BF16)
    gradient_terms(columns, cotangent, given)


def scene_kernel(breadth, bev, hidden, weight, scene):
    grid = wide_weight(weight, bev.shape[2])
    for y in range(2):
        value = conv_row(hidden, y + 1, grid)
        scene[y] = (bev[y + 2, :breadth].astype(F32) + value[:breadth]).astype(BF16)


def flipped_taps(weight, planes, rows):
    return jnp.concatenate(
        [
            jnp.concatenate(
                [weight[(a * 3 + b) * planes : (a * 3 + b + 1) * planes] for a in rows], axis=1
            )
            for b in (2, 1, 0)
        ],
        axis=0,
    )


def back_products(stacked, flipped):
    return lax.dot_general(
        stacked, flipped, (((1,), (1,)), ((), ())), preferred_element_type=F32
    )


def joined(product, planes):
    return (
        product[:, planes : 2 * planes]
        + turned(product[:, :planes], 1)
        + turned(product[:, 2 * planes :], -1)
    )


def inner_kernel(breadth, own, weight, back, field):
    wide, planes = back.shape[1:]
    for k in range(2):
        field[k, :breadth] = own[k]
        field[k, breadth:] = jnp.zeros((wide - breadth, planes), BF16)
    stacked = jnp.concatenate([field[0], field[1]], axis=1)
    back[0] = joined(back_products(stacked, flipped_taps(weight, planes, (1, 0))), planes)
    back[1] = joined(back_products(stacked, flipped_taps(weight, planes, (2, 1))), planes)


def derivative_kernel(breadth, first, second, back, weight, pre, derivative, field):
    wide, planes = pre.shape[1:]
    strip = lax.axis_index("tile")
    odd = strip % 2 == 1
    zero = jnp.zeros((breadth, planes), BF16)
    above = jnp.where(odd, first[...], jnp.where(strip == 0, zero, second[...]))
    below = jnp.where(
        odd, jnp.where(strip == lax.axis_size("tile") - 1, zero, second[...]), first[...]
    )
    for y, (row, a) in enumerate(((above, 2), (below, 0))):
        field[y, :breadth] = row
        field[y, breadth:] = jnp.zeros((wide - breadth, planes), BF16)
        rest = joined(back_products(field[y], flipped_taps(weight, planes, (a,))), planes)
        value = pre[y, :breadth]
        sigma = jax.nn.sigmoid(value)
        slope = sigma * (1.0 + value * (1.0 - sigma))
        derivative[y] = ((back[y, :breadth] + rest[:breadth]) * slope).astype(BF16)


def parts_kernel(kept, taken, *parts):
    own = lax.axis_index("tile") % 4
    for p in range(kept.shape[0] // 4):
        for k in range(4):
            t = 4 * p + (own ^ k)
            parts[k][p] = (kept[t] + taken[t].astype(F32)).astype(parts[k].dtype)


def planes_kernel(first, one, two, three, *parts):
    plane = lax.axis_index("tile") // 4
    for k in range(4):
        for i, p in enumerate((plane ^ k, 7 - (plane ^ k))):
            total = first[p] + one[p].astype(F32) + two[p].astype(F32) + three[p].astype(F32)
            parts[k][i] = total.astype(parts[k].dtype)


def gradient_kernel(scale, ours, other, gradient):
    odd = lax.axis_index("dp") % 2 == 1
    half = ours.shape[1]
    mine, theirs = ours[...] * scale, other[...] * scale
    gradient[:, :half] = jnp.where(odd, theirs, mine)
    gradient[:, half:] = jnp.where(odd, mine, theirs)


def swap(values, axis, partner):
    return lax.ppermute(values, axis, [(i, partner(i)) for i in range(lax.axis_size(axis))])


def line_swap(k):
    return lambda i: i ^ k


def mirror(i):
    return 28 - i // 4 * 4 + i % 4


def added(first, *others):
    for other in others:
        first = first + other.astype(F32)
    return first


def on_device(
    image_descriptors,
    image_distance_scores,
    entry_sender_location,
    entry_receiver_square,
    entry_valid_tally,
    predicted_adjoint,
    initial_plane_filter,
    predictor_filter,
):
    _, height, breadth, planes = predicted_adjoint.shape
    pixels = image_descriptors.shape[1]
    strips, slots = entry_sender_location.shape[2:]
    wide = breadth // 16 * 16 + 16
    taps = predictor_filter.shape[0]
    half = planes // 2
    struct = jax.ShapeDtypeStruct
    held = pltpu.VMEM

    places = pixels + strips
    packed = pl.pallas_call(
        pack_kernel,
        out_shape=held((places, planes), BF16),
        in_specs=[pl.BlockSpec(memory_space=pl.ANY)] * 5,
        out_specs=vmem(),
        scratch_shapes=[
            pltpu.VMEM((pixels, image_distance_scores.shape[2]), BF16),
            pltpu.VMEM((strips, slots), jnp.int32),
            pltpu.VMEM((strips, slots), jnp.int32),
            pltpu.VMEM((1, strips), jnp.int32),
            pltpu.SemaphoreType.DMA((5,)),
        ],
        compiler_params=params(8),
        name="pack",
    )(
        far_held(image_descriptors[0]),
        far_held(image_distance_scores[0]),
        far_held(entry_sender_location[0, 0]),
        far_held(entry_receiver_square[0, 0]),
        far_held(entry_valid_tally[0]),
    )
    line = pl.pallas_call(
        line_kernel,
        out_shape=(held((2 * pixels + 16, planes), BF16),) * 4,
        in_specs=[vmem()] * 2,
        out_specs=(vmem(),) * 4,
        scratch_shapes=[pltpu.VMEM((2, strips, planes), F32)],
        compiler_params=params(4),
        name="line",
    )(packed, swap(packed, "tile", mirror))
    line = [line[0]] + [swap(line[k], "tile", line_swap(4 * k)) for k in (3, 2, 1)]
    own = predicted_adjoint[0]
    keep, give, near, far = pl.pallas_call(
        functools.partial(moved_kernel, breadth),
        out_shape=(held((2, wide, 3 * half), BF16),) * 2 + (held((breadth, planes), BF16),) * 2,
        in_specs=[vmem()],
        out_specs=(vmem(),) * 4,
        compiler_params=params(4),
        cost_estimate=pl.CostEstimate(flops=10**6, bytes_accessed=10**6, transcendentals=0),
        name="moved",
    )(own)
    line, keep, give = lax.optimization_barrier((line, keep, give))
    messages = pl.pallas_call(
        strip_kernel,
        out_shape=(held((9 * pixels, planes), BF16),) * 4,
        in_specs=[vmem()] * 4,
        out_specs=(vmem(),) * 4,
        scratch_shapes=[pltpu.VMEM((4, 16, planes), F32)],
        compiler_params=params(4),
        name="strip",
    )(*line)
    arrived = [swap(messages[k], "tile", line_swap(k)) for k in (2, 1, 3)]

    def splat_scratch(count):
        total = count * 8 * slots
        return [
            pltpu.VMEM((3, 8, total), F32),
            pltpu.VMEM((3, planes, total), BF16),
            pltpu.VMEM((2, breadth, total), BF16),
        ]

    sums = pl.pallas_call(
        plane_kernel,
        out_shape=held((6, breadth, planes), F32),
        in_specs=[vmem()],
        out_specs=vmem(),
        scratch_shapes=splat_scratch(1),
        compiler_params=params(8),
        cost_estimate=pl.CostEstimate(flops=2 * 6 * breadth * 8 * slots * planes, bytes_accessed=10**6, transcendentals=0),
        name="plane",
    )(messages[0])
    sums = pl.pallas_call(
        more_kernel,
        out_shape=held((6, breadth, planes), F32),
        in_specs=[vmem()] * 2,
        out_specs=vmem(),
        scratch_shapes=splat_scratch(1),
        compiler_params=params(8),
        cost_estimate=pl.CostEstimate(flops=2 * 6 * breadth * 8 * slots * planes, bytes_accessed=10**6, transcendentals=0),
        name="more",
    )(arrived[0], sums)
    sums = pl.pallas_call(
        more_kernel,
        out_shape=held((6, breadth, planes), F32),
        in_specs=[vmem()] * 2,
        out_specs=vmem(),
        scratch_shapes=splat_scratch(1),
        compiler_params=params(8),
        cost_estimate=pl.CostEstimate(flops=2 * 6 * breadth * 8 * slots * planes, bytes_accessed=10**6, transcendentals=0),
        name="again",
    )(arrived[1], sums)
    bev = pl.pallas_call(
        splat_kernel,
        out_shape=held((6, wide, planes), BF16),
        in_specs=[vmem()] * 2,
        out_specs=vmem(),
        scratch_shapes=splat_scratch(1),
        compiler_params=params(8),
        name="splat",
    )(arrived[2], sums)
    pre, hidden, columns, given = pl.pallas_call(
        functools.partial(hidden_kernel, breadth),
        out_shape=(
            held((2, wide, planes), F32),
            held((4, wide, planes), BF16),
            held((4, planes, wide), BF16),
            held((taps, half), BF16),
        ),
        in_specs=[vmem()] * 3,
        out_specs=(vmem(),) * 4,
        compiler_params=params(10),
        name="hidden",
    )(bev, initial_plane_filter, give)
    taken = swap(given, "dp", line_swap(1))
    kept = pl.pallas_call(
        gradient_terms,
        out_shape=held((taps, half), F32),
        in_specs=[vmem()] * 2,
        out_specs=vmem(),
        compiler_params=params(8),
        cost_estimate=pl.CostEstimate(flops=4 * wide * taps * half, bytes_accessed=10**6, transcendentals=0),
        name="kept",
    )(columns, keep)
    kept, taken = lax.optimization_barrier((kept, taken))

    share = taps // strips
    parts = pl.pallas_call(
        parts_kernel,
        out_shape=tuple(held((strips // 4, share, half), F32 if k == 0 else BF16) for k in range(4)),
        in_specs=[vmem()] * 2,
        out_specs=(vmem(),) * 4,
        compiler_params=params(2),
        name="parts",
    )(kept.reshape(strips, share, half), taken.reshape(strips, share, half))
    fetched = [swap(parts[k], "tile", line_swap(k)) for k in (2, 3, 1)]
    scene = pl.pallas_call(
        functools.partial(scene_kernel, breadth),
        out_shape=struct((2, breadth, planes), BF16),
        in_specs=[vmem()] * 3,
        out_specs=vmem(),
        compiler_params=params(8),
        cost_estimate=pl.CostEstimate(flops=2 * 2 * wide * taps * planes, bytes_accessed=10**6, transcendentals=0),
        name="scene",
    )(bev, hidden, predictor_filter)
    back = pl.pallas_call(
        functools.partial(inner_kernel, breadth),
        out_shape=held((2, wide, planes), F32),
        in_specs=[vmem()] * 2,
        out_specs=vmem(),
        scratch_shapes=[pltpu.VMEM((2, wide, planes), BF16)],
        compiler_params=params(8),
        cost_estimate=pl.CostEstimate(flops=4 * wide * taps * planes // 3 * 2, bytes_accessed=10**6, transcendentals=0),
        name="inner",
    )(own, predictor_filter)
    fetched, scene, back = lax.optimization_barrier((fetched, scene, back))
    pairs = pl.pallas_call(
        planes_kernel,
        out_shape=tuple(held((2, share, half), F32 if k == 0 else BF16) for k in range(4)),
        in_specs=[vmem()] * 4,
        out_specs=(vmem(),) * 4,
        compiler_params=params(2),
        name="planes",
    )(parts[0], *fetched)
    fetched = [swap(pairs[k], "tile", line_swap(4 * k)) for k in (1, 2, 3)]
    pair = added(pairs[0], *fetched)
    ours = pair[0]
    theirs, near, far = lax.optimization_barrier((pair[1].astype(BF16), near, far))
    first = swap(near, "tile", line_swap(1))
    second = swap(far, "tile", lambda i: (i - 1 + 2 * (i % 2)) % strips)
    ours = added(ours, swap(theirs, "tile", mirror))
    fetched = [swap(ours.astype(BF16), "dp", line_swap(2 * k)) for k in (3, 2, 1)]
    fetched, first, second = lax.optimization_barrier((fetched, first, second))
    derivative = pl.pallas_call(
        functools.partial(derivative_kernel, breadth),
        out_shape=struct((2, breadth, planes), BF16),
        in_specs=[vmem()] * 5,
        out_specs=vmem(),
        scratch_shapes=[pltpu.VMEM((2, wide, planes), BF16)],
        compiler_params=params(8),
        cost_estimate=pl.CostEstimate(flops=4 * wide * taps * planes // 3, bytes_accessed=10**6, transcendentals=10**6),
        name="derivative",
    )(first, second, back, predictor_filter, pre)
    ours = added(ours, *fetched)
    other, derivative = lax.optimization_barrier((swap(ours, "dp", line_swap(1)), derivative))
    square_tally = lax.axis_size("dp") * height * strips * breadth
    gradient = pl.pallas_call(
        functools.partial(gradient_kernel, 1.0 / math.sqrt(square_tally)),
        out_shape=struct((share, planes), F32),
        in_specs=[vmem()] * 2,
        out_specs=vmem(),
        compiler_params=params(2),
        name="gradient",
    )(ours, other)
    return scene[None], derivative[None], gradient


def solution(mesh):
    placed = (
        P("dp", "tile", None),
        P("dp", "tile", None),
        P("dp", "tile", None, None),
        P("dp", "tile", None, None),
        P("dp", "tile", None),
        P("dp", "tile", None, None),
        P(),
        P(),
    )
    return jax.shard_map(
        on_device,
        mesh=mesh,
        in_specs=placed,
        out_specs=(P("dp", "tile", None, None), P("dp", "tile", None, None), P("tile", None)),
        check_vma=False,
    )
```
